32 devices in a mesh: groups: 2 (over y), fibre: 4 (over z), seg: 2 (over x), rec: 2 (over core).
Axes of the slice: x: 2, y: 2, z: 4, core: 2. Of those that a mesh axis runs over, the one named last changes fastest.
Arguments:
- records: bfloat16 [2, 2048, 1024], P('rec', 'fibre', ('groups', 'seg')), parts along dimension 2, may hold values from -6 to 6
- pairs: int32 [16, 2], replicated, may hold values from 0 to 15
- observed: float32 [32, 32, 256], P(('groups', 'fibre', 'seg')), parts along dimension 0, may hold values from -6 to 6
- lag_mask: int32 [32, 256], P(('groups', 'fibre', 'seg')), parts along dimension 0, may hold values 0 or 1
Outputs:
- adjoint_sources: bfloat16 [2, 2048, 1024], P('rec', 'fibre', ('groups', 'seg')), parts along dimension 2
The draws below stay inside these ranges and needn't reach their ends.
There are 2 independent parts, one for each index of `groups`. The reference program is written for one: setup_inputs(seed, part) draws one part's arguments, and reference() takes and returns one part's arrays. A program takes and returns all parts, laid end to end along the dimension named above; an argument that names none is the same for every part. Nothing has to cross between parts.
All inputs are finite; a program needn't handle non-finite values. No bound on the sum of `lag_mask` on one device may be relied on, other than what follows from the above.
Results may differ from the reference program's by a relative error of at most 0.015.
Values may be sent and summed in bfloat16 or wider, within the bound.
No kernel may reach another device: no remote copies, remote signals or barrier semaphores. Data moves between devices by JAX's collectives and lax.ppermute only.
A program may use at most 64 MiB of HBM per device.

```python
import jax
import jax.numpy as jnp

S = 2048
F = 1024
LAGS = 256
BLOCK = 32
CHANNELS = 512
NBLOCKS = 16
NPAIRS = 16


def set_ends(entries, own_key, least, largest):
    extent = entries.shape
    place = [jax.random.randint(jax.random.fold_in(own_key, axis), (), 0, extent[axis]) for axis in range(len(extent))]
    entries = entries.at[tuple(place)].set(least)
    longest = extent.index(max(extent))
    place[longest] = (place[longest] + 1) % extent[longest]
    return entries.at[tuple(place)].set(largest)


def steps_of(rng, shape, shards, low, top_value):
    loudness = 1.0
    for dim, shards_of in shards:
        steps = jax.random.uniform(jax.random.fold_in(jax.random.fold_in(rng, 6), dim), (shards_of,), jnp.float32, low / len(shards), top_value / len(shards))
        loudness = loudness * jnp.repeat(jnp.exp(steps), shape[dim] // shards_of).reshape((-1,) + (1,) * (len(shape) - 1 - dim))
    return loudness


def centred(stream_key, shape, deviation, limit, shards=(), kind=jnp.bfloat16):
    values = jax.random.normal(stream_key, shape, jnp.float32) * deviation
    if len(shards) > 0:
        values = steps_of(stream_key, shape, shards, -0.22, 0.18) * values
    return jnp.clip(values, min=-limit, max=limit).astype(kind)


def setup_inputs(seed: int = 0, part: int = 0) -> dict:
    streams_of = jax.random.split(jax.random.key(seed), 5)
    part_splits = jax.random.split(jax.random.fold_in(streams_of[4], part), 5)
    return {
        "records": centred(part_splits[0], (2, S, CHANNELS), 1.0, 6.0, ((0, 2), (1, 4), (2, 2))),
        "pairs": set_ends(jax.random.randint(streams_of[1], (NPAIRS, 2), 0, NBLOCKS), jax.random.fold_in(streams_of[1], 1), 0, NBLOCKS - 1).astype(jnp.int32),
        "observed": centred(part_splits[2], (NPAIRS, BLOCK, LAGS), 1.0, 6.0, ((0, 8),), jnp.float32),
        "lag_mask": set_ends((jax.random.randint(part_splits[3], (NPAIRS, LAGS), 0, 4) < 3).astype(jnp.int32), jax.random.fold_in(part_splits[3], 1), 0, 1),
    }


def forward_table():
    freq_index = jnp.arange(F, dtype=jnp.int32)
    time_index = jnp.arange(S, dtype=jnp.int32)
    phase = freq_index[:, None] * time_index[None, :] % S
    angles = phase.astype(jnp.float32) * (2.0 * jnp.pi / S)
    scale = 1.0 / jnp.sqrt(jnp.float32(S))
    return jnp.stack([(jnp.cos(angles) * scale).astype(jnp.bfloat16), (-jnp.sin(angles) * scale).astype(jnp.bfloat16)], axis=1)

def lag_table():
    freq_index = jnp.arange(F, dtype=jnp.int32)
    shifts = (jnp.arange(LAGS, dtype=jnp.int32) - LAGS // 2) % S
    phase = freq_index[:, None] * shifts[None, :] % S
    angles = phase.astype(jnp.float32) * (2.0 * jnp.pi / S)
    scale = 1.0 / jnp.sqrt(jnp.float32(F))
    return jnp.stack([(jnp.cos(angles) * scale).astype(jnp.bfloat16), (-jnp.sin(angles) * scale).astype(jnp.bfloat16)], axis=1)

def reference(records, pairs, observed, lag_mask):
    table = forward_table().astype(jnp.float32)
    lags = lag_table().astype(jnp.float32)
    spectra = jnp.einsum('wps,rsc->rwpc', table, records.astype(jnp.float32)).astype(jnp.bfloat16)
    blocks_grid = spectra.reshape(2, F, 2, NBLOCKS, BLOCK)
    first_side = jnp.take(blocks_grid, pairs[:, 0], axis=3).astype(jnp.float32)
    second_side = jnp.take(blocks_grid, pairs[:, 1], axis=3).astype(jnp.float32)
    first_re, first_im = (first_side[:, :, 0], first_side[:, :, 1])
    second_re, second_im = (second_side[:, :, 0], second_side[:, :, 1])
    cross_re = first_re * second_re + first_im * second_im
    cross_im = first_im * second_re - first_re * second_im
    cross_spec = jnp.stack([cross_re, cross_im], axis=2).astype(jnp.bfloat16)
    synthetic = jnp.einsum('rwpnk,wpl->nkl', cross_spec.astype(jnp.float32), lags)
    weights = lag_mask[:, None, :].astype(jnp.float32) * jnp.tanh(synthetic - observed)
    weights_low = weights.astype(jnp.bfloat16)
    adjoint_cross = jnp.einsum('nkl,wpl->wpnk', weights_low.astype(jnp.float32), lags).astype(jnp.bfloat16)
    adjoint_re = adjoint_cross[:, 0].astype(jnp.float32)[None]
    adjoint_im = adjoint_cross[:, 1].astype(jnp.float32)[None]
    grad_first = jnp.stack([adjoint_re * second_re - adjoint_im * second_im, adjoint_re * second_im + adjoint_im * second_re], axis=2)
    grad_second = jnp.stack([adjoint_re * first_re + adjoint_im * first_im, adjoint_re * first_im - adjoint_im * first_re], axis=2)
    contributions = jnp.concatenate([grad_first, grad_second], axis=3)
    endpoint_ids = jnp.concatenate([pairs[:, 0], pairs[:, 1]]).astype(jnp.int32)
    summed = jax.ops.segment_sum(jnp.moveaxis(contributions, 3, 0), endpoint_ids, num_segments=NBLOCKS)
    block_adjoint = jnp.moveaxis(summed, 0, 3).astype(jnp.bfloat16).reshape(2, F, 2, CHANNELS)
    adjoint_sources = jnp.einsum('rwpc,wps->rsc', block_adjoint.astype(jnp.float32), table)
    return adjoint_sources.astype(jnp.bfloat16)
```

```python
import functools

import jax
import jax.numpy as jnp
import numpy as np
from jax import lax
from jax.experimental import pallas as pl
from jax.experimental.pallas import tpu as pltpu
from jax.sharding import PartitionSpec as P

S = 2048
F = 1024
LAGS = 256
BLOCK = 32
SPANS = 4
MASKED = 16384.0
LANES = 128
EVERY = ("fibre", "seg", "rec")

_NT = (((1,), (1,)), ((), ()))
_TN = (((0,), (0,)), ((), ()))


def wave_table(freq, shift, scale):
    phase = freq[:, None].astype(np.int64) * shift[None, :] % S
    angles = phase.astype(np.float32) * np.float32(2.0 * np.pi / S)
    factor = np.float32(1.0) / np.sqrt(np.float32(scale))
    parts = [(np.cos(angles) * factor), (-np.sin(angles) * factor)]
    return np.stack(parts, axis=1).astype(jnp.bfloat16)


def forward_table():
    return wave_table(np.arange(F), np.arange(S), S)


def lag_table():
    return wave_table(np.arange(F), (np.arange(LAGS) - LAGS // 2) % S, F)


def dot(a, b, dims=(((1,), (0,)), ((), ()))):
    return lax.dot_general(a, b, dims, preferred_element_type=jnp.float32)


def one_hot(rows, cols, hit):
    row = lax.broadcasted_iota(jnp.int32, (rows, cols), 0)
    col = lax.broadcasted_iota(jnp.int32, (rows, cols), 1)
    return jnp.where(hit(row, col), 1.0, 0.0).astype(jnp.bfloat16)


def channel_of(row, blocks, own):
    return row % (blocks * own) // own * BLOCK + row // (blocks * own) * own + row % own


def pack_kernel(blocks, own, records_ref, observed_ref, mask_ref, out_ref):
    count = records_ref.shape[1]
    span = records_ref.shape[0]
    dests = BLOCK // own
    rows = blocks * own
    order = one_hot(count, count, lambda r, c: c == channel_of(r, blocks, own))
    moved = dot(order, records_ref[...], _NT).astype(jnp.bfloat16)
    out_ref[:, :, 0:span] = moved.reshape(dests, rows, span)
    pair_rows = observed_ref.shape[0]
    seen = jnp.where(mask_ref[...] != 0, observed_ref[...], MASKED)
    high = seen.astype(jnp.bfloat16)
    low = (seen - high.astype(jnp.float32)).astype(jnp.bfloat16)
    halves = LAGS // LANES
    parts = [v[:, h * LANES : (h + 1) * LANES] for v in (high, low) for h in range(halves)]
    stacked = jnp.concatenate(parts, axis=0)
    place = one_hot(
        count,
        stacked.shape[0],
        lambda r, c: (c % pair_rows // own == r // rows)
        & (c // pair_rows * own + c % own == r % rows),
    )
    packed = dot(place, stacked).astype(jnp.bfloat16)
    out_ref[:, :, span:] = packed.reshape(dests, rows, LANES)


def unpack_kernel(blocks, own, rows_ref, out_ref):
    count = out_ref.shape[1]
    order = one_hot(count, count, lambda r, c: c == channel_of(r, blocks, own))
    held = rows_ref[...].reshape(count, rows_ref.shape[2])
    out_ref[...] = dot(held, order, _TN).astype(jnp.bfloat16)


def main_kernel(segs, recs, blocks, own, pairs_ref, rows_ref, table_ref, lag_ref, out_ref):
    pair_total = pairs_ref.shape[0]
    span = S // SPANS
    band = F // SPANS
    count = segs * recs * blocks * own
    lines = pair_total * own
    every = recs * lines
    ways = segs * recs
    folds = [
        rows_ref[f * ways : (f + 1) * ways, :, 0:span].reshape(count, span).astype(jnp.float32)
        for f in range(SPANS)
    ]
    even, odd = folds[0] + folds[2], folds[1] + folds[3]
    e_part, d_part = folds[0] - folds[2], folds[1] - folds[3]
    both = jnp.concatenate([e_part, d_part], axis=0).astype(jnp.bfloat16)
    spectra = []
    for j in range(SPANS):
        if j % 2 == 0:
            signal = even + odd if j == 0 else even - odd
            part = dot(signal.astype(jnp.bfloat16), table_ref[j])
        else:
            mixed = dot(both, table_ref[j])
            e_c, e_s = mixed[:count, :band], mixed[:count, band:]
            d_c, d_s = mixed[count:, :band], mixed[count:, band:]
            sign = 1.0 if j == 1 else -1.0
            part = jnp.concatenate([e_c + sign * d_s, e_s - sign * d_c], axis=1)
        spectra.append(part.astype(jnp.bfloat16))

    def row_of(line, block):
        record, k = line // lines, line % own
        return ((block // blocks * recs + record) * blocks + block % blocks) * own + k

    def picks(side, line):
        pair = line % lines // own
        block = jnp.zeros_like(line)
        for n in range(pair_total):
            block = jnp.where(pair == n, pairs_ref[n, side], block)
        return row_of(line, block)

    take, give = [], []
    for side in range(2):
        line = lax.broadcasted_iota(jnp.int32, (every, count), 0)
        row = lax.broadcasted_iota(jnp.int32, (every, count), 1)
        take.append(jnp.where(picks(side, line) == row, 1.0, 0.0).astype(jnp.bfloat16))
        line = lax.broadcasted_iota(jnp.int32, (count, every), 1)
        row = lax.broadcasted_iota(jnp.int32, (count, every), 0)
        give.append(jnp.where(picks(side, line) == row, 1.0, 0.0).astype(jnp.bfloat16))
    take = jnp.concatenate(take, axis=0)
    give = jnp.concatenate(give + give, axis=1)

    sides = []
    total = None
    for j in range(SPANS):
        chosen = dot(take, spectra[j])
        a0, a1 = chosen[:every, :band], chosen[:every, band:]
        b0, b1 = chosen[every:, :band], chosen[every:, band:]
        sides.append((a0, a1, b0, b1))
        cross = jnp.concatenate([a0 * b0 + a1 * b1, a1 * b0 - a0 * b1], axis=1)
        term = dot(cross.astype(jnp.bfloat16), lag_ref[j])
        total = term if total is None else total + term
    synthetic = total[:lines]
    for r in range(1, recs):
        synthetic = synthetic + total[r * lines : (r + 1) * lines]

    halves = LAGS // LANES
    packed = rows_ref[:, :, span:].reshape(count * SPANS, LANES)
    rows = blocks * own
    seen = []
    for h in range(halves):
        find = one_hot(
            lines,
            packed.shape[0],
            lambda q, c: (q // own == c // rows)
            & ((c % rows == h * own + q % own) | (c % rows == (halves + h) * own + q % own)),
        )
        seen.append(dot(find, packed))
    seen = jnp.concatenate(seen, axis=1)
    weights = jnp.where(seen < 0.5 * MASKED, jnp.tanh(synthetic - seen), 0.0).astype(jnp.bfloat16)

    even, odd = None, None
    for j in range(SPANS):
        a0, a1, b0, b1 = sides[j]
        adjoint = dot(weights, lag_ref[j], _NT).astype(jnp.bfloat16).astype(jnp.float32)
        adjoint = jnp.concatenate([adjoint] * recs, axis=0)
        g0, g1 = adjoint[:, :band], adjoint[:, band:]
        first = jnp.concatenate([g0 * b0 - g1 * b1, g0 * b1 + g1 * b0], axis=1)
        second = jnp.concatenate([g0 * a0 + g1 * a1, g0 * a1 - g1 * a0], axis=1)
        terms = jnp.concatenate([first, second], axis=0)
        high = terms.astype(jnp.bfloat16)
        low = (terms - high.astype(jnp.float32)).astype(jnp.bfloat16)
        grad = dot(give, jnp.concatenate([high, low], axis=0))
        if j % 2 == 0:
            part = dot(grad.astype(jnp.bfloat16), table_ref[j], _NT)
            even = (part, part) if j == 0 else (even[0] + part, even[1] - part)
        else:
            turned = jnp.concatenate([-grad[:, band:], grad[:, :band]], axis=1)
            stacked = jnp.concatenate([grad, turned], axis=0).astype(jnp.bfloat16)
            part = dot(stacked, table_ref[j], _NT)
            u, v = part[:count], part[count:]
            odd = (u, v) if j == 1 else (odd[0] + u, odd[1] - v)
    rows = blocks * own
    for f in range(SPANS):
        base, side = even[f % 2], odd[f % 2]
        value = base + side if f < 2 else base - side
        out_ref[f * ways : (f + 1) * ways, :, :] = value.astype(jnp.bfloat16).reshape(ways, rows, span)


def by_own_k(records, pairs, observed, lag_mask):
    fibres, segs, recs = (lax.axis_size(a) for a in EVERY)
    devices = fibres * segs * recs
    own = BLOCK // devices
    span, count = records.shape[1:]
    blocks = count // BLOCK
    rows = blocks * own
    pairs_dev = observed.shape[0]
    share = pairs_dev // recs
    part = lax.axis_index("rec") * share
    observed = lax.dynamic_slice_in_dim(observed, part, share, 0).reshape(share * BLOCK, LAGS)
    lag_mask = lax.dynamic_slice_in_dim(lag_mask, part, share, 0)
    table = forward_table().reshape(F // SPANS, SPANS, 2, SPANS, span)[:, :, :, 0]
    table = np.ascontiguousarray(table.transpose(1, 3, 2, 0)).reshape(SPANS, span, S // SPANS)
    lags = lag_table().reshape(F // SPANS, SPANS, 2, LAGS)
    lags = np.ascontiguousarray(lags.transpose(1, 2, 0, 3)).reshape(SPANS, S // SPANS, LAGS)
    vmem = pl.BlockSpec(memory_space=pltpu.VMEM)
    send = pl.pallas_call(
        functools.partial(pack_kernel, blocks, own),
        out_shape=jax.ShapeDtypeStruct((devices, rows, span + LANES), jnp.bfloat16),
        in_specs=[vmem] * 3,
        out_specs=vmem,
    )(records[0], observed, lag_mask)
    held = lax.all_to_all(send, EVERY, 0, 0, tiled=True)
    back = pl.pallas_call(
        functools.partial(main_kernel, segs, recs, blocks, own),
        out_shape=jax.ShapeDtypeStruct((devices, rows, span), jnp.bfloat16),
        in_specs=[pl.BlockSpec(memory_space=pltpu.SMEM)] + [vmem] * 3,
        out_specs=vmem,
        compiler_params=pltpu.CompilerParams(vmem_limit_bytes=48 * 2**20),
    )(pairs, held, jnp.asarray(table), jnp.asarray(lags))
    mine = lax.all_to_all(back, EVERY, 0, 0, tiled=True)
    out = pl.pallas_call(
        functools.partial(unpack_kernel, blocks, own),
        out_shape=jax.ShapeDtypeStruct((span, count), jnp.bfloat16),
        in_specs=[vmem],
        out_specs=vmem,
    )(mine)
    return out[None]


def by_band(records, pairs, observed, lag_mask):
    fibres, segs = lax.axis_size("fibre"), lax.axis_size("seg")
    own = BLOCK // fibres
    span, count = records.shape[1:]
    blocks = count // BLOCK
    total_blocks = blocks * segs
    pair_total, pairs_dev = pairs.shape[0], observed.shape[0]
    low = jnp.bfloat16
    band = F // segs
    start = lax.axis_index("seg") * band
    table = lax.dynamic_slice_in_dim(jnp.asarray(forward_table()), start, band, 0)
    lags = lax.dynamic_slice_in_dim(jnp.asarray(lag_table()), start, band, 0)
    f32 = functools.partial(jnp.einsum, preferred_element_type=jnp.float32)
    grid = records.reshape(span, blocks, fibres, own).transpose(2, 0, 1, 3)
    signal = lax.all_to_all(grid, "fibre", 0, 0, tiled=True).reshape(S, blocks, own)
    signal = lax.all_gather(signal, "seg", axis=1, tiled=True)
    spectra = f32("wpt,tbk->wpbk", table, signal).astype(low)
    ids = jnp.arange(total_blocks)
    take = [(pairs[:, side, None] == ids).astype(low) for side in range(2)]
    a0, a1 = (f32("nb,wbk->wnk", take[0], spectra[:, p]) for p in range(2))
    b0, b1 = (f32("nb,wbk->wnk", take[1], spectra[:, p]) for p in range(2))
    cross = jnp.stack([a0 * b0 + a1 * b1, a1 * b0 - a0 * b1], axis=1).astype(low)
    corr = f32("wpnk,wpl->nkl", cross, lags)
    corr = corr.reshape(fibres, segs, pairs_dev, own, LAGS)
    corr = lax.psum_scatter(corr, "seg", scatter_dimension=1)
    synthetic = lax.psum(corr, "rec").reshape(fibres * pairs_dev, own, LAGS)
    seen = observed.reshape(pairs_dev, fibres, own, LAGS).transpose(1, 0, 2, 3)
    seen = lax.all_to_all(seen, "fibre", 0, 0, tiled=True).reshape(fibres * pairs_dev, own, LAGS)
    window = lax.all_gather(lag_mask.astype(jnp.float32), "fibre", axis=0, tiled=True)
    weights = (window[:, None, :] * jnp.tanh(synthetic - seen)).astype(low)
    weights = lax.all_gather(weights.reshape(fibres, pairs_dev, own, LAGS), "seg", axis=1)
    weights = weights.reshape(pair_total, own, LAGS)
    adjoint = f32("nkl,wpl->wpnk", weights, lags).astype(low).astype(jnp.float32)
    g0, g1 = adjoint[:, 0], adjoint[:, 1]

    def added(side, terms):
        high = terms.astype(low)
        rest = (terms - high.astype(jnp.float32)).astype(low)
        return f32("nb,wnk->wbk", take[side], high) + f32("nb,wnk->wbk", take[side], rest)

    grad = jnp.stack(
        [
            added(0, g0 * b0 - g1 * b1) + added(1, g0 * a0 + g1 * a1),
            added(0, g0 * b1 + g1 * b0) + added(1, g0 * a1 - g1 * a0),
        ],
        axis=1,
    ).astype(low)
    sources = f32("wpbk,wpt->tbk", grad, table)
    sources = lax.psum_scatter(sources, "seg", scatter_dimension=1, tiled=True).astype(low)
    sources = sources.reshape(fibres, span, blocks, own)
    sources = lax.all_to_all(sources, "fibre", 0, 0, tiled=True)
    return sources.transpose(1, 2, 0, 3).reshape(1, span, count)


def solution(mesh):
    devices = mesh.shape["fibre"] * mesh.shape["seg"] * mesh.shape["rec"]
    in_specs = (
        P("rec", "fibre", ("groups", "seg")),
        P(),
        P(("groups", "fibre", "seg"), None, None),
        P(("groups", "fibre", "seg"), None),
    )
    out_specs = P("rec", "fibre", ("groups", "seg"))
    small = mesh.shape["fibre"] == SPANS and BLOCK % devices == 0
    return jax.shard_map(
        by_own_k if small else by_band,
        mesh=mesh,
        in_specs=in_specs,
        out_specs=out_specs,
        check_vma=False,
    )
```

```python
import functools

import jax
import jax.numpy as jnp
import numpy as np
from jax import lax
from jax.experimental import pallas as pl
from jax.experimental.pallas import tpu as pltpu
from jax.sharding import PartitionSpec as P

S = 2048
F = 1024
LAGS = 256
BLOCK = 32
SPANS = 4
MASKED = 16384.0
LANES = 128
EVERY = ("fibre", "seg", "rec")

_NT = (((1,), (1,)), ((), ()))
_TN = (((0,), (0,)), ((), ()))


def wave_table(freq, shift, scale):
    phase = freq[:, None].astype(np.int64) * shift[None, :] % S
    angles = phase.astype(np.float32) * np.float32(2.0 * np.pi / S)
    factor = np.float32(1.0) / np.sqrt(np.float32(scale))
    parts = [(np.cos(angles) * factor), (-np.sin(angles) * factor)]
    return np.stack(parts, axis=1).astype(jnp.bfloat16)


def forward_table():
    return wave_table(np.arange(F), np.arange(S), S)


def lag_table():
    return wave_table(np.arange(F), (np.arange(LAGS) - LAGS // 2) % S, F)


def dot(a, b, dims=(((1,), (0,)), ((), ()))):
    return lax.dot_general(a, b, dims, preferred_element_type=jnp.float32)


def one_hot(rows, cols, hit):
    row = lax.broadcasted_iota(jnp.int32, (rows, cols), 0)
    col = lax.broadcasted_iota(jnp.int32, (rows, cols), 1)
    return jnp.where(hit(row, col), 1.0, 0.0).astype(jnp.bfloat16)


def channel_of(row, blocks, own):
    return row % (blocks * own) // own * BLOCK + row // (blocks * own) * own + row % own


def pack_kernel(blocks, own, records_hbm, observed_hbm, mask_hbm, out_ref, records, observed, mask, sems):
    span, count = records.shape
    dests = BLOCK // own
    rows = blocks * own
    tiles = span // LANES
    share = observed.shape[0]
    start = lax.axis_index("rec") * share
    seen_copy = pltpu.make_async_copy(observed_hbm.at[pl.ds(start, share)], observed, sems.at[0])
    mask_copy = pltpu.make_async_copy(mask_hbm, mask, sems.at[1])
    copies = [
        pltpu.make_async_copy(
            records_hbm.at[pl.ds(q * LANES, LANES)], records.at[pl.ds(q * LANES, LANES)], sems.at[2 + q]
        )
        for q in range(tiles)
    ]
    for copy in [seen_copy, mask_copy] + copies:
        copy.start()
    order = one_hot(count, count, lambda r, c: c == channel_of(r, blocks, own))
    lines = share * BLOCK
    halves = LAGS // LANES
    extra = 2 * halves * share * own
    place = one_hot(
        dests * extra,
        2 * halves * lines,
        lambda r, c: (c % BLOCK // own == r // extra)
        & (c // BLOCK * own + c % own == r % extra),
    )
    seen_copy.wait()
    mask_copy.wait()
    window = jnp.concatenate(
        [mask[pl.ds(start + i, 1), :] + jnp.zeros((BLOCK, 1), jnp.int32) for i in range(share)], axis=0
    )
    seen = jnp.where(window != 0, observed[...].reshape(lines, LAGS), MASKED)
    high = seen.astype(jnp.bfloat16)
    low = (seen - high.astype(jnp.float32)).astype(jnp.bfloat16)
    parts = [v[:, h * LANES : (h + 1) * LANES] for v in (high, low) for h in range(halves)]
    packed = dot(place, jnp.concatenate(parts, axis=0)).astype(jnp.bfloat16)
    out_ref[:, tiles * rows :, :] = packed.reshape(dests, extra, LANES)
    for q, copy in enumerate(copies):
        copy.wait()
        moved = dot(order, records[q * LANES : (q + 1) * LANES, :], _NT).astype(jnp.bfloat16)
        out_ref[:, q * rows : (q + 1) * rows, :] = moved.reshape(dests, rows, LANES)


def prepare_kernel(
    segs, recs, blocks, own, after_ref, pairs_ref, table_hbm, lag_hbm, table_ref, lag_ref, take_ref, give_ref, find_ref, order_ref, sems
):
    copies = [
        pltpu.make_async_copy(table_hbm, table_ref, sems.at[0]),
        pltpu.make_async_copy(lag_hbm, lag_ref, sems.at[1]),
    ]
    for copy in copies:
        copy.start()
    pair_total = pairs_ref.shape[0]
    count = segs * recs * blocks * own
    lines = pair_total * own
    every = recs * lines

    def picks(side, line):
        pair = line % lines // own
        block = jnp.zeros_like(line)
        for n in range(pair_total):
            block = jnp.where(pair == n, pairs_ref[n, side], block)
        return ((block // blocks * recs + line // lines) * blocks + block % blocks) * own + line % own

    for side in range(2):
        line = lax.broadcasted_iota(jnp.int32, (every, count), 0)
        row = lax.broadcasted_iota(jnp.int32, (every, count), 1)
        hit = jnp.where(picks(side, line) == row, 1.0, 0.0).astype(jnp.bfloat16)
        take_ref[side * every : (side + 1) * every, :] = hit
        line = lax.broadcasted_iota(jnp.int32, (count, 2 * every), 1)
        row = lax.broadcasted_iota(jnp.int32, (count, 2 * every), 0)
        hit = jnp.where(picks(side, line % every) == row, 1.0, 0.0)
        if side == 0:
            first = hit
        else:
            hit = jnp.where(line < every, first, hit).astype(jnp.bfloat16)
            give_ref[:, 0 : 2 * every] = hit
            give_ref[:, 2 * every :] = hit
    halves = LAGS // LANES
    extra = find_ref.shape[2]
    for h in range(halves):
        find_ref[h] = one_hot(
            lines,
            extra,
            lambda q, c: (c % (2 * halves * own) % (halves * own) == h * own + q % own)
            & (c // (2 * halves * own) == q // own),
        )
    side = order_ref.shape[0]
    order_ref[...] = one_hot(side, side, lambda r, c: c == channel_of(r, blocks, own))
    for copy in copies:
        copy.wait()


def unpack_kernel(rows_hbm, order_ref, out_hbm, rows, out, in_sems, out_sems):
    span, count = out.shape
    tiles = span // LANES
    cuts = [pl.ds(q * LANES, LANES) for q in range(tiles)]
    arrive = [pltpu.make_async_copy(rows_hbm.at[:, :, cut], rows.at[:, :, cut], in_sems.at[q]) for q, cut in enumerate(cuts)]
    leave = [pltpu.make_async_copy(out.at[cut], out_hbm.at[cut], out_sems.at[q]) for q, cut in enumerate(cuts)]
    for copy in arrive:
        copy.start()
    for q in range(tiles):
        arrive[q].wait()
        held = rows[:, :, q * LANES : (q + 1) * LANES].reshape(count, LANES)
        out[q * LANES : (q + 1) * LANES, :] = dot(held, order_ref[...], _TN).astype(jnp.bfloat16)
        leave[q].start()
    for copy in leave:
        copy.wait()


def main_kernel(segs, recs, blocks, own, rows_ref, table_ref, lag_ref, take_ref, give_ref, find_ref, out_ref):
    span = S // SPANS
    band = F // SPANS
    count = segs * recs * blocks * own
    every = take_ref.shape[0] // 2
    lines = every // recs
    rows = blocks * own
    tiles = span // LANES
    ways = segs * recs
    folds = []
    for f in range(SPANS):
        parts = [
            rows_ref[f * ways : (f + 1) * ways, q * rows : (q + 1) * rows, :].reshape(count, LANES)
            for q in range(tiles)
        ]
        folds.append(jnp.concatenate(parts, axis=1).astype(jnp.float32))
    even, odd = folds[0] + folds[2], folds[1] + folds[3]
    e_part, d_part = folds[0] - folds[2], folds[1] - folds[3]
    both = jnp.concatenate([e_part, d_part], axis=0).astype(jnp.bfloat16)
    sides = []
    total = None
    for j in range(SPANS):
        if j % 2 == 0:
            signal = even + odd if j == 0 else even - odd
            part = dot(signal.astype(jnp.bfloat16), table_ref[j])
        else:
            mixed = dot(both, table_ref[j])
            e_c, e_s = mixed[:count, :band], mixed[:count, band:]
            d_c, d_s = mixed[count:, :band], mixed[count:, band:]
            sign = 1.0 if j == 1 else -1.0
            part = jnp.concatenate([e_c + sign * d_s, e_s - sign * d_c], axis=1)
        chosen = dot(take_ref[...], part.astype(jnp.bfloat16))
        a0, a1 = chosen[:every, :band], chosen[:every, band:]
        b0, b1 = chosen[every:, :band], chosen[every:, band:]
        sides.append((a0, a1, b0, b1))
        cross = jnp.concatenate([a0 * b0 + a1 * b1, a1 * b0 - a0 * b1], axis=1)
        term = dot(cross.astype(jnp.bfloat16), lag_ref[j])
        total = term if total is None else total + term
    synthetic = total[:lines]
    for r in range(1, recs):
        synthetic = synthetic + total[r * lines : (r + 1) * lines]

    packed = rows_ref[:, tiles * rows :, :].reshape(find_ref.shape[2], LANES)
    seen = jnp.concatenate([dot(find_ref[h], packed) for h in range(LAGS // LANES)], axis=1)
    weights = jnp.where(seen < 0.5 * MASKED, jnp.tanh(synthetic - seen), 0.0).astype(jnp.bfloat16)

    even, odd = None, None
    for j in range(SPANS):
        a0, a1, b0, b1 = sides[j]
        adjoint = dot(weights, lag_ref[j], _NT).astype(jnp.bfloat16).astype(jnp.float32)
        adjoint = jnp.concatenate([adjoint] * recs, axis=0)
        g0, g1 = adjoint[:, :band], adjoint[:, band:]
        first = jnp.concatenate([g0 * b0 - g1 * b1, g0 * b1 + g1 * b0], axis=1)
        second = jnp.concatenate([g0 * a0 + g1 * a1, g0 * a1 - g1 * a0], axis=1)
        terms = jnp.concatenate([first, second], axis=0)
        high = terms.astype(jnp.bfloat16)
        low = (terms - high.astype(jnp.float32)).astype(jnp.bfloat16)
        grad = dot(give_ref[...], jnp.concatenate([high, low], axis=0))
        if j % 2 == 0:
            part = dot(grad.astype(jnp.bfloat16), table_ref[j], _NT)
            even = (part, part) if j == 0 else (even[0] + part, even[1] - part)
        else:
            turned = jnp.concatenate([-grad[:, band:], grad[:, :band]], axis=1)
            stacked = jnp.concatenate([grad, turned], axis=0).astype(jnp.bfloat16)
            part = dot(stacked, table_ref[j], _NT)
            u, v = part[:count], part[count:]
            odd = (u, v) if j == 1 else (odd[0] + u, odd[1] - v)
    for f in range(SPANS):
        base, side = even[f % 2], odd[f % 2]
        value = base + side if f < 2 else base - side
        out_ref[f * ways : (f + 1) * ways, :, :] = value.astype(jnp.bfloat16).reshape(ways, rows, span)


def by_own_k(records, pairs, observed, lag_mask):
    fibres, segs, recs = (lax.axis_size(a) for a in EVERY)
    devices = fibres * segs * recs
    own = BLOCK // devices
    span, count = records.shape[1:]
    blocks = count // BLOCK
    rows = blocks * own
    pair_total, pairs_dev = pairs.shape[0], observed.shape[0]
    share = pairs_dev // recs
    lines = pair_total * own
    every = recs * lines
    mine = segs * recs * rows
    extra = 2 * LAGS // LANES * share * own
    table = forward_table().reshape(F // SPANS, SPANS, 2, SPANS, span)[:, :, :, 0]
    table = np.ascontiguousarray(table.transpose(1, 3, 2, 0)).reshape(SPANS, span, S // SPANS)
    lags = lag_table().reshape(F // SPANS, SPANS, 2, LAGS)
    lags = np.ascontiguousarray(lags.transpose(1, 2, 0, 3)).reshape(SPANS, S // SPANS, LAGS)
    low = jnp.bfloat16
    vmem = pl.BlockSpec(memory_space=pltpu.VMEM)
    hbm = pl.BlockSpec(memory_space=pl.ANY)
    smem = pl.BlockSpec(memory_space=pltpu.SMEM)
    limit = pltpu.CompilerParams(vmem_limit_bytes=48 * 2**20)
    send = pl.pallas_call(
        functools.partial(pack_kernel, blocks, own),
        out_shape=jax.ShapeDtypeStruct((devices, span // LANES * rows + extra, LANES), low),
        in_specs=[hbm] * 3,
        out_specs=vmem,
        scratch_shapes=[
            pltpu.VMEM((span, count), low),
            pltpu.VMEM((share, BLOCK, LAGS), jnp.float32),
            pltpu.VMEM(lag_mask.shape, jnp.int32),
            pltpu.SemaphoreType.DMA((2 + span // LANES,)),
        ],
    )(records[0], observed, lag_mask)
    held = lax.all_to_all(send, EVERY, 0, 0, tiled=True)
    prepared = pl.pallas_call(
        functools.partial(prepare_kernel, segs, recs, blocks, own),
        out_shape=[
            jax.ShapeDtypeStruct(table.shape, low),
            jax.ShapeDtypeStruct(lags.shape, low),
            jax.ShapeDtypeStruct((2 * every, mine), low),
            jax.ShapeDtypeStruct((mine, 4 * every), low),
            jax.ShapeDtypeStruct((LAGS // LANES, lines, devices * extra), low),
            jax.ShapeDtypeStruct((count, count), low),
        ],
        in_specs=[hbm, smem, hbm, hbm],
        out_specs=[vmem] * 6,
        scratch_shapes=[pltpu.SemaphoreType.DMA((2,))],
        compiler_params=limit,
        cost_estimate=pl.CostEstimate(flops=0, bytes_accessed=4 * 2**20, transcendentals=0),
    )(send, pairs, jnp.asarray(table), jnp.asarray(lags))
    order = prepared[-1]
    back = pl.pallas_call(
        functools.partial(main_kernel, segs, recs, blocks, own),
        out_shape=jax.ShapeDtypeStruct((devices, rows, span), low),
        in_specs=[vmem] * 6,
        out_specs=vmem,
        compiler_params=limit,
    )(held, *prepared[:-1])
    back = lax.all_to_all(back, EVERY, 0, 0, tiled=True)
    out = pl.pallas_call(
        unpack_kernel,
        out_shape=jax.ShapeDtypeStruct((span, count), low),
        in_specs=[hbm, vmem],
        out_specs=hbm,
        scratch_shapes=[
            pltpu.VMEM((devices, rows, span), low),
            pltpu.VMEM((span, count), low),
            pltpu.SemaphoreType.DMA((span // LANES,)),
            pltpu.SemaphoreType.DMA((span // LANES,)),
        ],
    )(back, order)
    return out[None]


def by_band(records, pairs, observed, lag_mask):
    fibres, segs = lax.axis_size("fibre"), lax.axis_size("seg")
    own = BLOCK // fibres
    span, count = records.shape[1:]
    blocks = count // BLOCK
    total_blocks = blocks * segs
    pair_total, pairs_dev = pairs.shape[0], observed.shape[0]
    low = jnp.bfloat16
    band = F // segs
    start = lax.axis_index("seg") * band
    table = lax.dynamic_slice_in_dim(jnp.asarray(forward_table()), start, band, 0)
    lags = lax.dynamic_slice_in_dim(jnp.asarray(lag_table()), start, band, 0)
    f32 = functools.partial(jnp.einsum, preferred_element_type=jnp.float32)
    grid = records.reshape(span, blocks, fibres, own).transpose(2, 0, 1, 3)
    signal = lax.all_to_all(grid, "fibre", 0, 0, tiled=True).reshape(S, blocks, own)
    signal = lax.all_gather(signal, "seg", axis=1, tiled=True)
    spectra = f32("wpt,tbk->wpbk", table, signal).astype(low)
    ids = jnp.arange(total_blocks)
    take = [(pairs[:, side, None] == ids).astype(low) for side in range(2)]
    a0, a1 = (f32("nb,wbk->wnk", take[0], spectra[:, p]) for p in range(2))
    b0, b1 = (f32("nb,wbk->wnk", take[1], spectra[:, p]) for p in range(2))
    cross = jnp.stack([a0 * b0 + a1 * b1, a1 * b0 - a0 * b1], axis=1).astype(low)
    corr = f32("wpnk,wpl->nkl", cross, lags)
    corr = corr.reshape(fibres, segs, pairs_dev, own, LAGS)
    corr = lax.psum_scatter(corr, "seg", scatter_dimension=1)
    synthetic = lax.psum(corr, "rec").reshape(fibres * pairs_dev, own, LAGS)
    seen = observed.reshape(pairs_dev, fibres, own, LAGS).transpose(1, 0, 2, 3)
    seen = lax.all_to_all(seen, "fibre", 0, 0, tiled=True).reshape(fibres * pairs_dev, own, LAGS)
    window = lax.all_gather(lag_mask.astype(jnp.float32), "fibre", axis=0, tiled=True)
    weights = (window[:, None, :] * jnp.tanh(synthetic - seen)).astype(low)
    weights = lax.all_gather(weights.reshape(fibres, pairs_dev, own, LAGS), "seg", axis=1)
    weights = weights.reshape(pair_total, own, LAGS)
    adjoint = f32("nkl,wpl->wpnk", weights, lags).astype(low).astype(jnp.float32)
    g0, g1 = adjoint[:, 0], adjoint[:, 1]

    def added(side, terms):
        high = terms.astype(low)
        rest = (terms - high.astype(jnp.float32)).astype(low)
        return f32("nb,wnk->wbk", take[side], high) + f32("nb,wnk->wbk", take[side], rest)

    grad = jnp.stack(
        [
            added(0, g0 * b0 - g1 * b1) + added(1, g0 * a0 + g1 * a1),
            added(0, g0 * b1 + g1 * b0) + added(1, g0 * a1 - g1 * a0),
        ],
        axis=1,
    ).astype(low)
    sources = f32("wpbk,wpt->tbk", grad, table)
    sources = lax.psum_scatter(sources, "seg", scatter_dimension=1, tiled=True).astype(low)
    sources = sources.reshape(fibres, span, blocks, own)
    sources = lax.all_to_all(sources, "fibre", 0, 0, tiled=True)
    return sources.transpose(1, 2, 0, 3).reshape(1, span, count)


def solution(mesh):
    devices = mesh.shape["fibre"] * mesh.shape["seg"] * mesh.shape["rec"]
    in_specs = (
        P("rec", "fibre", ("groups", "seg")),
        P(),
        P(("groups", "fibre", "seg"), None, None),
        P(("groups", "fibre", "seg"), None),
    )
    out_specs = P("rec", "fibre", ("groups", "seg"))
    small = mesh.shape["fibre"] == SPANS and BLOCK % devices == 0
    return jax.shard_map(
        by_own_k if small else by_band,
        mesh=mesh,
        in_specs=in_specs,
        out_specs=out_specs,
        check_vma=False,
    )
```

```python
import functools

import jax
import jax.numpy as jnp
import numpy as np
from jax import lax
from jax.experimental import pallas as pl
from jax.experimental.pallas import tpu as pltpu
from jax.sharding import PartitionSpec as P

S = 2048
F = 1024
LAGS = 256
BLOCK = 32
SPANS = 4
MASKED = 16384.0
LANES = 128
EVERY = ("fibre", "seg", "rec")

_NT = (((1,), (1,)), ((), ()))
_TN = (((0,), (0,)), ((), ()))


def wave_table(freq, shift, scale):
    phase = freq[:, None].astype(np.int64) * shift[None, :] % S
    angles = phase.astype(np.float32) * np.float32(2.0 * np.pi / S)
    factor = np.float32(1.0) / np.sqrt(np.float32(scale))
    parts = [(np.cos(angles) * factor), (-np.sin(angles) * factor)]
    return np.stack(parts, axis=1).astype(jnp.bfloat16)


def forward_table():
    return wave_table(np.arange(F), np.arange(S), S)


def lag_table():
    return wave_table(np.arange(F), (np.arange(LAGS) - LAGS // 2) % S, F)


def dot(a, b, dims=(((1,), (0,)), ((), ()))):
    return lax.dot_general(a, b, dims, preferred_element_type=jnp.float32)


def one_hot(rows, cols, hit):
    row = lax.broadcasted_iota(jnp.int32, (rows, cols), 0)
    col = lax.broadcasted_iota(jnp.int32, (rows, cols), 1)
    return jnp.where(hit(row, col), 1.0, 0.0).astype(jnp.bfloat16)


def channel_of(row, blocks, own):
    return row % (blocks * own) // own * BLOCK + row // (blocks * own) * own + row % own


def pack_kernel(blocks, own, records_hbm, observed_hbm, mask_hbm, out_ref, records, observed, mask, sems):
    span, count = records.shape
    dests = BLOCK // own
    rows = blocks * own
    tiles = span // LANES
    share = observed.shape[0]
    start = lax.axis_index("rec") * share
    seen_copy = pltpu.make_async_copy(observed_hbm.at[pl.ds(start, share)], observed, sems.at[0])
    mask_copy = pltpu.make_async_copy(mask_hbm, mask, sems.at[1])
    records_copy = pltpu.make_async_copy(records_hbm, records, sems.at[2])
    for copy in (records_copy, seen_copy, mask_copy):
        copy.start()
    order = one_hot(count, count, lambda r, c: c == channel_of(r, blocks, own))
    lines = share * BLOCK
    halves = LAGS // LANES
    extra = 2 * halves * share * own
    place = one_hot(
        dests * extra,
        2 * halves * lines,
        lambda r, c: (c % BLOCK // own == r // extra)
        & (c % own == r % own)
        & (c // lines == r % (2 * halves * own) // own)
        & (c % lines // BLOCK == r % extra // (2 * halves * own)),
    )
    seen_copy.wait()
    mask_copy.wait()
    window = jnp.concatenate(
        [mask[pl.ds(start + i, 1), :] + jnp.zeros((BLOCK, 1), jnp.int32) for i in range(share)], axis=0
    )
    seen = jnp.where(window != 0, observed[...].reshape(lines, LAGS), MASKED)
    high = seen.astype(jnp.bfloat16)
    low = (seen - high.astype(jnp.float32)).astype(jnp.bfloat16)
    parts = [v[:, h * LANES : (h + 1) * LANES] for v in (high, low) for h in range(halves)]
    packed = dot(place, jnp.concatenate(parts, axis=0)).astype(jnp.bfloat16)
    out_ref[:, tiles * rows :, :] = packed.reshape(dests, extra, LANES)
    records_copy.wait()
    moved = dot(order, records[...], _NT).astype(jnp.bfloat16)
    for q in range(tiles):
        part = moved[:, q * LANES : (q + 1) * LANES]
        out_ref[:, q * rows : (q + 1) * rows, :] = part.reshape(dests, rows, LANES)


def prepare_kernel(segs, recs, blocks, own, pairs_ref, *refs):
    constants = (len(refs) - 3) // 2
    take_ref, give_ref = refs[2 * constants : 2 * constants + 2]
    copies = [
        pltpu.make_async_copy(refs[i], refs[constants + i], refs[-1].at[i]) for i in range(constants)
    ]
    for copy in copies:
        copy.start()
    pair_total = pairs_ref.shape[0]
    count = segs * recs * blocks * own
    lines = pair_total * own
    every = recs * lines

    def picks(side, line):
        pair = line % lines // own
        block = jnp.zeros_like(line)
        for n in range(pair_total):
            block = jnp.where(pair == n, pairs_ref[n, side], block)
        return ((block // blocks * recs + line // lines) * blocks + block % blocks) * own + line % own

    for side in range(2):
        line = lax.broadcasted_iota(jnp.int32, (every, count), 0)
        row = lax.broadcasted_iota(jnp.int32, (every, count), 1)
        hit = jnp.where(picks(side, line) == row, 1.0, 0.0).astype(jnp.bfloat16)
        take_ref[side * every : (side + 1) * every, :] = hit
    line = lax.broadcasted_iota(jnp.int32, (count, 2 * every), 1)
    row = lax.broadcasted_iota(jnp.int32, (count, 2 * every), 0)
    first, second = (picks(side, line % every) for side in range(2))
    chosen = jnp.where(line < every, first, second)
    hit = jnp.where(chosen == row, 1.0, 0.0).astype(jnp.bfloat16)
    give_ref[:, 0 : 2 * every] = hit
    give_ref[:, 2 * every :] = hit
    for copy in copies:
        copy.wait()


def unpack_kernel(rows, order_ref, out_hbm, out, out_sems):
    span, count = out.shape
    tiles = span // LANES
    cuts = [pl.ds(q * LANES, LANES) for q in range(tiles)]
    leave = [pltpu.make_async_copy(out.at[cut], out_hbm.at[cut], out_sems.at[q]) for q, cut in enumerate(cuts)]
    for q in range(tiles):
        held = rows[:, :, q * LANES : (q + 1) * LANES].reshape(count, LANES)
        out[q * LANES : (q + 1) * LANES, :] = dot(held, order_ref[...], _TN).astype(jnp.bfloat16)
        leave[q].start()
    for copy in leave:
        copy.wait()


def main_kernel(segs, recs, blocks, own, rows_ref, table_ref, lag_ref, take_ref, give_ref, find_ref, out_ref):
    span = S // SPANS
    band = F // SPANS
    count = segs * recs * blocks * own
    every = take_ref.shape[0] // 2
    lines = every // recs
    rows = blocks * own
    tiles = span // LANES
    ways = segs * recs
    folds = []
    for f in range(SPANS):
        parts = [
            rows_ref[f * ways : (f + 1) * ways, q * rows : (q + 1) * rows, :].reshape(count, LANES)
            for q in range(tiles)
        ]
        folds.append(jnp.concatenate(parts, axis=1).astype(jnp.float32))
    even, odd = folds[0] + folds[2], folds[1] + folds[3]
    e_part, d_part = folds[0] - folds[2], folds[1] - folds[3]
    both = jnp.concatenate([e_part, d_part], axis=0).astype(jnp.bfloat16)
    reals, imags = [], []
    for j in range(SPANS):
        if j % 2 == 0:
            signal = even + odd if j == 0 else even - odd
            part = dot(signal.astype(jnp.bfloat16), table_ref[j])
            real, imag = part[:, :band], part[:, band:]
        else:
            mixed = dot(both, table_ref[j])
            e_c, e_s = mixed[:count, :band], mixed[:count, band:]
            d_c, d_s = mixed[count:, :band], mixed[count:, band:]
            real, imag = (e_c + d_s, e_s - d_c) if j == 1 else (e_c - d_s, e_s + d_c)
        reals.append(real.astype(jnp.bfloat16))
        imags.append(imag.astype(jnp.bfloat16))
    spectra = jnp.concatenate(reals + imags, axis=1)
    chosen = dot(take_ref[...], spectra)
    a0, a1 = chosen[:every, :F], chosen[:every, F:]
    b0, b1 = chosen[every:, :F], chosen[every:, F:]
    cross_re = (a0 * b0 + a1 * b1).astype(jnp.bfloat16)
    cross_im = (a1 * b0 - a0 * b1).astype(jnp.bfloat16)
    total = dot(jnp.concatenate([cross_re, cross_im], axis=1), lag_ref[...])
    synthetic = total[:lines]
    for r in range(1, recs):
        synthetic = synthetic + total[r * lines : (r + 1) * lines]

    packed = rows_ref[:, tiles * rows :, :].reshape(find_ref.shape[2], LANES)
    seen = jnp.concatenate([dot(find_ref[h], packed) for h in range(LAGS // LANES)], axis=1)
    weights = jnp.where(seen < 0.5 * MASKED, jnp.tanh(synthetic - seen), 0.0).astype(jnp.bfloat16)

    adjoint = dot(weights, lag_ref[...], _NT).astype(jnp.bfloat16).astype(jnp.float32)
    adjoint = jnp.concatenate([adjoint] * recs, axis=0)
    g0, g1 = adjoint[:, :F], adjoint[:, F:]
    first = jnp.concatenate([g0 * b0 - g1 * b1, g0 * b1 + g1 * b0], axis=1)
    second = jnp.concatenate([g0 * a0 + g1 * a1, g0 * a1 - g1 * a0], axis=1)
    terms = jnp.concatenate([first, second], axis=0)
    high = terms.astype(jnp.bfloat16)
    low = (terms - high.astype(jnp.float32)).astype(jnp.bfloat16)
    grad = dot(give_ref[...], jnp.concatenate([high, low], axis=0)).astype(jnp.bfloat16)
    even, odd = None, None
    for j in range(SPANS):
        real = grad[:, j * band : (j + 1) * band]
        imag = grad[:, F + j * band : F + (j + 1) * band]
        line = jnp.concatenate([real, imag], axis=1)
        if j % 2 == 0:
            part = dot(line, table_ref[j], _NT)
            even = (part, part) if j == 0 else (even[0] + part, even[1] - part)
        else:
            turned = jnp.concatenate([-imag, real], axis=1)
            part = dot(jnp.concatenate([line, turned], axis=0), table_ref[j], _NT)
            u, v = part[:count], part[count:]
            odd = (u, v) if j == 1 else (odd[0] + u, odd[1] - v)
    for f in range(SPANS):
        base, side = even[f % 2], odd[f % 2]
        value = base + side if f < 2 else base - side
        out_ref[f * ways : (f + 1) * ways, :, :] = value.astype(jnp.bfloat16).reshape(ways, rows, span)


def by_own_k(records, pairs, observed, lag_mask):
    fibres, segs, recs = (lax.axis_size(a) for a in EVERY)
    devices = fibres * segs * recs
    own = BLOCK // devices
    span, count = records.shape[1:]
    blocks = count // BLOCK
    rows = blocks * own
    pair_total, pairs_dev = pairs.shape[0], observed.shape[0]
    share = pairs_dev // recs
    lines = pair_total * own
    every = recs * lines
    mine = segs * recs * rows
    extra = 2 * LAGS // LANES * share * own
    table = forward_table().reshape(F // SPANS, SPANS, 2, SPANS, span)[:, :, :, 0]
    table = np.ascontiguousarray(table.transpose(1, 3, 2, 0)).reshape(SPANS, span, S // SPANS)
    lags = lag_table().reshape(F // SPANS, SPANS, 2, LAGS)
    lags = np.ascontiguousarray(lags.transpose(2, 1, 0, 3)).reshape(2 * F, LAGS)
    low = jnp.bfloat16
    order = channel_of(np.arange(count), blocks, own)[:, None] == np.arange(count)
    order = order.astype(low)
    halves = LAGS // LANES
    line, place = np.arange(lines)[:, None], np.arange(devices * extra)
    same = (place // (extra // share) == line // own) & (place % own == line % own)
    find = np.stack([same & (place % (halves * own) // own == h) for h in range(halves)]).astype(low)
    vmem = pl.BlockSpec(memory_space=pltpu.VMEM)
    hbm = pl.BlockSpec(memory_space=pl.ANY)
    smem = pl.BlockSpec(memory_space=pltpu.SMEM)
    limit = pltpu.CompilerParams(vmem_limit_bytes=16 * 2**20)
    send = pl.pallas_call(
        functools.partial(pack_kernel, blocks, own),
        out_shape=pltpu.VMEM((devices, span // LANES * rows + extra, LANES), low),
        in_specs=[hbm] * 3,
        out_specs=vmem,
        scratch_shapes=[
            pltpu.VMEM((span, count), low),
            pltpu.VMEM((share, BLOCK, LAGS), jnp.float32),
            pltpu.VMEM(lag_mask.shape, jnp.int32),
            pltpu.SemaphoreType.DMA((3,)),
        ],
        compiler_params=limit,
    )(*(pltpu.with_memory_space_constraint(x, pltpu.HBM) for x in (records[0], observed, lag_mask)))
    held = lax.all_to_all(send, EVERY, 0, 0, tiled=True)
    constants = [jnp.asarray(c) for c in (table, lags, find)]
    table, lags, find, take, give = pl.pallas_call(
        functools.partial(prepare_kernel, segs, recs, blocks, own),
        out_shape=[pltpu.VMEM(c.shape, low) for c in constants]
        + [pltpu.VMEM((2 * every, mine), low), pltpu.VMEM((mine, 4 * every), low)],
        in_specs=[smem] + [hbm] * len(constants),
        out_specs=[vmem] * 5,
        scratch_shapes=[pltpu.SemaphoreType.DMA((len(constants),))],
        compiler_params=limit,
        cost_estimate=pl.CostEstimate(flops=0, bytes_accessed=4 * 2**20, transcendentals=0),
    )(pairs, *(pltpu.with_memory_space_constraint(c, pltpu.HBM) for c in constants))
    back = pl.pallas_call(
        functools.partial(main_kernel, segs, recs, blocks, own),
        out_shape=jax.ShapeDtypeStruct((devices, rows, span), low),
        in_specs=[vmem] * 6,
        out_specs=vmem,
        compiler_params=limit,
    )(held, table, lags, take, give, find)
    back = lax.all_to_all(back, EVERY, 0, 0, tiled=True)
    out = pl.pallas_call(
        unpack_kernel,
        out_shape=jax.ShapeDtypeStruct((span, count), low),
        in_specs=[vmem, vmem],
        out_specs=hbm,
        scratch_shapes=[
            pltpu.VMEM((span, count), low),
            pltpu.SemaphoreType.DMA((span // LANES,)),
        ],
        compiler_params=limit,
    )(pltpu.with_memory_space_constraint(back, pltpu.VMEM), jnp.asarray(order))
    return out[None]


def by_band(records, pairs, observed, lag_mask):
    fibres, segs = lax.axis_size("fibre"), lax.axis_size("seg")
    own = BLOCK // fibres
    span, count = records.shape[1:]
    blocks = count // BLOCK
    total_blocks = blocks * segs
    pair_total, pairs_dev = pairs.shape[0], observed.shape[0]
    low = jnp.bfloat16
    band = F // segs
    start = lax.axis_index("seg") * band
    table = lax.dynamic_slice_in_dim(jnp.asarray(forward_table()), start, band, 0)
    lags = lax.dynamic_slice_in_dim(jnp.asarray(lag_table()), start, band, 0)
    f32 = functools.partial(jnp.einsum, preferred_element_type=jnp.float32)
    grid = records.reshape(span, blocks, fibres, own).transpose(2, 0, 1, 3)
    signal = lax.all_to_all(grid, "fibre", 0, 0, tiled=True).reshape(S, blocks, own)
    signal = lax.all_gather(signal, "seg", axis=1, tiled=True)
    spectra = f32("wpt,tbk->wpbk", table, signal).astype(low)
    ids = jnp.arange(total_blocks)
    take = [(pairs[:, side, None] == ids).astype(low) for side in range(2)]
    a0, a1 = (f32("nb,wbk->wnk", take[0], spectra[:, p]) for p in range(2))
    b0, b1 = (f32("nb,wbk->wnk", take[1], spectra[:, p]) for p in range(2))
    cross = jnp.stack([a0 * b0 + a1 * b1, a1 * b0 - a0 * b1], axis=1).astype(low)
    corr = f32("wpnk,wpl->nkl", cross, lags)
    corr = corr.reshape(fibres, segs, pairs_dev, own, LAGS)
    corr = lax.psum_scatter(corr, "seg", scatter_dimension=1)
    synthetic = lax.psum(corr, "rec").reshape(fibres * pairs_dev, own, LAGS)
    seen = observed.reshape(pairs_dev, fibres, own, LAGS).transpose(1, 0, 2, 3)
    seen = lax.all_to_all(seen, "fibre", 0, 0, tiled=True).reshape(fibres * pairs_dev, own, LAGS)
    window = lax.all_gather(lag_mask.astype(jnp.float32), "fibre", axis=0, tiled=True)
    weights = (window[:, None, :] * jnp.tanh(synthetic - seen)).astype(low)
    weights = lax.all_gather(weights.reshape(fibres, pairs_dev, own, LAGS), "seg", axis=1)
    weights = weights.reshape(pair_total, own, LAGS)
    adjoint = f32("nkl,wpl->wpnk", weights, lags).astype(low).astype(jnp.float32)
    g0, g1 = adjoint[:, 0], adjoint[:, 1]

    def added(side, terms):
        high = terms.astype(low)
        rest = (terms - high.astype(jnp.float32)).astype(low)
        return f32("nb,wnk->wbk", take[side], high) + f32("nb,wnk->wbk", take[side], rest)

    grad = jnp.stack(
        [
            added(0, g0 * b0 - g1 * b1) + added(1, g0 * a0 + g1 * a1),
            added(0, g0 * b1 + g1 * b0) + added(1, g0 * a1 - g1 * a0),
        ],
        axis=1,
    ).astype(low)
    sources = f32("wpbk,wpt->tbk", grad, table)
    sources = lax.psum_scatter(sources, "seg", scatter_dimension=1, tiled=True).astype(low)
    sources = sources.reshape(fibres, span, blocks, own)
    sources = lax.all_to_all(sources, "fibre", 0, 0, tiled=True)
    return sources.transpose(1, 2, 0, 3).reshape(1, span, count)


def solution(mesh):
    devices = mesh.shape["fibre"] * mesh.shape["seg"] * mesh.shape["rec"]
    in_specs = (
        P("rec", "fibre", ("groups", "seg")),
        P(),
        P(("groups", "fibre", "seg"), None, None),
        P(("groups", "fibre", "seg"), None),
    )
    out_specs = P("rec", "fibre", ("groups", "seg"))
    small = mesh.shape["fibre"] == SPANS and BLOCK % devices == 0
    return jax.shard_map(
        by_own_k if small else by_band,
        mesh=mesh,
        in_specs=in_specs,
        out_specs=out_specs,
        check_vma=False,
    )
```

```python
import functools

import jax
import jax.numpy as jnp
import numpy as np
from jax import lax
from jax.experimental import pallas as pl
from jax.experimental.pallas import tpu as pltpu
from jax.sharding import PartitionSpec as P

S = 2048
F = 1024
LAGS = 256
BLOCK = 32
SPANS = 4
MASKED = 16384.0
LANES = 128

_NT = (((1,), (1,)), ((), ()))
_TN = (((0,), (0,)), ((), ()))


def wave_table(freq, shift, scale):
    phase = freq[:, None].astype(np.int64) * shift[None, :] % S
    angles = phase.astype(np.float32) * np.float32(2.0 * np.pi / S)
    factor = np.float32(1.0) / np.sqrt(np.float32(scale))
    parts = [(np.cos(angles) * factor), (-np.sin(angles) * factor)]
    return np.stack(parts, axis=1).astype(jnp.bfloat16)


def forward_table():
    return wave_table(np.arange(F), np.arange(S), S)


def lag_table():
    return wave_table(np.arange(F), (np.arange(LAGS) - LAGS // 2) % S, F)


def dot(a, b, dims=(((1,), (0,)), ((), ()))):
    return lax.dot_general(a, b, dims, preferred_element_type=jnp.float32)


def one_hot(rows, cols, hit):
    row = lax.broadcasted_iota(jnp.int32, (rows, cols), 0)
    col = lax.broadcasted_iota(jnp.int32, (rows, cols), 1)
    return jnp.where(hit(row, col), 1.0, 0.0).astype(jnp.bfloat16)


def channel_of(row, fibre, blocks, own):
    to = row // (blocks * own) ^ fibre
    return row % (blocks * own) // own * BLOCK + to * own + row % own


def channel_order(fibre, blocks, own):
    count = blocks * BLOCK
    return one_hot(count, count, lambda r, c: c == channel_of(r, fibre, blocks, own))


def pack_kernel(blocks, own, records_hbm, observed_hbm, mask_hbm, *refs):
    out_refs, (records, observed, mask, sems) = refs[:SPANS], refs[SPANS:]
    fibre = lax.axis_index("fibre")
    span, count = records.shape
    rows = blocks * own
    tiles = span // LANES
    share = observed.shape[0]
    start = lax.axis_index("rec") * share
    records_copy = pltpu.make_async_copy(records_hbm, records, sems.at[0])
    seen_copy = pltpu.make_async_copy(observed_hbm.at[pl.ds(start, share)], observed, sems.at[1])
    mask_copy = pltpu.make_async_copy(mask_hbm, mask, sems.at[2])
    for copy in (records_copy, seen_copy, mask_copy):
        copy.start()
    order = channel_order(fibre, blocks, own)
    lines = share * BLOCK
    halves = LAGS // LANES
    extra = 2 * halves * share * own
    place = one_hot(
        SPANS * extra,
        2 * halves * lines,
        lambda r, c: (c % BLOCK // own == r // extra ^ fibre)
        & (c % own == r % own)
        & (c // lines == r % (2 * halves * own) // own)
        & (c % lines // BLOCK == r % extra // (2 * halves * own)),
    )
    seen_copy.wait()
    mask_copy.wait()
    window = jnp.concatenate(
        [mask[pl.ds(start + i, 1), :] + jnp.zeros((BLOCK, 1), jnp.int32) for i in range(share)], axis=0
    )
    seen = jnp.where(window != 0, observed[...].reshape(lines, LAGS), MASKED)
    high = seen.astype(jnp.bfloat16)
    low = (seen - high.astype(jnp.float32)).astype(jnp.bfloat16)
    parts = [v[:, h * LANES : (h + 1) * LANES] for v in (high, low) for h in range(halves)]
    packed = dot(place, jnp.concatenate(parts, axis=0)).astype(jnp.bfloat16)
    for k, out_ref in enumerate(out_refs):
        out_ref[tiles * rows :, :] = packed[k * extra : (k + 1) * extra]
    records_copy.wait()
    moved = dot(order, records[...], _NT).astype(jnp.bfloat16)
    for k, out_ref in enumerate(out_refs):
        for q in range(tiles):
            part = moved[k * rows : (k + 1) * rows, q * LANES : (q + 1) * LANES]
            out_ref[q * rows : (q + 1) * rows, :] = part


def prepare_kernel(segs, blocks, own, pairs_dev, share, pairs_ref, *refs):
    constants = (len(refs) - 5) // 2
    take_ref, give_ref, find_ref, order_ref, sems = refs[2 * constants :]
    copies = [pltpu.make_async_copy(refs[i], refs[constants + i], sems.at[i]) for i in range(constants)]
    for copy in copies:
        copy.start()
    fibre, seg, rec = (lax.axis_index(axis) for axis in ("fibre", "seg", "rec"))
    pair_total = pairs_ref.shape[0]
    rows = blocks * own
    lines = pair_total * own

    def picks(side, line):
        block = jnp.zeros_like(line)
        for n in range(pair_total):
            block = jnp.where(line // own == n, pairs_ref[n, side], block)
        distance = (seg + segs - block // blocks) % segs
        return distance * rows + block % blocks * own + line % own

    for side in range(2):
        line = lax.broadcasted_iota(jnp.int32, (lines, segs * rows), 0)
        row = lax.broadcasted_iota(jnp.int32, (lines, segs * rows), 1)
        hit = jnp.where(picks(side, line) == row, 1.0, 0.0).astype(jnp.bfloat16)
        take_ref[side * lines : (side + 1) * lines, :] = hit
        line = lax.broadcasted_iota(jnp.int32, (rows, lines), 1)
        row = lax.broadcasted_iota(jnp.int32, (rows, lines), 0)
        hit = jnp.where(picks(side, line) == row, 1.0, 0.0).astype(jnp.bfloat16)
        give_ref[:, side * lines : (side + 1) * lines] = hit
    halves = LAGS // LANES
    extra = 2 * halves * share * own

    def here(half, line, place):
        part = place % extra
        owner = (place // extra % SPANS ^ fibre) * segs + (seg + segs - place // (extra * SPANS)) % segs
        pair = owner * pairs_dev + rec * share + part // (2 * halves * own)
        return (line // own == pair) & (line % own == part % own) & (part % (halves * own) // own == half)

    for h in range(halves):
        find_ref[h] = one_hot(lines, segs * SPANS * extra, functools.partial(here, h))
    order_ref[...] = channel_order(fibre, blocks, own)
    for copy in copies:
        copy.wait()


def correlate_kernel(segs, blocks, own, *refs):
    chunks = refs[: segs * SPANS]
    table_ref, lag_ref, take_ref, find_ref, chosen_ref, partial_ref = refs[segs * SPANS :]
    fibre = lax.axis_index("fibre")
    span = S // SPANS
    band = F // SPANS
    rows = blocks * own
    count = segs * rows
    lines = take_ref.shape[0] // 2
    tiles = span // LANES
    folds = []
    for k in range(SPANS):
        whole = [
            jnp.concatenate([chunks[u * SPANS + k][q * rows : (q + 1) * rows, :] for q in range(tiles)], axis=1)
            for u in range(segs)
        ]
        folds.append(jnp.concatenate(whole, axis=0).astype(jnp.float32))
    flip = fibre % 2 == 1
    turn = jnp.where(flip, -1.0, 1.0)
    late = jnp.where(fibre >= 2, -1.0, 1.0)
    near, far = folds[0] + folds[2], folds[1] + folds[3]
    near_gap, far_gap = folds[0] - folds[2], folds[1] - folds[3]
    e_part = late * jnp.where(flip, far_gap, near_gap)
    d_part = late * jnp.where(flip, near_gap, far_gap)
    both = jnp.concatenate([e_part, d_part], axis=0).astype(jnp.bfloat16)
    reals, imags = [], []
    for j in range(SPANS):
        if j % 2 == 0:
            signal = near + far if j == 0 else turn * (near - far)
            part = dot(signal.astype(jnp.bfloat16), table_ref[j])
            real, imag = part[:, :band], part[:, band:]
        else:
            mixed = dot(both, table_ref[j])
            e_c, e_s = mixed[:count, :band], mixed[:count, band:]
            d_c, d_s = mixed[count:, :band], mixed[count:, band:]
            real, imag = (e_c + d_s, e_s - d_c) if j == 1 else (e_c - d_s, e_s + d_c)
        reals.append(real.astype(jnp.bfloat16))
        imags.append(imag.astype(jnp.bfloat16))
    spectra = jnp.concatenate(reals + imags, axis=1)
    chosen = dot(take_ref[...], spectra)
    chosen_ref[...] = chosen.astype(jnp.bfloat16)
    a0, a1 = chosen[:lines, :F], chosen[:lines, F:]
    b0, b1 = chosen[lines:, :F], chosen[lines:, F:]
    cross_re = (a0 * b0 + a1 * b1).astype(jnp.bfloat16)
    cross_im = (a1 * b0 - a0 * b1).astype(jnp.bfloat16)
    partial = dot(jnp.concatenate([cross_re, cross_im], axis=1), lag_ref[...])
    packed = jnp.concatenate([chunk[tiles * rows :, :] for chunk in chunks], axis=0)
    seen = jnp.concatenate([dot(find_ref[h], packed) for h in range(LAGS // LANES)], axis=1)
    partial_ref[...] = partial - seen


def adjoint_kernel(blocks, own, chosen_ref, mine_ref, other_ref, table_ref, lag_ref, give_ref, *out_refs):
    fibre = lax.axis_index("fibre")
    band = F // SPANS
    lines = mine_ref.shape[0]
    count = blocks * own
    misfit = mine_ref[...] + other_ref[...]
    weights = jnp.where(misfit > -0.5 * MASKED, jnp.tanh(misfit), 0.0).astype(jnp.bfloat16)
    adjoint = dot(weights, lag_ref[...], _NT).astype(jnp.bfloat16).astype(jnp.float32)
    g0, g1 = adjoint[:, :F], adjoint[:, F:]
    a0 = chosen_ref[:lines, :F].astype(jnp.float32)
    a1 = chosen_ref[:lines, F:].astype(jnp.float32)
    b0 = chosen_ref[lines:, :F].astype(jnp.float32)
    b1 = chosen_ref[lines:, F:].astype(jnp.float32)
    low = jnp.bfloat16
    first = jnp.concatenate([(g0 * b0 - g1 * b1).astype(low), (g0 * b1 + g1 * b0).astype(low)], axis=1)
    second = jnp.concatenate([(g0 * a0 + g1 * a1).astype(low), (g0 * a1 - g1 * a0).astype(low)], axis=1)
    grad = dot(give_ref[...], jnp.concatenate([first, second], axis=0)).astype(low)
    even, odd = None, None
    for j in range(SPANS):
        real = grad[:, j * band : (j + 1) * band]
        imag = grad[:, F + j * band : F + (j + 1) * band]
        line = jnp.concatenate([real, imag], axis=1)
        if j % 2 == 0:
            part = dot(line, table_ref[j], _NT)
            even = (part, part) if j == 0 else (even[0] + part, even[1] - part)
        else:
            turned = jnp.concatenate([-imag, real], axis=1)
            part = dot(jnp.concatenate([line, turned], axis=0), table_ref[j], _NT)
            u, v = part[:count], part[count:]
            odd = (u, v) if j == 1 else (odd[0] + u, odd[1] - v)
    flip = fibre % 2 == 1
    late = jnp.where(fibre >= 2, -1.0, 1.0)
    for k, out_ref in enumerate(out_refs):
        other = flip if k % 2 == 0 else ~flip
        base = jnp.where(other, even[1], even[0])
        side = late * jnp.where(other, odd[1], odd[0])
        out_ref[...] = (base + side if k < 2 else base - side).astype(low)


def unpack_kernel(*refs):
    chunks, (order_ref, out_hbm, out, sems) = refs[:SPANS], refs[SPANS:]
    span = out.shape[0]
    cuts = [pl.ds(q * LANES, LANES) for q in range(span // LANES)]
    leave = [pltpu.make_async_copy(out.at[cut], out_hbm.at[cut], sems.at[q]) for q, cut in enumerate(cuts)]
    for q, copy in enumerate(leave):
        held = jnp.concatenate([chunk[:, q * LANES : (q + 1) * LANES] for chunk in chunks], axis=0)
        out[q * LANES : (q + 1) * LANES, :] = dot(held, order_ref[...], _TN).astype(jnp.bfloat16)
        copy.start()
    for copy in leave:
        copy.wait()


def by_own_k(records, pairs, observed, lag_mask):
    recs, segs, fibres = (lax.axis_size(axis) for axis in ("rec", "seg", "fibre"))
    own = BLOCK // fibres
    span, count = records.shape[1:]
    blocks = count // BLOCK
    rows = blocks * own
    pair_total, pairs_dev = pairs.shape[0], observed.shape[0]
    share = pairs_dev // recs
    lines = pair_total * own
    extra = 2 * LAGS // LANES * share * own
    table = forward_table().reshape(F // SPANS, SPANS, 2, SPANS, span)[:, :, :, 0]
    table = np.ascontiguousarray(table.transpose(1, 3, 2, 0)).reshape(SPANS, span, S // SPANS)
    lags = lag_table().reshape(F // SPANS, SPANS, 2, LAGS)
    lags = np.ascontiguousarray(lags.transpose(2, 1, 0, 3)).reshape(2 * F, LAGS)
    low = jnp.bfloat16
    vmem = pl.BlockSpec(memory_space=pltpu.VMEM)
    hbm = pl.BlockSpec(memory_space=pl.ANY)
    smem = pl.BlockSpec(memory_space=pltpu.SMEM)
    limit = pltpu.CompilerParams(vmem_limit_bytes=16 * 2**20)

    def along(axis, array, target):
        return lax.ppermute(array, axis, [(i, target(i)) for i in range(lax.axis_size(axis))])

    send = pl.pallas_call(
        functools.partial(pack_kernel, blocks, own),
        out_shape=[pltpu.VMEM((span // LANES * rows + extra, LANES), low)] * SPANS,
        in_specs=[hbm] * 3,
        out_specs=[vmem] * SPANS,
        scratch_shapes=[
            pltpu.VMEM((span, count), low),
            pltpu.VMEM((share, BLOCK, LAGS), jnp.float32),
            pltpu.VMEM(lag_mask.shape, jnp.int32),
            pltpu.SemaphoreType.DMA((3,)),
        ],
        compiler_params=limit,
    )(*(pltpu.with_memory_space_constraint(x, pltpu.HBM) for x in (records[0], observed, lag_mask)))
    held = [send[0]] + [along("fibre", send[k], lambda i: i ^ k) for k in range(1, SPANS)]
    for u in range(1, segs):
        held += [along("seg", chunk, lambda i: (i + u) % segs) for chunk in held[:SPANS]]
    constants = [jnp.asarray(c) for c in (table, lags)]
    table, lags, take, give, find, order = pl.pallas_call(
        functools.partial(prepare_kernel, segs, blocks, own, pairs_dev, share),
        out_shape=[pltpu.VMEM(c.shape, low) for c in constants]
        + [
            pltpu.VMEM((2 * lines, segs * rows), low),
            pltpu.VMEM((rows, 2 * lines), low),
            pltpu.VMEM((LAGS // LANES, lines, segs * SPANS * extra), low),
            pltpu.VMEM((count, count), low),
        ],
        in_specs=[smem] + [hbm] * len(constants),
        out_specs=[vmem] * (len(constants) + 4),
        scratch_shapes=[pltpu.SemaphoreType.DMA((len(constants),))],
        compiler_params=limit,
        cost_estimate=pl.CostEstimate(flops=0, bytes_accessed=4 * 2**20, transcendentals=0),
    )(pairs, *(pltpu.with_memory_space_constraint(c, pltpu.HBM) for c in constants))
    chosen, partial = pl.pallas_call(
        functools.partial(correlate_kernel, segs, blocks, own),
        out_shape=[pltpu.VMEM((2 * lines, 2 * F), low), pltpu.VMEM((lines, LAGS), jnp.float32)],
        in_specs=[vmem] * (segs * SPANS + 4),
        out_specs=[vmem] * 2,
        compiler_params=limit,
    )(*held, table, lags, take, find)
    mine, other = partial, along("rec", partial, lambda i: (i + 1) % recs)
    for _ in range(2, recs):
        mine, other = mine + other, along("rec", other, lambda i: (i + 1) % recs)
    back = pl.pallas_call(
        functools.partial(adjoint_kernel, blocks, own),
        out_shape=[pltpu.VMEM((rows, span), low)] * SPANS,
        in_specs=[vmem] * 6,
        out_specs=[vmem] * SPANS,
        compiler_params=limit,
    )(chosen, mine, other, table, lags, give)
    back = [back[0]] + [along("fibre", back[k], lambda i: i ^ k) for k in range(1, SPANS)]
    out = pl.pallas_call(
        unpack_kernel,
        out_shape=jax.ShapeDtypeStruct((span, count), low),
        in_specs=[vmem] * (SPANS + 1),
        out_specs=hbm,
        scratch_shapes=[
            pltpu.VMEM((span, count), low),
            pltpu.SemaphoreType.DMA((span // LANES,)),
        ],
        compiler_params=limit,
    )(*back, order)
    return out[None]


def by_band(records, pairs, observed, lag_mask):
    fibres, segs = lax.axis_size("fibre"), lax.axis_size("seg")
    own = BLOCK // fibres
    span, count = records.shape[1:]
    blocks = count // BLOCK
    total_blocks = blocks * segs
    pair_total, pairs_dev = pairs.shape[0], observed.shape[0]
    low = jnp.bfloat16
    band = F // segs
    start = lax.axis_index("seg") * band
    table = lax.dynamic_slice_in_dim(jnp.asarray(forward_table()), start, band, 0)
    lags = lax.dynamic_slice_in_dim(jnp.asarray(lag_table()), start, band, 0)
    f32 = functools.partial(jnp.einsum, preferred_element_type=jnp.float32)
    grid = records.reshape(span, blocks, fibres, own).transpose(2, 0, 1, 3)
    signal = lax.all_to_all(grid, "fibre", 0, 0, tiled=True).reshape(S, blocks, own)
    signal = lax.all_gather(signal, "seg", axis=1, tiled=True)
    spectra = f32("wpt,tbk->wpbk", table, signal).astype(low)
    ids = jnp.arange(total_blocks)
    take = [(pairs[:, side, None] == ids).astype(low) for side in range(2)]
    a0, a1 = (f32("nb,wbk->wnk", take[0], spectra[:, p]) for p in range(2))
    b0, b1 = (f32("nb,wbk->wnk", take[1], spectra[:, p]) for p in range(2))
    cross = jnp.stack([a0 * b0 + a1 * b1, a1 * b0 - a0 * b1], axis=1).astype(low)
    corr = f32("wpnk,wpl->nkl", cross, lags)
    corr = corr.reshape(fibres, segs, pairs_dev, own, LAGS)
    corr = lax.psum_scatter(corr, "seg", scatter_dimension=1)
    synthetic = lax.psum(corr, "rec").reshape(fibres * pairs_dev, own, LAGS)
    seen = observed.reshape(pairs_dev, fibres, own, LAGS).transpose(1, 0, 2, 3)
    seen = lax.all_to_all(seen, "fibre", 0, 0, tiled=True).reshape(fibres * pairs_dev, own, LAGS)
    window = lax.all_gather(lag_mask.astype(jnp.float32), "fibre", axis=0, tiled=True)
    weights = (window[:, None, :] * jnp.tanh(synthetic - seen)).astype(low)
    weights = lax.all_gather(weights.reshape(fibres, pairs_dev, own, LAGS), "seg", axis=1)
    weights = weights.reshape(pair_total, own, LAGS)
    adjoint = f32("nkl,wpl->wpnk", weights, lags).astype(low).astype(jnp.float32)
    g0, g1 = adjoint[:, 0], adjoint[:, 1]

    def added(side, terms):
        high = terms.astype(low)
        rest = (terms - high.astype(jnp.float32)).astype(low)
        return f32("nb,wnk->wbk", take[side], high) + f32("nb,wnk->wbk", take[side], rest)

    grad = jnp.stack(
        [
            added(0, g0 * b0 - g1 * b1) + added(1, g0 * a0 + g1 * a1),
            added(0, g0 * b1 + g1 * b0) + added(1, g0 * a1 - g1 * a0),
        ],
        axis=1,
    ).astype(low)
    sources = f32("wpbk,wpt->tbk", grad, table)
    sources = lax.psum_scatter(sources, "seg", scatter_dimension=1, tiled=True).astype(low)
    sources = sources.reshape(fibres, span, blocks, own)
    sources = lax.all_to_all(sources, "fibre", 0, 0, tiled=True)
    return sources.transpose(1, 2, 0, 3).reshape(1, span, count)


def solution(mesh):
    in_specs = (
        P("rec", "fibre", ("groups", "seg")),
        P(),
        P(("groups", "fibre", "seg"), None, None),
        P(("groups", "fibre", "seg"), None),
    )
    out_specs = P("rec", "fibre", ("groups", "seg"))
    small = mesh.shape["fibre"] == SPANS
    return jax.shard_map(
        by_own_k if small else by_band,
        mesh=mesh,
        in_specs=in_specs,
        out_specs=out_specs,
        check_vma=False,
    )
```

```python
import functools

import jax
import jax.numpy as jnp
import numpy as np
from jax import lax
from jax.experimental import pallas as pl
from jax.experimental.pallas import tpu as pltpu
from jax.sharding import PartitionSpec as P

S = 2048
F = 1024
LAGS = 256
BLOCK = 32
SPANS = 4
MASKED = 16384.0
LANES = 128

_NT = (((1,), (1,)), ((), ()))
_TN = (((0,), (0,)), ((), ()))


def wave_table(freq, shift, scale):
    phase = freq[:, None].astype(np.int64) * shift[None, :] % S
    angles = phase.astype(np.float32) * np.float32(2.0 * np.pi / S)
    factor = np.float32(1.0) / np.sqrt(np.float32(scale))
    parts = [(np.cos(angles) * factor), (-np.sin(angles) * factor)]
    return np.stack(parts, axis=1).astype(jnp.bfloat16)


def forward_table():
    return wave_table(np.arange(F), np.arange(S), S)


def lag_table():
    return wave_table(np.arange(F), (np.arange(LAGS) - LAGS // 2) % S, F)


def dot(a, b, dims=(((1,), (0,)), ((), ()))):
    return lax.dot_general(a, b, dims, preferred_element_type=jnp.float32)


def one_hot(rows, cols, hit):
    row = lax.broadcasted_iota(jnp.int32, (rows, cols), 0)
    col = lax.broadcasted_iota(jnp.int32, (rows, cols), 1)
    return jnp.where(hit(row, col), 1.0, 0.0).astype(jnp.bfloat16)


def channel_of(row, fibre, blocks, own):
    to = row // (blocks * own) ^ fibre
    return row % (blocks * own) // own * BLOCK + to * own + row % own


def channel_order(fibre, blocks, own):
    count = blocks * BLOCK
    return one_hot(count, count, lambda r, c: c == channel_of(r, fibre, blocks, own))


def pack_kernel(blocks, own, records_hbm, observed_hbm, mask_hbm, *refs):
    out_refs, (records, observed, mask, sems) = refs[:SPANS], refs[SPANS:]
    fibre = lax.axis_index("fibre")
    span, count = records.shape
    rows = blocks * own
    tiles = span // LANES
    share = observed.shape[0]
    start = lax.axis_index("rec") * share
    records_copy = pltpu.make_async_copy(records_hbm, records, sems.at[0])
    seen_copy = pltpu.make_async_copy(observed_hbm.at[pl.ds(start, share)], observed, sems.at[1])
    mask_copy = pltpu.make_async_copy(mask_hbm, mask, sems.at[2])
    for copy in (records_copy, seen_copy, mask_copy):
        copy.start()
    order = channel_order(fibre, blocks, own)
    lines = share * BLOCK
    halves = LAGS // LANES
    extra = 2 * halves * share * own
    place = one_hot(
        SPANS * extra,
        2 * halves * lines,
        lambda r, c: (c % BLOCK // own == r // extra ^ fibre)
        & (c % own == r % own)
        & (c // lines == r % (2 * halves * own) // own)
        & (c % lines // BLOCK == r % extra // (2 * halves * own)),
    )
    seen_copy.wait()
    mask_copy.wait()
    window = jnp.concatenate(
        [mask[pl.ds(start + i, 1), :] + jnp.zeros((BLOCK, 1), jnp.int32) for i in range(share)], axis=0
    )
    seen = jnp.where(window != 0, observed[...].reshape(lines, LAGS), MASKED)
    high = seen.astype(jnp.bfloat16)
    low = (seen - high.astype(jnp.float32)).astype(jnp.bfloat16)
    parts = [v[:, h * LANES : (h + 1) * LANES] for v in (high, low) for h in range(halves)]
    packed = dot(place, jnp.concatenate(parts, axis=0)).astype(jnp.bfloat16)
    for k, out_ref in enumerate(out_refs):
        out_ref[tiles * rows :, :] = packed[k * extra : (k + 1) * extra]
    records_copy.wait()
    moved = dot(order, records[...], _NT).astype(jnp.bfloat16)
    for k, out_ref in enumerate(out_refs):
        for q in range(tiles):
            part = moved[k * rows : (k + 1) * rows, q * LANES : (q + 1) * LANES]
            out_ref[q * rows : (q + 1) * rows, :] = part


def prepare_kernel(segs, blocks, own, pairs_dev, share, pairs_hbm, *refs):
    constants = (len(refs) - 6) // 2
    take_ref, give_ref, find_ref, order_ref, pairs_ref, sems = refs[2 * constants :]
    pairs_copy = pltpu.make_async_copy(pairs_hbm, pairs_ref, sems.at[constants])
    copies = [pltpu.make_async_copy(refs[i], refs[constants + i], sems.at[i]) for i in range(constants)]
    for copy in [pairs_copy] + copies:
        copy.start()
    fibre, seg, rec = (lax.axis_index(axis) for axis in ("fibre", "seg", "rec"))
    pair_total = pairs_ref.shape[1]
    rows = blocks * own
    lines = pair_total * own

    def picks(side, line):
        block = jnp.zeros_like(line)
        for n in range(pair_total):
            block = jnp.where(line // own == n, pairs_ref[side, n], block)
        distance = (seg + segs - block // blocks) % segs
        return distance * rows + block % blocks * own + line % own

    halves = LAGS // LANES
    extra = 2 * halves * share * own

    def here(half, line, place):
        part = place % extra
        owner = (place // extra % SPANS ^ fibre) * segs + (seg + segs - place // (extra * SPANS)) % segs
        pair = owner * pairs_dev + rec * share + part // (2 * halves * own)
        return (line // own == pair) & (line % own == part % own) & (part % (halves * own) // own == half)

    for h in range(halves):
        find_ref[h] = one_hot(lines, segs * SPANS * extra, functools.partial(here, h))
    order_ref[...] = channel_order(fibre, blocks, own)
    pairs_copy.wait()
    for side in range(2):
        line = lax.broadcasted_iota(jnp.int32, (lines, segs * rows), 0)
        row = lax.broadcasted_iota(jnp.int32, (lines, segs * rows), 1)
        hit = jnp.where(picks(side, line) == row, 1.0, 0.0).astype(jnp.bfloat16)
        take_ref[side * lines : (side + 1) * lines, :] = hit
        line = lax.broadcasted_iota(jnp.int32, (rows, lines), 1)
        row = lax.broadcasted_iota(jnp.int32, (rows, lines), 0)
        hit = jnp.where(picks(side, line) == row, 1.0, 0.0).astype(jnp.bfloat16)
        give_ref[:, side * lines : (side + 1) * lines] = hit
    for copy in copies:
        copy.wait()


def correlate_kernel(segs, blocks, own, *refs):
    chunks = refs[segs * SPANS - 1 :: -1]
    table_ref, lag_ref, take_ref, find_ref, chosen_ref, partial_ref = refs[segs * SPANS :]
    fibre = lax.axis_index("fibre")
    span = S // SPANS
    band = F // SPANS
    rows = blocks * own
    count = segs * rows
    lines = take_ref.shape[0] // 2
    tiles = span // LANES
    folds = []
    for k in range(SPANS):
        whole = [
            jnp.concatenate([chunks[u * SPANS + k][q * rows : (q + 1) * rows, :] for q in range(tiles)], axis=1)
            for u in range(segs)
        ]
        folds.append(jnp.concatenate(whole, axis=0).astype(jnp.float32))
    flip = fibre % 2 == 1
    turn = jnp.where(flip, -1.0, 1.0)
    late = jnp.where(fibre >= 2, -1.0, 1.0)
    near, far = folds[0] + folds[2], folds[1] + folds[3]
    near_gap, far_gap = folds[0] - folds[2], folds[1] - folds[3]
    e_part = late * jnp.where(flip, far_gap, near_gap)
    d_part = late * jnp.where(flip, near_gap, far_gap)
    both = jnp.concatenate([e_part, d_part], axis=0).astype(jnp.bfloat16)
    reals, imags = [], []
    for j in range(SPANS):
        if j % 2 == 0:
            signal = near + far if j == 0 else turn * (near - far)
            part = dot(signal.astype(jnp.bfloat16), table_ref[j])
            real, imag = part[:, :band], part[:, band:]
        else:
            mixed = dot(both, table_ref[j])
            e_c, e_s = mixed[:count, :band], mixed[:count, band:]
            d_c, d_s = mixed[count:, :band], mixed[count:, band:]
            real, imag = (e_c + d_s, e_s - d_c) if j == 1 else (e_c - d_s, e_s + d_c)
        reals.append(real.astype(jnp.bfloat16))
        imags.append(imag.astype(jnp.bfloat16))
    spectra = jnp.concatenate(reals + imags, axis=1)
    chosen = dot(take_ref[...], spectra)
    chosen_ref[...] = chosen.astype(jnp.bfloat16)
    a0, a1 = chosen[:lines, :F], chosen[:lines, F:]
    b0, b1 = chosen[lines:, :F], chosen[lines:, F:]
    cross_re = (a0 * b0 + a1 * b1).astype(jnp.bfloat16)
    cross_im = (a1 * b0 - a0 * b1).astype(jnp.bfloat16)
    partial = dot(jnp.concatenate([cross_re, cross_im], axis=1), lag_ref[...])
    packed = jnp.concatenate([chunk[tiles * rows :, :] for chunk in chunks], axis=0)
    seen = jnp.concatenate([dot(find_ref[h], packed) for h in range(LAGS // LANES)], axis=1)
    partial_ref[...] = partial - seen


def adjoint_kernel(blocks, own, chosen_ref, mine_ref, other_ref, table_ref, lag_ref, give_ref, *out_refs):
    fibre = lax.axis_index("fibre")
    band = F // SPANS
    lines = mine_ref.shape[0]
    count = blocks * own
    misfit = mine_ref[...] + other_ref[...]
    weights = jnp.where(misfit > -0.5 * MASKED, jnp.tanh(misfit), 0.0).astype(jnp.bfloat16)
    adjoint = dot(weights, lag_ref[...], _NT).astype(jnp.bfloat16).astype(jnp.float32)
    g0, g1 = adjoint[:, :F], adjoint[:, F:]
    a0 = chosen_ref[:lines, :F].astype(jnp.float32)
    a1 = chosen_ref[:lines, F:].astype(jnp.float32)
    b0 = chosen_ref[lines:, :F].astype(jnp.float32)
    b1 = chosen_ref[lines:, F:].astype(jnp.float32)
    low = jnp.bfloat16
    first = jnp.concatenate([(g0 * b0 - g1 * b1).astype(low), (g0 * b1 + g1 * b0).astype(low)], axis=1)
    second = jnp.concatenate([(g0 * a0 + g1 * a1).astype(low), (g0 * a1 - g1 * a0).astype(low)], axis=1)
    grad = dot(give_ref[...], jnp.concatenate([first, second], axis=0)).astype(low)
    even, odd = None, None
    for j in range(SPANS):
        real = grad[:, j * band : (j + 1) * band]
        imag = grad[:, F + j * band : F + (j + 1) * band]
        line = jnp.concatenate([real, imag], axis=1)
        if j % 2 == 0:
            part = dot(line, table_ref[j], _NT)
            even = (part, part) if j == 0 else (even[0] + part, even[1] - part)
        else:
            turned = jnp.concatenate([-imag, real], axis=1)
            part = dot(jnp.concatenate([line, turned], axis=0), table_ref[j], _NT)
            u, v = part[:count], part[count:]
            odd = (u, v) if j == 1 else (odd[0] + u, odd[1] - v)
    flip = fibre % 2 == 1
    late = jnp.where(fibre >= 2, -1.0, 1.0)
    for k, out_ref in enumerate(out_refs):
        other = flip if k % 2 == 0 else ~flip
        base = jnp.where(other, even[1], even[0])
        side = late * jnp.where(other, odd[1], odd[0])
        out_ref[...] = (base + side if k < 2 else base - side).astype(low)


def unpack_kernel(*refs):
    chunks, (order_ref, out_hbm, out, sems) = refs[SPANS - 1 :: -1], refs[SPANS:]
    span = out.shape[0]
    cuts = [pl.ds(q * LANES, LANES) for q in range(span // LANES)]
    leave = [pltpu.make_async_copy(out.at[cut], out_hbm.at[cut], sems.at[q]) for q, cut in enumerate(cuts)]
    for q, copy in enumerate(leave):
        held = jnp.concatenate([chunk[:, q * LANES : (q + 1) * LANES] for chunk in chunks], axis=0)
        out[q * LANES : (q + 1) * LANES, :] = dot(held, order_ref[...], _TN).astype(jnp.bfloat16)
        copy.start()
    for copy in leave:
        copy.wait()


def by_own_k(records, pairs, observed, lag_mask):
    recs, segs, fibres = (lax.axis_size(axis) for axis in ("rec", "seg", "fibre"))
    own = BLOCK // fibres
    span, count = records.shape[1:]
    blocks = count // BLOCK
    rows = blocks * own
    pair_total, pairs_dev = pairs.shape[0], observed.shape[0]
    share = pairs_dev // recs
    lines = pair_total * own
    extra = 2 * LAGS // LANES * share * own
    table = forward_table().reshape(F // SPANS, SPANS, 2, SPANS, span)[:, :, :, 0]
    table = np.ascontiguousarray(table.transpose(1, 3, 2, 0)).reshape(SPANS, span, S // SPANS)
    lags = lag_table().reshape(F // SPANS, SPANS, 2, LAGS)
    lags = np.ascontiguousarray(lags.transpose(2, 1, 0, 3)).reshape(2 * F, LAGS)
    low = jnp.bfloat16
    vmem = pl.BlockSpec(memory_space=pltpu.VMEM)
    hbm = pl.BlockSpec(memory_space=pl.ANY)
    limit = pltpu.CompilerParams(vmem_limit_bytes=16 * 2**20)

    def along(axis, array, target):
        return lax.ppermute(array, axis, [(i, target(i)) for i in range(lax.axis_size(axis))])

    send = pl.pallas_call(
        functools.partial(pack_kernel, blocks, own),
        out_shape=[pltpu.VMEM((span // LANES * rows + extra, LANES), low)] * SPANS,
        in_specs=[hbm] * 3,
        out_specs=[vmem] * SPANS,
        scratch_shapes=[
            pltpu.VMEM((span, count), low),
            pltpu.VMEM((share, BLOCK, LAGS), jnp.float32),
            pltpu.VMEM(lag_mask.shape, jnp.int32),
            pltpu.SemaphoreType.DMA((3,)),
        ],
        compiler_params=limit,
    )(*(pltpu.with_memory_space_constraint(x, pltpu.HBM) for x in (records[0], observed, lag_mask)))
    held = [along("fibre", send[k], lambda i: i ^ k) for k in range(SPANS - 1, 0, -1)]
    held = [send[0]] + held[::-1]
    constants = [jnp.asarray(c) for c in (table, lags)]
    table, lags, take, give, find, order = pl.pallas_call(
        functools.partial(prepare_kernel, segs, blocks, own, pairs_dev, share),
        out_shape=[pltpu.VMEM(c.shape, low) for c in constants]
        + [
            pltpu.VMEM((2 * lines, segs * rows), low),
            pltpu.VMEM((rows, 2 * lines), low),
            pltpu.VMEM((LAGS // LANES, lines, segs * SPANS * extra), low),
            pltpu.VMEM((count, count), low),
        ],
        in_specs=[hbm] * (1 + len(constants)),
        out_specs=[vmem] * (len(constants) + 4),
        scratch_shapes=[pltpu.SMEM(pairs.shape[::-1], jnp.int32), pltpu.SemaphoreType.DMA((1 + len(constants),))],
        compiler_params=limit,
        cost_estimate=pl.CostEstimate(flops=0, bytes_accessed=4 * 2**20, transcendentals=0),
    )(*(pltpu.with_memory_space_constraint(c, pltpu.HBM) for c in [pairs.T] + constants))
    for u in range(1, segs):
        held += [
            along(("fibre", "seg"), send[k], lambda i: (i // segs ^ k) * segs + (i + u) % segs)
            if k in (1,)
            else along("seg", held[k], lambda i: (i + u) % segs)
            for k in range(SPANS - 1, -1, -1)
        ][::-1]
    chosen, partial = pl.pallas_call(
        functools.partial(correlate_kernel, segs, blocks, own),
        out_shape=[pltpu.VMEM((2 * lines, 2 * F), low), pltpu.VMEM((lines, LAGS), jnp.float32)],
        in_specs=[vmem] * (segs * SPANS + 4),
        out_specs=[vmem] * 2,
        compiler_params=limit,
    )(*held[::-1], table, lags, take, find)
    mine, other = partial, along("rec", partial, lambda i: (i + 1) % recs)
    for _ in range(2, recs):
        mine, other = mine + other, along("rec", other, lambda i: (i + 1) % recs)
    back = pl.pallas_call(
        functools.partial(adjoint_kernel, blocks, own),
        out_shape=[pltpu.VMEM((rows, span), low)] * SPANS,
        in_specs=[vmem] * 6,
        out_specs=[vmem] * SPANS,
        compiler_params=limit,
    )(chosen, mine, other, table, lags, give)
    own_part = back[0]
    back = [along("fibre", back[k], lambda i: i ^ k) for k in range(SPANS - 1, 0, -1)][::-1]
    back = [own_part] + back
    out = pl.pallas_call(
        unpack_kernel,
        out_shape=jax.ShapeDtypeStruct((span, count), low),
        in_specs=[vmem] * (SPANS + 1),
        out_specs=hbm,
        scratch_shapes=[
            pltpu.VMEM((span, count), low),
            pltpu.SemaphoreType.DMA((span // LANES,)),
        ],
        compiler_params=limit,
    )(*back[::-1], order)
    return out[None]


def by_band(records, pairs, observed, lag_mask):
    fibres, segs = lax.axis_size("fibre"), lax.axis_size("seg")
    own = BLOCK // fibres
    span, count = records.shape[1:]
    blocks = count // BLOCK
    total_blocks = blocks * segs
    pair_total, pairs_dev = pairs.shape[0], observed.shape[0]
    low = jnp.bfloat16
    band = F // segs
    start = lax.axis_index("seg") * band
    table = lax.dynamic_slice_in_dim(jnp.asarray(forward_table()), start, band, 0)
    lags = lax.dynamic_slice_in_dim(jnp.asarray(lag_table()), start, band, 0)
    f32 = functools.partial(jnp.einsum, preferred_element_type=jnp.float32)
    grid = records.reshape(span, blocks, fibres, own).transpose(2, 0, 1, 3)
    signal = lax.all_to_all(grid, "fibre", 0, 0, tiled=True).reshape(S, blocks, own)
    signal = lax.all_gather(signal, "seg", axis=1, tiled=True)
    spectra = f32("wpt,tbk->wpbk", table, signal).astype(low)
    ids = jnp.arange(total_blocks)
    take = [(pairs[:, side, None] == ids).astype(low) for side in range(2)]
    a0, a1 = (f32("nb,wbk->wnk", take[0], spectra[:, p]) for p in range(2))
    b0, b1 = (f32("nb,wbk->wnk", take[1], spectra[:, p]) for p in range(2))
    cross = jnp.stack([a0 * b0 + a1 * b1, a1 * b0 - a0 * b1], axis=1).astype(low)
    corr = f32("wpnk,wpl->nkl", cross, lags)
    corr = corr.reshape(fibres, segs, pairs_dev, own, LAGS)
    corr = lax.psum_scatter(corr, "seg", scatter_dimension=1)
    synthetic = lax.psum(corr, "rec").reshape(fibres * pairs_dev, own, LAGS)
    seen = observed.reshape(pairs_dev, fibres, own, LAGS).transpose(1, 0, 2, 3)
    seen = lax.all_to_all(seen, "fibre", 0, 0, tiled=True).reshape(fibres * pairs_dev, own, LAGS)
    window = lax.all_gather(lag_mask.astype(jnp.float32), "fibre", axis=0, tiled=True)
    weights = (window[:, None, :] * jnp.tanh(synthetic - seen)).astype(low)
    weights = lax.all_gather(weights.reshape(fibres, pairs_dev, own, LAGS), "seg", axis=1)
    weights = weights.reshape(pair_total, own, LAGS)
    adjoint = f32("nkl,wpl->wpnk", weights, lags).astype(low).astype(jnp.float32)
    g0, g1 = adjoint[:, 0], adjoint[:, 1]

    def added(side, terms):
        high = terms.astype(low)
        rest = (terms - high.astype(jnp.float32)).astype(low)
        return f32("nb,wnk->wbk", take[side], high) + f32("nb,wnk->wbk", take[side], rest)

    grad = jnp.stack(
        [
            added(0, g0 * b0 - g1 * b1) + added(1, g0 * a0 + g1 * a1),
            added(0, g0 * b1 + g1 * b0) + added(1, g0 * a1 - g1 * a0),
        ],
        axis=1,
    ).astype(low)
    sources = f32("wpbk,wpt->tbk", grad, table)
    sources = lax.psum_scatter(sources, "seg", scatter_dimension=1, tiled=True).astype(low)
    sources = sources.reshape(fibres, span, blocks, own)
    sources = lax.all_to_all(sources, "fibre", 0, 0, tiled=True)
    return sources.transpose(1, 2, 0, 3).reshape(1, span, count)


def solution(mesh):
    in_specs = (
        P("rec", "fibre", ("groups", "seg")),
        P(),
        P(("groups", "fibre", "seg"), None, None),
        P(("groups", "fibre", "seg"), None),
    )
    out_specs = P("rec", "fibre", ("groups", "seg"))
    small = mesh.shape["fibre"] == SPANS
    return jax.shard_map(
        by_own_k if small else by_band,
        mesh=mesh,
        in_specs=in_specs,
        out_specs=out_specs,
        check_vma=False,
    )
```

```python
import functools

import jax
import jax.numpy as jnp
import numpy as np
from jax import lax
from jax.experimental import pallas as pl
from jax.experimental.pallas import tpu as pltpu
from jax.sharding import PartitionSpec as P

S = 2048
F = 1024
LAGS = 256
BLOCK = 32
SPANS = 4
MASKED = 16384.0
LANES = 128

_NT = (((1,), (1,)), ((), ()))
_TN = (((0,), (0,)), ((), ()))


def wave_table(freq, shift, scale):
    phase = freq[:, None].astype(np.int64) * shift[None, :] % S
    angles = phase.astype(np.float32) * np.float32(2.0 * np.pi / S)
    factor = np.float32(1.0) / np.sqrt(np.float32(scale))
    parts = [(np.cos(angles) * factor), (-np.sin(angles) * factor)]
    return np.stack(parts, axis=1).astype(jnp.bfloat16)


def forward_table():
    return wave_table(np.arange(F), np.arange(S), S)


def lag_table():
    return wave_table(np.arange(F), (np.arange(LAGS) - LAGS // 2) % S, F)


def dot(a, b, dims=(((1,), (0,)), ((), ()))):
    return lax.dot_general(a, b, dims, preferred_element_type=jnp.float32)


def one_hot(rows, cols, hit):
    row = lax.broadcasted_iota(jnp.int32, (rows, cols), 0)
    col = lax.broadcasted_iota(jnp.int32, (rows, cols), 1)
    return jnp.where(hit(row, col), 1.0, 0.0).astype(jnp.bfloat16)


def channel_of(row, fibre, blocks, own):
    to = row // (blocks * own) ^ fibre
    return row % (blocks * own) // own * BLOCK + to * own + row % own


def channel_order(fibre, blocks, own):
    count = blocks * BLOCK
    return one_hot(count, count, lambda r, c: c == channel_of(r, fibre, blocks, own))


def pack_kernel(blocks, own, records_hbm, observed_hbm, mask_hbm, *refs):
    out_refs, (records, observed, mask, sems) = refs[:SPANS], refs[SPANS:]
    fibre = lax.axis_index("fibre")
    span, count = records.shape
    rows = blocks * own
    tiles = span // LANES
    share = observed.shape[0]
    start = lax.axis_index("rec") * share
    records_copy = pltpu.make_async_copy(records_hbm, records, sems.at[0])
    seen_copy = pltpu.make_async_copy(observed_hbm.at[pl.ds(start, share)], observed, sems.at[1])
    mask_copy = pltpu.make_async_copy(mask_hbm, mask, sems.at[2])
    for copy in (records_copy, seen_copy, mask_copy):
        copy.start()
    order = channel_order(fibre, blocks, own)
    lines = share * BLOCK
    halves = LAGS // LANES
    extra = 2 * halves * share * own
    place = one_hot(
        SPANS * extra,
        2 * halves * lines,
        lambda r, c: (c % BLOCK // own == r // extra ^ fibre)
        & (c % own == r % own)
        & (c // lines == r % (2 * halves * own) // own)
        & (c % lines // BLOCK == r % extra // (2 * halves * own)),
    )
    seen_copy.wait()
    mask_copy.wait()
    window = jnp.concatenate(
        [mask[pl.ds(start + i, 1), :] + jnp.zeros((BLOCK, 1), jnp.int32) for i in range(share)], axis=0
    )
    seen = jnp.where(window != 0, observed[...].reshape(lines, LAGS), MASKED)
    high = seen.astype(jnp.bfloat16)
    low = (seen - high.astype(jnp.float32)).astype(jnp.bfloat16)
    parts = [v[:, h * LANES : (h + 1) * LANES] for v in (high, low) for h in range(halves)]
    packed = dot(place, jnp.concatenate(parts, axis=0)).astype(jnp.bfloat16)
    for k, out_ref in enumerate(out_refs):
        out_ref[tiles * rows :, :] = packed[k * extra : (k + 1) * extra]
    records_copy.wait()
    moved = dot(order, records[...], _NT).astype(jnp.bfloat16)
    for k, out_ref in enumerate(out_refs):
        for q in range(tiles):
            part = moved[k * rows : (k + 1) * rows, q * LANES : (q + 1) * LANES]
            out_ref[q * rows : (q + 1) * rows, :] = part


def prepare_kernel(segs, blocks, own, pairs_dev, share, pairs_hbm, *refs):
    constants = (len(refs) - 6) // 2
    take_ref, give_ref, find_ref, order_ref, pairs_ref, sems = refs[2 * constants :]
    pairs_copy = pltpu.make_async_copy(pairs_hbm, pairs_ref, sems.at[constants])
    copies = [pltpu.make_async_copy(refs[i], refs[constants + i], sems.at[i]) for i in range(constants)]
    for copy in [pairs_copy] + copies:
        copy.start()
    fibre, seg, rec = (lax.axis_index(axis) for axis in ("fibre", "seg", "rec"))
    pair_total = pairs_ref.shape[1]
    rows = blocks * own
    lines = pair_total * own

    def picks(side, line):
        block = jnp.zeros_like(line)
        for n in range(pair_total):
            block = jnp.where(line // own == n, pairs_ref[side, n], block)
        distance = (seg + segs - block // blocks) % segs
        return distance * rows + block % blocks * own + line % own

    halves = LAGS // LANES
    extra = 2 * halves * share * own

    def here(half, line, place):
        part = place % extra
        owner = (place // extra % SPANS ^ fibre) * segs + (seg + segs - place // (extra * SPANS)) % segs
        pair = owner * pairs_dev + rec * share + part // (2 * halves * own)
        return (line // own == pair) & (line % own == part % own) & (part % (halves * own) // own == half)

    for h in range(halves):
        find_ref[h] = one_hot(lines, segs * SPANS * extra, functools.partial(here, h))
    order_ref[...] = channel_order(fibre, blocks, own)
    pairs_copy.wait()
    for side in range(2):
        line = lax.broadcasted_iota(jnp.int32, (lines, segs * rows), 0)
        row = lax.broadcasted_iota(jnp.int32, (lines, segs * rows), 1)
        hit = jnp.where(picks(side, line) == row, 1.0, 0.0).astype(jnp.bfloat16)
        take_ref[side * lines : (side + 1) * lines, :] = hit
        line = lax.broadcasted_iota(jnp.int32, (rows, lines), 1)
        row = lax.broadcasted_iota(jnp.int32, (rows, lines), 0)
        hit = jnp.where(picks(side, line) == row, 1.0, 0.0).astype(jnp.bfloat16)
        give_ref[:, side * lines : (side + 1) * lines] = hit
    for copy in copies:
        copy.wait()


def correlate_kernel(segs, blocks, own, *refs):
    chunks = [refs[i] for i in [7, 2, 6, 5, 3, 4, 1, 0]]
    table_ref, lag_ref, take_ref, find_ref, chosen_ref, partial_ref = refs[segs * SPANS :]
    fibre = lax.axis_index("fibre")
    span = S // SPANS
    band = F // SPANS
    rows = blocks * own
    count = segs * rows
    lines = take_ref.shape[0] // 2
    tiles = span // LANES
    folds = []
    for k in range(SPANS):
        whole = [
            jnp.concatenate([chunks[u * SPANS + k][q * rows : (q + 1) * rows, :] for q in range(tiles)], axis=1)
            for u in range(segs)
        ]
        folds.append(jnp.concatenate(whole, axis=0).astype(jnp.float32))
    flip = fibre % 2 == 1
    turn = jnp.where(flip, -1.0, 1.0)
    late = jnp.where(fibre >= 2, -1.0, 1.0)
    near, far = folds[0] + folds[2], folds[1] + folds[3]
    near_gap, far_gap = folds[0] - folds[2], folds[1] - folds[3]
    e_part = late * jnp.where(flip, far_gap, near_gap)
    d_part = late * jnp.where(flip, near_gap, far_gap)
    both = jnp.concatenate([e_part, d_part], axis=0).astype(jnp.bfloat16)
    reals, imags = [], []
    for j in range(SPANS):
        if j % 2 == 0:
            signal = near + far if j == 0 else turn * (near - far)
            part = dot(signal.astype(jnp.bfloat16), table_ref[j])
            real, imag = part[:, :band], part[:, band:]
        else:
            mixed = dot(both, table_ref[j])
            e_c, e_s = mixed[:count, :band], mixed[:count, band:]
            d_c, d_s = mixed[count:, :band], mixed[count:, band:]
            real, imag = (e_c + d_s, e_s - d_c) if j == 1 else (e_c - d_s, e_s + d_c)
        reals.append(real.astype(jnp.bfloat16))
        imags.append(imag.astype(jnp.bfloat16))
    spectra = jnp.concatenate(reals + imags, axis=1)
    chosen = dot(take_ref[...], spectra)
    chosen_ref[...] = chosen.astype(jnp.bfloat16)
    a0, a1 = chosen[:lines, :F], chosen[:lines, F:]
    b0, b1 = chosen[lines:, :F], chosen[lines:, F:]
    cross_re = (a0 * b0 + a1 * b1).astype(jnp.bfloat16)
    cross_im = (a1 * b0 - a0 * b1).astype(jnp.bfloat16)
    partial = dot(jnp.concatenate([cross_re, cross_im], axis=1), lag_ref[...])
    packed = jnp.concatenate([chunk[tiles * rows :, :] for chunk in chunks], axis=0)
    seen = jnp.concatenate([dot(find_ref[h], packed) for h in range(LAGS // LANES)], axis=1)
    partial_ref[...] = partial - seen


def adjoint_kernel(blocks, own, chosen_ref, mine_ref, other_ref, back_ref, lag_ref, give_ref, *out_refs):
    fibre = lax.axis_index("fibre")
    band = F // SPANS
    lines = mine_ref.shape[0]
    count = blocks * own
    misfit = mine_ref[...] + other_ref[...]
    weights = jnp.where(misfit > -0.5 * MASKED, jnp.tanh(misfit), 0.0).astype(jnp.bfloat16)
    adjoint = dot(weights, lag_ref[...], _NT).astype(jnp.bfloat16).astype(jnp.float32)
    g0, g1 = adjoint[:, :F], adjoint[:, F:]
    a0 = chosen_ref[:lines, :F].astype(jnp.float32)
    a1 = chosen_ref[:lines, F:].astype(jnp.float32)
    b0 = chosen_ref[lines:, :F].astype(jnp.float32)
    b1 = chosen_ref[lines:, F:].astype(jnp.float32)
    low = jnp.bfloat16
    first = jnp.concatenate([(g0 * b0 - g1 * b1).astype(low), (g0 * b1 + g1 * b0).astype(low)], axis=1)
    second = jnp.concatenate([(g0 * a0 + g1 * a1).astype(low), (g0 * a1 - g1 * a0).astype(low)], axis=1)
    grad = dot(give_ref[...], jnp.concatenate([first, second], axis=0)).astype(low)
    even, odd = None, None
    for j in range(SPANS):
        real = grad[:, j * band : (j + 1) * band]
        imag = grad[:, F + j * band : F + (j + 1) * band]
        line = jnp.concatenate([real, imag], axis=1)
        if j % 2 == 0:
            part = dot(line, back_ref[j])
            even = (part, part) if j == 0 else (even[0] + part, even[1] - part)
        else:
            turned = jnp.concatenate([-imag, real], axis=1)
            part = dot(jnp.concatenate([line, turned], axis=0), back_ref[j])
            u, v = part[:count], part[count:]
            odd = (u, v) if j == 1 else (odd[0] + u, odd[1] - v)
    flip = fibre % 2 == 1
    late = jnp.where(fibre >= 2, -1.0, 1.0)
    for k, out_ref in enumerate(out_refs):
        other = flip if k % 2 == 0 else ~flip
        base = jnp.where(other, even[1], even[0])
        side = late * jnp.where(other, odd[1], odd[0])
        out_ref[...] = (base + side if k < 2 else base - side).astype(low)


def unpack_kernel(*refs):
    chunks = [refs[i] for i in [3, 1, 2, 0]]
    order_ref, out_hbm, out, sems = refs[SPANS:]
    span = out.shape[0]
    cuts = [pl.ds(q * LANES, LANES) for q in range(span // LANES)]
    leave = [pltpu.make_async_copy(out.at[cut], out_hbm.at[cut], sems.at[q]) for q, cut in enumerate(cuts)]
    for q, copy in enumerate(leave):
        held = jnp.concatenate([chunk[:, q * LANES : (q + 1) * LANES] for chunk in chunks], axis=0)
        out[q * LANES : (q + 1) * LANES, :] = dot(held, order_ref[...], _TN).astype(jnp.bfloat16)
        copy.start()
    for copy in leave:
        copy.wait()


def by_own_k(records, pairs, observed, lag_mask):
    recs, segs, fibres = (lax.axis_size(axis) for axis in ("rec", "seg", "fibre"))
    own = BLOCK // fibres
    span, count = records.shape[1:]
    blocks = count // BLOCK
    rows = blocks * own
    pair_total, pairs_dev = pairs.shape[0], observed.shape[0]
    share = pairs_dev // recs
    lines = pair_total * own
    extra = 2 * LAGS // LANES * share * own
    table = forward_table().reshape(F // SPANS, SPANS, 2, SPANS, span)[:, :, :, 0]
    table = np.ascontiguousarray(table.transpose(1, 3, 2, 0)).reshape(SPANS, span, S // SPANS)
    lags = lag_table().reshape(F // SPANS, SPANS, 2, LAGS)
    lags = np.ascontiguousarray(lags.transpose(2, 1, 0, 3)).reshape(2 * F, LAGS)
    low = jnp.bfloat16
    vmem = pl.BlockSpec(memory_space=pltpu.VMEM)
    hbm = pl.BlockSpec(memory_space=pl.ANY)
    limit = pltpu.CompilerParams(vmem_limit_bytes=16 * 2**20)

    def along(axis, array, target):
        return lax.ppermute(array, axis, [(i, target(i)) for i in range(lax.axis_size(axis))])

    send = pl.pallas_call(
        functools.partial(pack_kernel, blocks, own),
        out_shape=[pltpu.VMEM((span // LANES * rows + extra, LANES), low)] * SPANS,
        in_specs=[hbm] * 3,
        out_specs=[vmem] * SPANS,
        scratch_shapes=[
            pltpu.VMEM((span, count), low),
            pltpu.VMEM((share, BLOCK, LAGS), jnp.float32),
            pltpu.VMEM(lag_mask.shape, jnp.int32),
            pltpu.SemaphoreType.DMA((3,)),
        ],
        compiler_params=limit,
    )(*(pltpu.with_memory_space_constraint(x, pltpu.HBM) for x in (records[0], observed, lag_mask)))
    held = [along("fibre", send[k], lambda i: i ^ k) for k in range(SPANS - 1, 0, -1)]
    held = [send[0]] + held[::-1]
    constants = [jnp.asarray(c) for c in (table, np.ascontiguousarray(table.transpose(0, 2, 1)), lags)]
    table, table_back, lags, take, give, find, order = pl.pallas_call(
        functools.partial(prepare_kernel, segs, blocks, own, pairs_dev, share),
        out_shape=[pltpu.VMEM(c.shape, low) for c in constants]
        + [
            pltpu.VMEM((2 * lines, segs * rows), low),
            pltpu.VMEM((rows, 2 * lines), low),
            pltpu.VMEM((LAGS // LANES, lines, segs * SPANS * extra), low),
            pltpu.VMEM((count, count), low),
        ],
        in_specs=[hbm] * (1 + len(constants)),
        out_specs=[vmem] * (len(constants) + 4),
        scratch_shapes=[pltpu.SMEM(pairs.shape[::-1], jnp.int32), pltpu.SemaphoreType.DMA((1 + len(constants),))],
        compiler_params=limit,
        cost_estimate=pl.CostEstimate(flops=0, bytes_accessed=4 * 2**20, transcendentals=0),
    )(*(pltpu.with_memory_space_constraint(c, pltpu.HBM) for c in [pairs.T] + constants))
    for u in range(1, segs):
        held += [
            along(("fibre", "seg"), send[k], lambda i: (i // segs ^ k) * segs + (i + u) % segs)
            if k in (1,)
            else along("seg", held[k], lambda i: (i + u) % segs)
            for k in range(SPANS - 1, -1, -1)
        ][::-1]
    chosen, partial = pl.pallas_call(
        functools.partial(correlate_kernel, segs, blocks, own),
        out_shape=[pltpu.VMEM((2 * lines, 2 * F), low), pltpu.VMEM((lines, LAGS), jnp.float32)],
        in_specs=[vmem] * (segs * SPANS + 4),
        out_specs=[vmem] * 2,
        compiler_params=limit,
    )(*[held[i] for i in (7, 6, 1, 4, 5, 3, 2, 0)], table, lags, take, find)
    mine, other = partial, along("rec", partial, lambda i: (i + 1) % recs)
    for _ in range(2, recs):
        mine, other = mine + other, along("rec", other, lambda i: (i + 1) % recs)
    back = pl.pallas_call(
        functools.partial(adjoint_kernel, blocks, own),
        out_shape=[pltpu.VMEM((rows, span), low)] * SPANS,
        in_specs=[vmem] * 6,
        out_specs=[vmem] * SPANS,
        compiler_params=limit,
    )(chosen, mine, other, table_back, lags, give)
    own_part = back[0]
    sent = {k: along("fibre", back[k], lambda i: i ^ k) for k in (3, 1, 2)}
    out = pl.pallas_call(
        unpack_kernel,
        out_shape=jax.ShapeDtypeStruct((span, count), low),
        in_specs=[vmem] * (SPANS + 1),
        out_specs=hbm,
        scratch_shapes=[
            pltpu.VMEM((span, count), low),
            pltpu.SemaphoreType.DMA((span // LANES,)),
        ],
        compiler_params=limit,
    )(*sent.values(), own_part, order)
    return out[None]


def by_band(records, pairs, observed, lag_mask):
    fibres, segs = lax.axis_size("fibre"), lax.axis_size("seg")
    own = BLOCK // fibres
    span, count = records.shape[1:]
    blocks = count // BLOCK
    total_blocks = blocks * segs
    pair_total, pairs_dev = pairs.shape[0], observed.shape[0]
    low = jnp.bfloat16
    band = F // segs
    start = lax.axis_index("seg") * band
    table = lax.dynamic_slice_in_dim(jnp.asarray(forward_table()), start, band, 0)
    lags = lax.dynamic_slice_in_dim(jnp.asarray(lag_table()), start, band, 0)
    f32 = functools.partial(jnp.einsum, preferred_element_type=jnp.float32)
    grid = records.reshape(span, blocks, fibres, own).transpose(2, 0, 1, 3)
    signal = lax.all_to_all(grid, "fibre", 0, 0, tiled=True).reshape(S, blocks, own)
    signal = lax.all_gather(signal, "seg", axis=1, tiled=True)
    spectra = f32("wpt,tbk->wpbk", table, signal).astype(low)
    ids = jnp.arange(total_blocks)
    take = [(pairs[:, side, None] == ids).astype(low) for side in range(2)]
    a0, a1 = (f32("nb,wbk->wnk", take[0], spectra[:, p]) for p in range(2))
    b0, b1 = (f32("nb,wbk->wnk", take[1], spectra[:, p]) for p in range(2))
    cross = jnp.stack([a0 * b0 + a1 * b1, a1 * b0 - a0 * b1], axis=1).astype(low)
    corr = f32("wpnk,wpl->nkl", cross, lags)
    corr = corr.reshape(fibres, segs, pairs_dev, own, LAGS)
    corr = lax.psum_scatter(corr, "seg", scatter_dimension=1)
    synthetic = lax.psum(corr, "rec").reshape(fibres * pairs_dev, own, LAGS)
    seen = observed.reshape(pairs_dev, fibres, own, LAGS).transpose(1, 0, 2, 3)
    seen = lax.all_to_all(seen, "fibre", 0, 0, tiled=True).reshape(fibres * pairs_dev, own, LAGS)
    window = lax.all_gather(lag_mask.astype(jnp.float32), "fibre", axis=0, tiled=True)
    weights = (window[:, None, :] * jnp.tanh(synthetic - seen)).astype(low)
    weights = lax.all_gather(weights.reshape(fibres, pairs_dev, own, LAGS), "seg", axis=1)
    weights = weights.reshape(pair_total, own, LAGS)
    adjoint = f32("nkl,wpl->wpnk", weights, lags).astype(low).astype(jnp.float32)
    g0, g1 = adjoint[:, 0], adjoint[:, 1]

    def added(side, terms):
        high = terms.astype(low)
        rest = (terms - high.astype(jnp.float32)).astype(low)
        return f32("nb,wnk->wbk", take[side], high) + f32("nb,wnk->wbk", take[side], rest)

    grad = jnp.stack(
        [
            added(0, g0 * b0 - g1 * b1) + added(1, g0 * a0 + g1 * a1),
            added(0, g0 * b1 + g1 * b0) + added(1, g0 * a1 - g1 * a0),
        ],
        axis=1,
    ).astype(low)
    sources = f32("wpbk,wpt->tbk", grad, table)
    sources = lax.psum_scatter(sources, "seg", scatter_dimension=1, tiled=True).astype(low)
    sources = sources.reshape(fibres, span, blocks, own)
    sources = lax.all_to_all(sources, "fibre", 0, 0, tiled=True)
    return sources.transpose(1, 2, 0, 3).reshape(1, span, count)


def solution(mesh):
    in_specs = (
        P("rec", "fibre", ("groups", "seg")),
        P(),
        P(("groups", "fibre", "seg"), None, None),
        P(("groups", "fibre", "seg"), None),
    )
    out_specs = P("rec", "fibre", ("groups", "seg"))
    small = mesh.shape["fibre"] == SPANS
    return jax.shard_map(
        by_own_k if small else by_band,
        mesh=mesh,
        in_specs=in_specs,
        out_specs=out_specs,
        check_vma=False,
    )
```

```python
import functools

import jax
import jax.numpy as jnp
import numpy as np
from jax import lax
from jax.experimental import pallas as pl
from jax.experimental.pallas import tpu as pltpu
from jax.sharding import PartitionSpec as P

S = 2048
F = 1024
LAGS = 256
BLOCK = 32
SPANS = 4
MASKED = 16384.0
LANES = 128

_NT = (((1,), (1,)), ((), ()))
_TN = (((0,), (0,)), ((), ()))


def wave_table(freq, shift, scale):
    phase = freq[:, None].astype(np.int64) * shift[None, :] % S
    angles = phase.astype(np.float32) * np.float32(2.0 * np.pi / S)
    factor = np.float32(1.0) / np.sqrt(np.float32(scale))
    parts = [(np.cos(angles) * factor), (-np.sin(angles) * factor)]
    return np.stack(parts, axis=1).astype(jnp.bfloat16)


def forward_table():
    return wave_table(np.arange(F), np.arange(S), S)


def lag_table():
    return wave_table(np.arange(F), (np.arange(LAGS) - LAGS // 2) % S, F)


def dot(a, b, dims=(((1,), (0,)), ((), ()))):
    return lax.dot_general(a, b, dims, preferred_element_type=jnp.float32)


def one_hot(rows, cols, hit):
    row = lax.broadcasted_iota(jnp.int32, (rows, cols), 0)
    col = lax.broadcasted_iota(jnp.int32, (rows, cols), 1)
    return jnp.where(hit(row, col), 1.0, 0.0).astype(jnp.bfloat16)


def channel_of(row, fibre, blocks, own):
    to = row // (blocks * own) ^ fibre
    return row % (blocks * own) // own * BLOCK + to * own + row % own


def channel_order(fibre, blocks, own):
    count = blocks * BLOCK
    return one_hot(count, count, lambda r, c: c == channel_of(r, fibre, blocks, own))


def pack_kernel(blocks, own, records_hbm, observed_hbm, mask_hbm, *refs):
    out_refs, (records, observed, mask, sems) = refs[:SPANS], refs[SPANS:]
    fibre = lax.axis_index("fibre")
    span, count = records.shape
    rows = blocks * own
    tiles = span // LANES
    share = observed.shape[0]
    start = lax.axis_index("rec") * share
    records_copy = pltpu.make_async_copy(records_hbm, records, sems.at[0])
    seen_copy = pltpu.make_async_copy(observed_hbm.at[pl.ds(start, share)], observed, sems.at[1])
    mask_copy = pltpu.make_async_copy(mask_hbm, mask, sems.at[2])
    for copy in (records_copy, seen_copy, mask_copy):
        copy.start()
    order = channel_order(fibre, blocks, own)
    lines = share * BLOCK
    halves = LAGS // LANES
    extra = halves * share * own
    place = one_hot(
        SPANS * extra,
        halves * lines,
        lambda r, c: (c % BLOCK // own == r // extra ^ fibre)
        & (c % own == r % own)
        & (c // lines == r % (halves * own) // own)
        & (c % lines // BLOCK == r % extra // (halves * own)),
    )
    seen_copy.wait()
    mask_copy.wait()
    window = jnp.concatenate(
        [mask[pl.ds(start + i, 1), :] + jnp.zeros((BLOCK, 1), jnp.int32) for i in range(share)], axis=0
    )
    seen = jnp.where(window != 0, observed[...].reshape(lines, LAGS), MASKED)
    seen = seen.astype(jnp.bfloat16)
    parts = [seen[:, h * LANES : (h + 1) * LANES] for h in range(halves)]
    packed = dot(place, jnp.concatenate(parts, axis=0)).astype(jnp.bfloat16)
    for k, out_ref in enumerate(out_refs):
        out_ref[tiles * rows :, :] = packed[k * extra : (k + 1) * extra]
    records_copy.wait()
    moved = dot(order, records[...], _NT).astype(jnp.bfloat16)
    for k, out_ref in enumerate(out_refs):
        for q in range(tiles):
            part = moved[k * rows : (k + 1) * rows, q * LANES : (q + 1) * LANES]
            out_ref[q * rows : (q + 1) * rows, :] = part


def prepare_kernel(segs, blocks, own, pairs_dev, share, pairs_hbm, *refs):
    constants = (len(refs) - 6) // 2
    take_ref, give_ref, find_ref, order_ref, pairs_ref, sems = refs[2 * constants :]
    pairs_copy = pltpu.make_async_copy(pairs_hbm, pairs_ref, sems.at[constants])
    copies = [pltpu.make_async_copy(refs[i], refs[constants + i], sems.at[i]) for i in range(constants)]
    for copy in [pairs_copy] + copies:
        copy.start()
    fibre, seg, rec = (lax.axis_index(axis) for axis in ("fibre", "seg", "rec"))
    pair_total = pairs_ref.shape[1]
    rows = blocks * own
    lines = pair_total * own

    def picks(side, line):
        block = jnp.zeros_like(line)
        for n in range(pair_total):
            block = jnp.where(line // own == n, pairs_ref[side, n], block)
        distance = (seg + segs - block // blocks) % segs
        return distance * rows + block % blocks * own + line % own

    halves = LAGS // LANES
    extra = halves * share * own

    def here(half, line, place):
        part = place % extra
        owner = (place // extra % SPANS ^ fibre) * segs + (seg + segs - place // (extra * SPANS)) % segs
        pair = owner * pairs_dev + rec * share + part // (halves * own)
        return (line // own == pair) & (line % own == part % own) & (part % (halves * own) // own == half)

    for h in range(halves):
        find_ref[h] = one_hot(lines, segs * SPANS * extra, functools.partial(here, h))
    order_ref[...] = channel_order(fibre, blocks, own)
    pairs_copy.wait()
    for side in range(2):
        line = lax.broadcasted_iota(jnp.int32, (lines, segs * rows), 0)
        row = lax.broadcasted_iota(jnp.int32, (lines, segs * rows), 1)
        hit = jnp.where(picks(side, line) == row, 1.0, 0.0).astype(jnp.bfloat16)
        take_ref[side * lines : (side + 1) * lines, :] = hit
        line = lax.broadcasted_iota(jnp.int32, (rows, lines), 1)
        row = lax.broadcasted_iota(jnp.int32, (rows, lines), 0)
        hit = jnp.where(picks(side, line) == row, 1.0, 0.0).astype(jnp.bfloat16)
        give_ref[:, side * lines : (side + 1) * lines] = hit
    for copy in copies:
        copy.wait()


def correlate_kernel(segs, blocks, own, *refs):
    chunks = [refs[i] for i in [7, 2, 6, 5, 3, 4, 1, 0]]
    table_ref, lag_ref, take_ref, find_ref, chosen_ref, partial_ref = refs[segs * SPANS :]
    fibre = lax.axis_index("fibre")
    span = S // SPANS
    band = F // SPANS
    rows = blocks * own
    count = segs * rows
    lines = take_ref.shape[0] // 2
    tiles = span // LANES
    folds = []
    for k in range(SPANS):
        whole = [
            jnp.concatenate([chunks[u * SPANS + k][q * rows : (q + 1) * rows, :] for q in range(tiles)], axis=1)
            for u in range(segs)
        ]
        folds.append(jnp.concatenate(whole, axis=0).astype(jnp.float32))
    flip = fibre % 2 == 1
    turn = jnp.where(flip, -1.0, 1.0)
    late = jnp.where(fibre >= 2, -1.0, 1.0)
    near, far = folds[0] + folds[2], folds[1] + folds[3]
    near_gap, far_gap = folds[0] - folds[2], folds[1] - folds[3]
    e_part = late * jnp.where(flip, far_gap, near_gap)
    d_part = late * jnp.where(flip, near_gap, far_gap)
    both = jnp.concatenate([e_part, d_part], axis=0).astype(jnp.bfloat16)
    reals, imags = [], []
    for j in range(SPANS):
        if j % 2 == 0:
            signal = near + far if j == 0 else turn * (near - far)
            part = dot(signal.astype(jnp.bfloat16), table_ref[j])
            real, imag = part[:, :band], part[:, band:]
        else:
            mixed = dot(both, table_ref[j])
            e_c, e_s = mixed[:count, :band], mixed[:count, band:]
            d_c, d_s = mixed[count:, :band], mixed[count:, band:]
            real, imag = (e_c + d_s, e_s - d_c) if j == 1 else (e_c - d_s, e_s + d_c)
        reals.append(real.astype(jnp.bfloat16))
        imags.append(imag.astype(jnp.bfloat16))
    spectra = jnp.concatenate(reals + imags, axis=1)
    chosen = dot(take_ref[...], spectra)
    chosen_ref[...] = chosen.astype(jnp.bfloat16)
    a0, a1 = chosen[:lines, :F], chosen[:lines, F:]
    b0, b1 = chosen[lines:, :F], chosen[lines:, F:]
    cross_re = (a0 * b0 + a1 * b1).astype(jnp.bfloat16)
    cross_im = (a1 * b0 - a0 * b1).astype(jnp.bfloat16)
    partial = dot(jnp.concatenate([cross_re, cross_im], axis=1), lag_ref[...])
    packed = jnp.concatenate([chunk[tiles * rows :, :] for chunk in chunks], axis=0)
    seen = jnp.concatenate([dot(find_ref[h], packed) for h in range(LAGS // LANES)], axis=1)
    partial_ref[...] = partial - seen


def adjoint_kernel(blocks, own, chosen_ref, mine_ref, other_ref, back_ref, lag_ref, give_ref, *out_refs):
    fibre = lax.axis_index("fibre")
    band = F // SPANS
    lines = mine_ref.shape[0]
    count = blocks * own
    misfit = mine_ref[...] + other_ref[...]
    weights = jnp.where(misfit > -0.5 * MASKED, jnp.tanh(misfit), 0.0).astype(jnp.bfloat16)
    adjoint = dot(weights, lag_ref[...], _NT).astype(jnp.bfloat16).astype(jnp.float32)
    g0, g1 = adjoint[:, :F], adjoint[:, F:]
    a0 = chosen_ref[:lines, :F].astype(jnp.float32)
    a1 = chosen_ref[:lines, F:].astype(jnp.float32)
    b0 = chosen_ref[lines:, :F].astype(jnp.float32)
    b1 = chosen_ref[lines:, F:].astype(jnp.float32)
    low = jnp.bfloat16
    first = jnp.concatenate([(g0 * b0 - g1 * b1).astype(low), (g0 * b1 + g1 * b0).astype(low)], axis=1)
    second = jnp.concatenate([(g0 * a0 + g1 * a1).astype(low), (g0 * a1 - g1 * a0).astype(low)], axis=1)
    grad = dot(give_ref[...], jnp.concatenate([first, second], axis=0)).astype(low)
    even, odd = None, None
    for j in range(SPANS):
        real = grad[:, j * band : (j + 1) * band]
        imag = grad[:, F + j * band : F + (j + 1) * band]
        line = jnp.concatenate([real, imag], axis=1)
        if j % 2 == 0:
            part = dot(line, back_ref[j])
            even = (part, part) if j == 0 else (even[0] + part, even[1] - part)
        else:
            turned = jnp.concatenate([-imag, real], axis=1)
            part = dot(jnp.concatenate([line, turned], axis=0), back_ref[j])
            u, v = part[:count], part[count:]
            odd = (u, v) if j == 1 else (odd[0] + u, odd[1] - v)
    flip = fibre % 2 == 1
    late = jnp.where(fibre >= 2, -1.0, 1.0)
    for k, out_ref in enumerate(out_refs):
        other = flip if k % 2 == 0 else ~flip
        base = jnp.where(other, even[1], even[0])
        side = late * jnp.where(other, odd[1], odd[0])
        out_ref[...] = (base + side if k < 2 else base - side).astype(low)


def unpack_kernel(*refs):
    chunks = [refs[i] for i in [3, 1, 2, 0]]
    order_ref, out_hbm, out, sems = refs[SPANS:]
    span = out.shape[0]
    cuts = [pl.ds(q * LANES, LANES) for q in range(span // LANES)]
    leave = [pltpu.make_async_copy(out.at[cut], out_hbm.at[cut], sems.at[q]) for q, cut in enumerate(cuts)]
    for q, copy in enumerate(leave):
        held = jnp.concatenate([chunk[:, q * LANES : (q + 1) * LANES] for chunk in chunks], axis=0)
        out[q * LANES : (q + 1) * LANES, :] = dot(held, order_ref[...], _TN).astype(jnp.bfloat16)
        copy.start()
    for copy in leave:
        copy.wait()


def by_own_k(records, pairs, observed, lag_mask):
    recs, segs, fibres = (lax.axis_size(axis) for axis in ("rec", "seg", "fibre"))
    own = BLOCK // fibres
    span, count = records.shape[1:]
    blocks = count // BLOCK
    rows = blocks * own
    pair_total, pairs_dev = pairs.shape[0], observed.shape[0]
    share = pairs_dev // recs
    lines = pair_total * own
    extra = LAGS // LANES * share * own
    table = forward_table().reshape(F // SPANS, SPANS, 2, SPANS, span)[:, :, :, 0]
    table = np.ascontiguousarray(table.transpose(1, 3, 2, 0)).reshape(SPANS, span, S // SPANS)
    lags = lag_table().reshape(F // SPANS, SPANS, 2, LAGS)
    lags = np.ascontiguousarray(lags.transpose(2, 1, 0, 3)).reshape(2 * F, LAGS)
    low = jnp.bfloat16
    vmem = pl.BlockSpec(memory_space=pltpu.VMEM)
    hbm = pl.BlockSpec(memory_space=pl.ANY)
    limit = pltpu.CompilerParams(vmem_limit_bytes=16 * 2**20)

    def along(axis, array, target):
        return lax.ppermute(array, axis, [(i, target(i)) for i in range(lax.axis_size(axis))])

    send = pl.pallas_call(
        functools.partial(pack_kernel, blocks, own),
        out_shape=[pltpu.VMEM((span // LANES * rows + extra, LANES), low)] * SPANS,
        in_specs=[hbm] * 3,
        out_specs=[vmem] * SPANS,
        scratch_shapes=[
            pltpu.VMEM((span, count), low),
            pltpu.VMEM((share, BLOCK, LAGS), jnp.float32),
            pltpu.VMEM(lag_mask.shape, jnp.int32),
            pltpu.SemaphoreType.DMA((3,)),
        ],
        compiler_params=limit,
    )(*(pltpu.with_memory_space_constraint(x, pltpu.HBM) for x in (records[0], observed, lag_mask)))
    held = [along("fibre", send[k], lambda i: i ^ k) for k in range(SPANS - 1, 0, -1)]
    held = [send[0]] + held[::-1]
    constants = [jnp.asarray(c) for c in (table, np.ascontiguousarray(table.transpose(0, 2, 1)), lags)]
    table, table_back, lags, take, give, find, order = pl.pallas_call(
        functools.partial(prepare_kernel, segs, blocks, own, pairs_dev, share),
        out_shape=[pltpu.VMEM(c.shape, low) for c in constants]
        + [
            pltpu.VMEM((2 * lines, segs * rows), low),
            pltpu.VMEM((rows, 2 * lines), low),
            pltpu.VMEM((LAGS // LANES, lines, segs * SPANS * extra), low),
            pltpu.VMEM((count, count), low),
        ],
        in_specs=[hbm] * (1 + len(constants)),
        out_specs=[vmem] * (len(constants) + 4),
        scratch_shapes=[pltpu.SMEM(pairs.shape[::-1], jnp.int32), pltpu.SemaphoreType.DMA((1 + len(constants),))],
        compiler_params=limit,
        cost_estimate=pl.CostEstimate(flops=0, bytes_accessed=4 * 2**20, transcendentals=0),
    )(*(pltpu.with_memory_space_constraint(c, pltpu.HBM) for c in [pairs.T] + constants))
    for u in range(1, segs):
        held += [
            along(("fibre", "seg"), send[k], lambda i: (i // segs ^ k) * segs + (i + u) % segs)
            if k in (1,)
            else along("seg", held[k], lambda i: (i + u) % segs)
            for k in range(SPANS - 1, -1, -1)
        ][::-1]
    chosen, partial = pl.pallas_call(
        functools.partial(correlate_kernel, segs, blocks, own),
        out_shape=[pltpu.VMEM((2 * lines, 2 * F), low), pltpu.VMEM((lines, LAGS), jnp.float32)],
        in_specs=[vmem] * (segs * SPANS + 4),
        out_specs=[vmem] * 2,
        compiler_params=limit,
    )(*[held[i] for i in (7, 6, 1, 4, 5, 3, 2, 0)], table, lags, take, find)
    mine, other = partial, along("rec", partial, lambda i: (i + 1) % recs)
    for _ in range(2, recs):
        mine, other = mine + other, along("rec", other, lambda i: (i + 1) % recs)
    back = pl.pallas_call(
        functools.partial(adjoint_kernel, blocks, own),
        out_shape=[pltpu.VMEM((rows, span), low)] * SPANS,
        in_specs=[vmem] * 6,
        out_specs=[vmem] * SPANS,
        compiler_params=limit,
    )(chosen, mine, other, table_back, lags, give)
    own_part = back[0]
    sent = {k: along("fibre", back[k], lambda i: i ^ k) for k in (3, 1, 2)}
    out = pl.pallas_call(
        unpack_kernel,
        out_shape=jax.ShapeDtypeStruct((span, count), low),
        in_specs=[vmem] * (SPANS + 1),
        out_specs=hbm,
        scratch_shapes=[
            pltpu.VMEM((span, count), low),
            pltpu.SemaphoreType.DMA((span // LANES,)),
        ],
        compiler_params=limit,
    )(*sent.values(), own_part, order)
    return out[None]


def by_band(records, pairs, observed, lag_mask):
    fibres, segs = lax.axis_size("fibre"), lax.axis_size("seg")
    own = BLOCK // fibres
    span, count = records.shape[1:]
    blocks = count // BLOCK
    total_blocks = blocks * segs
    pair_total, pairs_dev = pairs.shape[0], observed.shape[0]
    low = jnp.bfloat16
    band = F // segs
    start = lax.axis_index("seg") * band
    table = lax.dynamic_slice_in_dim(jnp.asarray(forward_table()), start, band, 0)
    lags = lax.dynamic_slice_in_dim(jnp.asarray(lag_table()), start, band, 0)
    f32 = functools.partial(jnp.einsum, preferred_element_type=jnp.float32)
    grid = records.reshape(span, blocks, fibres, own).transpose(2, 0, 1, 3)
    signal = lax.all_to_all(grid, "fibre", 0, 0, tiled=True).reshape(S, blocks, own)
    signal = lax.all_gather(signal, "seg", axis=1, tiled=True)
    spectra = f32("wpt,tbk->wpbk", table, signal).astype(low)
    ids = jnp.arange(total_blocks)
    take = [(pairs[:, side, None] == ids).astype(low) for side in range(2)]
    a0, a1 = (f32("nb,wbk->wnk", take[0], spectra[:, p]) for p in range(2))
    b0, b1 = (f32("nb,wbk->wnk", take[1], spectra[:, p]) for p in range(2))
    cross = jnp.stack([a0 * b0 + a1 * b1, a1 * b0 - a0 * b1], axis=1).astype(low)
    corr = f32("wpnk,wpl->nkl", cross, lags)
    corr = corr.reshape(fibres, segs, pairs_dev, own, LAGS)
    corr = lax.psum_scatter(corr, "seg", scatter_dimension=1)
    synthetic = lax.psum(corr, "rec").reshape(fibres * pairs_dev, own, LAGS)
    seen = observed.reshape(pairs_dev, fibres, own, LAGS).transpose(1, 0, 2, 3)
    seen = lax.all_to_all(seen, "fibre", 0, 0, tiled=True).reshape(fibres * pairs_dev, own, LAGS)
    window = lax.all_gather(lag_mask.astype(jnp.float32), "fibre", axis=0, tiled=True)
    weights = (window[:, None, :] * jnp.tanh(synthetic - seen)).astype(low)
    weights = lax.all_gather(weights.reshape(fibres, pairs_dev, own, LAGS), "seg", axis=1)
    weights = weights.reshape(pair_total, own, LAGS)
    adjoint = f32("nkl,wpl->wpnk", weights, lags).astype(low).astype(jnp.float32)
    g0, g1 = adjoint[:, 0], adjoint[:, 1]

    def added(side, terms):
        high = terms.astype(low)
        rest = (terms - high.astype(jnp.float32)).astype(low)
        return f32("nb,wnk->wbk", take[side], high) + f32("nb,wnk->wbk", take[side], rest)

    grad = jnp.stack(
        [
            added(0, g0 * b0 - g1 * b1) + added(1, g0 * a0 + g1 * a1),
            added(0, g0 * b1 + g1 * b0) + added(1, g0 * a1 - g1 * a0),
        ],
        axis=1,
    ).astype(low)
    sources = f32("wpbk,wpt->tbk", grad, table)
    sources = lax.psum_scatter(sources, "seg", scatter_dimension=1, tiled=True).astype(low)
    sources = sources.reshape(fibres, span, blocks, own)
    sources = lax.all_to_all(sources, "fibre", 0, 0, tiled=True)
    return sources.transpose(1, 2, 0, 3).reshape(1, span, count)


def solution(mesh):
    in_specs = (
        P("rec", "fibre", ("groups", "seg")),
        P(),
        P(("groups", "fibre", "seg"), None, None),
        P(("groups", "fibre", "seg"), None),
    )
    out_specs = P("rec", "fibre", ("groups", "seg"))
    small = mesh.shape["fibre"] == SPANS
    return jax.shard_map(
        by_own_k if small else by_band,
        mesh=mesh,
        in_specs=in_specs,
        out_specs=out_specs,
        check_vma=False,
    )
```

```python
import functools

import jax
import jax.numpy as jnp
import numpy as np
from jax import lax
from jax.experimental import pallas as pl
from jax.experimental.pallas import tpu as pltpu
from jax.sharding import PartitionSpec as P

S = 2048
F = 1024
LAGS = 256
BLOCK = 32
SPANS = 4
MASKED = 16384.0
LANES = 128

_NT = (((1,), (1,)), ((), ()))
_TN = (((0,), (0,)), ((), ()))


def wave_table(freq, shift, scale):
    phase = freq[:, None].astype(np.int64) * shift[None, :] % S
    angles = phase.astype(np.float32) * np.float32(2.0 * np.pi / S)
    factor = np.float32(1.0) / np.sqrt(np.float32(scale))
    parts = [(np.cos(angles) * factor), (-np.sin(angles) * factor)]
    return np.stack(parts, axis=1).astype(jnp.bfloat16)


def forward_table():
    return wave_table(np.arange(F), np.arange(S), S)


def lag_table():
    return wave_table(np.arange(F), (np.arange(LAGS) - LAGS // 2) % S, F)


def dot(a, b, dims=(((1,), (0,)), ((), ()))):
    return lax.dot_general(a, b, dims, preferred_element_type=jnp.float32)


def one_hot(rows, cols, hit):
    row = lax.broadcasted_iota(jnp.int32, (rows, cols), 0)
    col = lax.broadcasted_iota(jnp.int32, (rows, cols), 1)
    return jnp.where(hit(row, col), 1.0, 0.0).astype(jnp.bfloat16)


def channel_of(row, fibre, blocks, own):
    to = row // (blocks * own) ^ fibre
    return row % (blocks * own) // own * BLOCK + to * own + row % own


def channel_order(fibre, blocks, own):
    count = blocks * BLOCK
    return one_hot(count, count, lambda r, c: c == channel_of(r, fibre, blocks, own))


def pack_kernel(blocks, own, records_hbm, observed_hbm, mask_hbm, *refs):
    out_refs, (records, observed, mask, sems) = refs[:SPANS], refs[SPANS:]
    fibre = lax.axis_index("fibre")
    span, count = records.shape
    rows = blocks * own
    tiles = span // LANES
    share = observed.shape[0]
    start = lax.axis_index("rec") * share
    records_copy = pltpu.make_async_copy(records_hbm, records, sems.at[0])
    seen_copy = pltpu.make_async_copy(observed_hbm.at[pl.ds(start, share)], observed, sems.at[1])
    mask_copy = pltpu.make_async_copy(mask_hbm, mask, sems.at[2])
    for copy in (records_copy, seen_copy, mask_copy):
        copy.start()
    order = channel_order(fibre, blocks, own)
    lines = share * BLOCK
    halves = LAGS // LANES
    extra = halves * share * own
    place = one_hot(
        SPANS * extra,
        halves * lines,
        lambda r, c: (c % BLOCK // own == r // extra ^ fibre)
        & (c % own == r % own)
        & (c // lines == r % (halves * own) // own)
        & (c % lines // BLOCK == r % extra // (halves * own)),
    )
    seen_copy.wait()
    mask_copy.wait()
    window = jnp.concatenate(
        [mask[pl.ds(start + i, 1), :] + jnp.zeros((BLOCK, 1), jnp.int32) for i in range(share)], axis=0
    )
    seen = jnp.where(window != 0, observed[...].reshape(lines, LAGS), MASKED)
    seen = seen.astype(jnp.bfloat16)
    parts = [seen[:, h * LANES : (h + 1) * LANES] for h in range(halves)]
    packed = dot(place, jnp.concatenate(parts, axis=0)).astype(jnp.bfloat16)
    for k, out_ref in enumerate(out_refs):
        out_ref[tiles * rows :, :] = packed[k * extra : (k + 1) * extra]
    records_copy.wait()
    moved = dot(order, records[...], _NT).astype(jnp.bfloat16)
    for k, out_ref in enumerate(out_refs):
        for q in range(tiles):
            part = moved[k * rows : (k + 1) * rows, q * LANES : (q + 1) * LANES]
            out_ref[q * rows : (q + 1) * rows, :] = part


def prepare_kernel(segs, blocks, own, pairs_dev, share, pairs_hbm, *refs):
    constants = (len(refs) - 6) // 2
    take_ref, give_ref, find_ref, order_ref, pairs_ref, sems = refs[2 * constants :]
    pairs_copy = pltpu.make_async_copy(pairs_hbm, pairs_ref, sems.at[constants])
    copies = [pltpu.make_async_copy(refs[i], refs[constants + i], sems.at[i]) for i in range(constants)]
    for copy in [pairs_copy] + copies:
        copy.start()
    fibre, seg, rec = (lax.axis_index(axis) for axis in ("fibre", "seg", "rec"))
    pair_total = pairs_ref.shape[1]
    rows = blocks * own
    lines = pair_total * own

    def picks(side, line):
        block = jnp.zeros_like(line)
        for n in range(pair_total):
            block = jnp.where(line // own == n, pairs_ref[side, n], block)
        distance = (seg + segs - block // blocks) % segs
        return distance * rows + block % blocks * own + line % own

    halves = LAGS // LANES
    extra = halves * share * own

    def here(half, line, place):
        part = place % extra
        owner = (place // extra % SPANS ^ fibre) * segs + (seg + segs - place // (extra * SPANS)) % segs
        pair = owner * pairs_dev + rec * share + part // (halves * own)
        return (line // own == pair) & (line % own == part % own) & (part % (halves * own) // own == half)

    for h in range(halves):
        find_ref[h] = one_hot(lines, segs * SPANS * extra, functools.partial(here, h))
    order_ref[...] = channel_order(fibre, blocks, own)
    pairs_copy.wait()
    for side in range(2):
        line = lax.broadcasted_iota(jnp.int32, (lines, segs * rows), 0)
        row = lax.broadcasted_iota(jnp.int32, (lines, segs * rows), 1)
        hit = jnp.where(picks(side, line) == row, 1.0, 0.0).astype(jnp.bfloat16)
        take_ref[side * lines : (side + 1) * lines, :] = hit
        line = lax.broadcasted_iota(jnp.int32, (rows, lines), 1)
        row = lax.broadcasted_iota(jnp.int32, (rows, lines), 0)
        hit = jnp.where(picks(side, line) == row, 1.0, 0.0).astype(jnp.bfloat16)
        give_ref[:, side * lines : (side + 1) * lines] = hit
    for copy in copies:
        copy.wait()


def transform(chunks, rows, table_ref):
    fibre = lax.axis_index("fibre")
    span = S // SPANS
    band = F // SPANS
    folds = []
    for chunk in chunks:
        whole = [chunk[q * rows : (q + 1) * rows, :] for q in range(span // LANES)]
        folds.append(jnp.concatenate(whole, axis=1).astype(jnp.float32))
    flip = fibre % 2 == 1
    turn = jnp.where(flip, -1.0, 1.0)
    late = jnp.where(fibre >= 2, -1.0, 1.0)
    near, far = folds[0] + folds[2], folds[1] + folds[3]
    near_gap, far_gap = folds[0] - folds[2], folds[1] - folds[3]
    e_part = late * jnp.where(flip, far_gap, near_gap)
    d_part = late * jnp.where(flip, near_gap, far_gap)
    both = jnp.concatenate([e_part, d_part], axis=0).astype(jnp.bfloat16)
    reals, imags = [], []
    for j in range(SPANS):
        if j % 2 == 0:
            signal = near + far if j == 0 else turn * (near - far)
            part = dot(signal.astype(jnp.bfloat16), table_ref[j])
            real, imag = part[:, :band], part[:, band:]
        else:
            mixed = dot(both, table_ref[j])
            e_c, e_s = mixed[:rows, :band], mixed[:rows, band:]
            d_c, d_s = mixed[rows:, :band], mixed[rows:, band:]
            real, imag = (e_c + d_s, e_s - d_c) if j == 1 else (e_c - d_s, e_s + d_c)
        reals.append(real.astype(jnp.bfloat16))
        imags.append(imag.astype(jnp.bfloat16))
    return jnp.concatenate(reals + imags, axis=1)


def spectra_kernel(blocks, own, *refs):
    refs[-1][...] = transform(refs[:SPANS], blocks * own, refs[SPANS])


def correlate_kernel(segs, blocks, own, *refs):
    chunks = [refs[i] for i in [7, 2, 6, 5, 3, 4, 1, 0]]
    own_ref, table_ref, lag_ref, take_ref, find_ref, chosen_ref, partial_ref = refs[segs * SPANS :]
    rows = blocks * own
    lines = take_ref.shape[0] // 2
    tiles = S // SPANS // LANES
    spectra = [own_ref[...]] + [
        transform(chunks[u * SPANS : (u + 1) * SPANS], rows, table_ref) for u in range(1, segs)
    ]
    spectra = jnp.concatenate(spectra, axis=0)
    chosen = dot(take_ref[...], spectra)
    chosen_ref[...] = chosen.astype(jnp.bfloat16)
    a0, a1 = chosen[:lines, :F], chosen[:lines, F:]
    b0, b1 = chosen[lines:, :F], chosen[lines:, F:]
    cross_re = (a0 * b0 + a1 * b1).astype(jnp.bfloat16)
    cross_im = (a1 * b0 - a0 * b1).astype(jnp.bfloat16)
    partial = dot(jnp.concatenate([cross_re, cross_im], axis=1), lag_ref[...])
    packed = jnp.concatenate([chunk[tiles * rows :, :] for chunk in chunks], axis=0)
    seen = jnp.concatenate([dot(find_ref[h], packed) for h in range(LAGS // LANES)], axis=1)
    partial_ref[...] = partial - seen


def adjoint_kernel(blocks, own, chosen_ref, mine_ref, other_ref, back_ref, lag_ref, give_ref, *out_refs):
    fibre = lax.axis_index("fibre")
    band = F // SPANS
    lines = mine_ref.shape[0]
    count = blocks * own
    misfit = mine_ref[...] + other_ref[...]
    weights = jnp.where(misfit > -0.5 * MASKED, jnp.tanh(misfit), 0.0).astype(jnp.bfloat16)
    adjoint = dot(weights, lag_ref[...], _NT).astype(jnp.bfloat16).astype(jnp.float32)
    g0, g1 = adjoint[:, :F], adjoint[:, F:]
    a0 = chosen_ref[:lines, :F].astype(jnp.float32)
    a1 = chosen_ref[:lines, F:].astype(jnp.float32)
    b0 = chosen_ref[lines:, :F].astype(jnp.float32)
    b1 = chosen_ref[lines:, F:].astype(jnp.float32)
    low = jnp.bfloat16
    first = jnp.concatenate([(g0 * b0 - g1 * b1).astype(low), (g0 * b1 + g1 * b0).astype(low)], axis=1)
    second = jnp.concatenate([(g0 * a0 + g1 * a1).astype(low), (g0 * a1 - g1 * a0).astype(low)], axis=1)
    grad = dot(give_ref[...], jnp.concatenate([first, second], axis=0)).astype(low)
    even, odd = None, None
    for j in range(SPANS):
        real = grad[:, j * band : (j + 1) * band]
        imag = grad[:, F + j * band : F + (j + 1) * band]
        line = jnp.concatenate([real, imag], axis=1)
        if j % 2 == 0:
            part = dot(line, back_ref[j])
            even = (part, part) if j == 0 else (even[0] + part, even[1] - part)
        else:
            turned = jnp.concatenate([-imag, real], axis=1)
            part = dot(jnp.concatenate([line, turned], axis=0), back_ref[j])
            u, v = part[:count], part[count:]
            odd = (u, v) if j == 1 else (odd[0] + u, odd[1] - v)
    flip = fibre % 2 == 1
    late = jnp.where(fibre >= 2, -1.0, 1.0)
    for k, out_ref in enumerate(out_refs):
        other = flip if k % 2 == 0 else ~flip
        base = jnp.where(other, even[1], even[0])
        side = late * jnp.where(other, odd[1], odd[0])
        out_ref[...] = (base + side if k < 2 else base - side).astype(low)


def unpack_kernel(*refs):
    chunks = [refs[i] for i in [3, 1, 2, 0]]
    order_ref, out_hbm, out, sems = refs[SPANS:]
    span = out.shape[0]
    cuts = [pl.ds(q * LANES, LANES) for q in range(span // LANES)]
    leave = [pltpu.make_async_copy(out.at[cut], out_hbm.at[cut], sems.at[q]) for q, cut in enumerate(cuts)]
    for q, copy in enumerate(leave):
        held = jnp.concatenate([chunk[:, q * LANES : (q + 1) * LANES] for chunk in chunks], axis=0)
        out[q * LANES : (q + 1) * LANES, :] = dot(held, order_ref[...], _TN).astype(jnp.bfloat16)
        copy.start()
    for copy in leave:
        copy.wait()


def by_own_k(records, pairs, observed, lag_mask):
    recs, segs, fibres = (lax.axis_size(axis) for axis in ("rec", "seg", "fibre"))
    own = BLOCK // fibres
    span, count = records.shape[1:]
    blocks = count // BLOCK
    rows = blocks * own
    pair_total, pairs_dev = pairs.shape[0], observed.shape[0]
    share = pairs_dev // recs
    lines = pair_total * own
    extra = LAGS // LANES * share * own
    table = forward_table().reshape(F // SPANS, SPANS, 2, SPANS, span)[:, :, :, 0]
    table = np.ascontiguousarray(table.transpose(1, 3, 2, 0)).reshape(SPANS, span, S // SPANS)
    lags = lag_table().reshape(F // SPANS, SPANS, 2, LAGS)
    lags = np.ascontiguousarray(lags.transpose(2, 1, 0, 3)).reshape(2 * F, LAGS)
    low = jnp.bfloat16
    vmem = pl.BlockSpec(memory_space=pltpu.VMEM)
    hbm = pl.BlockSpec(memory_space=pl.ANY)
    limit = pltpu.CompilerParams(vmem_limit_bytes=16 * 2**20)

    def along(axis, array, target):
        return lax.ppermute(array, axis, [(i, target(i)) for i in range(lax.axis_size(axis))])

    send = pl.pallas_call(
        functools.partial(pack_kernel, blocks, own),
        out_shape=[pltpu.VMEM((span // LANES * rows + extra, LANES), low)] * SPANS,
        in_specs=[hbm] * 3,
        out_specs=[vmem] * SPANS,
        scratch_shapes=[
            pltpu.VMEM((span, count), low),
            pltpu.VMEM((share, BLOCK, LAGS), jnp.float32),
            pltpu.VMEM(lag_mask.shape, jnp.int32),
            pltpu.SemaphoreType.DMA((3,)),
        ],
        compiler_params=limit,
    )(*(pltpu.with_memory_space_constraint(x, pltpu.HBM) for x in (records[0], observed, lag_mask)))
    held = [along("fibre", send[k], lambda i: i ^ k) for k in range(SPANS - 1, 0, -1)]
    held = [send[0]] + held[::-1]
    table_back = jnp.asarray(np.ascontiguousarray(table.transpose(0, 2, 1)))
    constants = [jnp.asarray(c) for c in (table, lags)]
    table, lags, take, give, find, order = pl.pallas_call(
        functools.partial(prepare_kernel, segs, blocks, own, pairs_dev, share),
        out_shape=[pltpu.VMEM(c.shape, low) for c in constants]
        + [
            pltpu.VMEM((2 * lines, segs * rows), low),
            pltpu.VMEM((rows, 2 * lines), low),
            pltpu.VMEM((LAGS // LANES, lines, segs * SPANS * extra), low),
            pltpu.VMEM((count, count), low),
        ],
        in_specs=[hbm] * (1 + len(constants)),
        out_specs=[vmem] * (len(constants) + 4),
        scratch_shapes=[pltpu.SMEM(pairs.shape[::-1], jnp.int32), pltpu.SemaphoreType.DMA((1 + len(constants),))],
        compiler_params=limit,
        cost_estimate=pl.CostEstimate(flops=0, bytes_accessed=4 * 2**20, transcendentals=0),
    )(*(pltpu.with_memory_space_constraint(c, pltpu.HBM) for c in [pairs.T] + constants))
    for u in range(1, segs):
        held += [
            along(("fibre", "seg"), send[k], lambda i: (i // segs ^ k) * segs + (i + u) % segs)
            if k in (1,)
            else along("seg", held[k], lambda i: (i + u) % segs)
            for k in range(SPANS - 1, -1, -1)
        ][::-1]
    spectra = pl.pallas_call(
        functools.partial(spectra_kernel, blocks, own),
        out_shape=pltpu.VMEM((rows, 2 * F), low),
        in_specs=[vmem] * (SPANS + 1),
        out_specs=vmem,
        compiler_params=limit,
    )(*held[:SPANS], table)
    chosen, partial = pl.pallas_call(
        functools.partial(correlate_kernel, segs, blocks, own),
        out_shape=[pltpu.VMEM((2 * lines, 2 * F), low), pltpu.VMEM((lines, LAGS), jnp.float32)],
        in_specs=[vmem] * (segs * SPANS + 5),
        out_specs=[vmem] * 2,
        compiler_params=limit,
    )(*[held[i] for i in (7, 6, 1, 4, 5, 3, 2, 0)], spectra, table, lags, take, find)
    mine, other = partial, along("rec", partial, lambda i: (i + 1) % recs)
    for _ in range(2, recs):
        mine, other = mine + other, along("rec", other, lambda i: (i + 1) % recs)
    back = pl.pallas_call(
        functools.partial(adjoint_kernel, blocks, own),
        out_shape=[pltpu.VMEM((rows, span), low)] * SPANS,
        in_specs=[vmem] * 6,
        out_specs=[vmem] * SPANS,
        compiler_params=limit,
    )(chosen, mine, other, table_back, lags, give)
    own_part = back[0]
    sent = {k: along("fibre", back[k], lambda i: i ^ k) for k in (3, 1, 2)}
    out = pl.pallas_call(
        unpack_kernel,
        out_shape=jax.ShapeDtypeStruct((span, count), low),
        in_specs=[vmem] * (SPANS + 1),
        out_specs=hbm,
        scratch_shapes=[
            pltpu.VMEM((span, count), low),
            pltpu.SemaphoreType.DMA((span // LANES,)),
        ],
        compiler_params=limit,
    )(*sent.values(), own_part, order)
    return out[None]


def by_band(records, pairs, observed, lag_mask):
    fibres, segs = lax.axis_size("fibre"), lax.axis_size("seg")
    own = BLOCK // fibres
    span, count = records.shape[1:]
    blocks = count // BLOCK
    total_blocks = blocks * segs
    pair_total, pairs_dev = pairs.shape[0], observed.shape[0]
    low = jnp.bfloat16
    band = F // segs
    start = lax.axis_index("seg") * band
    table = lax.dynamic_slice_in_dim(jnp.asarray(forward_table()), start, band, 0)
    lags = lax.dynamic_slice_in_dim(jnp.asarray(lag_table()), start, band, 0)
    f32 = functools.partial(jnp.einsum, preferred_element_type=jnp.float32)
    grid = records.reshape(span, blocks, fibres, own).transpose(2, 0, 1, 3)
    signal = lax.all_to_all(grid, "fibre", 0, 0, tiled=True).reshape(S, blocks, own)
    signal = lax.all_gather(signal, "seg", axis=1, tiled=True)
    spectra = f32("wpt,tbk->wpbk", table, signal).astype(low)
    ids = jnp.arange(total_blocks)
    take = [(pairs[:, side, None] == ids).astype(low) for side in range(2)]
    a0, a1 = (f32("nb,wbk->wnk", take[0], spectra[:, p]) for p in range(2))
    b0, b1 = (f32("nb,wbk->wnk", take[1], spectra[:, p]) for p in range(2))
    cross = jnp.stack([a0 * b0 + a1 * b1, a1 * b0 - a0 * b1], axis=1).astype(low)
    corr = f32("wpnk,wpl->nkl", cross, lags)
    corr = corr.reshape(fibres, segs, pairs_dev, own, LAGS)
    corr = lax.psum_scatter(corr, "seg", scatter_dimension=1)
    synthetic = lax.psum(corr, "rec").reshape(fibres * pairs_dev, own, LAGS)
    seen = observed.reshape(pairs_dev, fibres, own, LAGS).transpose(1, 0, 2, 3)
    seen = lax.all_to_all(seen, "fibre", 0, 0, tiled=True).reshape(fibres * pairs_dev, own, LAGS)
    window = lax.all_gather(lag_mask.astype(jnp.float32), "fibre", axis=0, tiled=True)
    weights = (window[:, None, :] * jnp.tanh(synthetic - seen)).astype(low)
    weights = lax.all_gather(weights.reshape(fibres, pairs_dev, own, LAGS), "seg", axis=1)
    weights = weights.reshape(pair_total, own, LAGS)
    adjoint = f32("nkl,wpl->wpnk", weights, lags).astype(low).astype(jnp.float32)
    g0, g1 = adjoint[:, 0], adjoint[:, 1]

    def added(side, terms):
        high = terms.astype(low)
        rest = (terms - high.astype(jnp.float32)).astype(low)
        return f32("nb,wnk->wbk", take[side], high) + f32("nb,wnk->wbk", take[side], rest)

    grad = jnp.stack(
        [
            added(0, g0 * b0 - g1 * b1) + added(1, g0 * a0 + g1 * a1),
            added(0, g0 * b1 + g1 * b0) + added(1, g0 * a1 - g1 * a0),
        ],
        axis=1,
    ).astype(low)
    sources = f32("wpbk,wpt->tbk", grad, table)
    sources = lax.psum_scatter(sources, "seg", scatter_dimension=1, tiled=True).astype(low)
    sources = sources.reshape(fibres, span, blocks, own)
    sources = lax.all_to_all(sources, "fibre", 0, 0, tiled=True)
    return sources.transpose(1, 2, 0, 3).reshape(1, span, count)


def solution(mesh):
    in_specs = (
        P("rec", "fibre", ("groups", "seg")),
        P(),
        P(("groups", "fibre", "seg"), None, None),
        P(("groups", "fibre", "seg"), None),
    )
    out_specs = P("rec", "fibre", ("groups", "seg"))
    small = mesh.shape["fibre"] == SPANS
    return jax.shard_map(
        by_own_k if small else by_band,
        mesh=mesh,
        in_specs=in_specs,
        out_specs=out_specs,
        check_vma=False,
    )
```

```python
import functools

import jax
import jax.numpy as jnp
import numpy as np
from jax import lax
from jax.experimental import pallas as pl
from jax.experimental.pallas import tpu as pltpu
from jax.sharding import PartitionSpec as P

S = 2048
F = 1024
LAGS = 256
BLOCK = 32
SPANS = 4
MASKED = 16384.0
LANES = 128

_NT = (((1,), (1,)), ((), ()))
_TN = (((0,), (0,)), ((), ()))


def wave_table(freq, shift, scale):
    phase = freq[:, None].astype(np.int64) * shift[None, :] % S
    angles = phase.astype(np.float32) * np.float32(2.0 * np.pi / S)
    factor = np.float32(1.0) / np.sqrt(np.float32(scale))
    parts = [(np.cos(angles) * factor), (-np.sin(angles) * factor)]
    return np.stack(parts, axis=1).astype(jnp.bfloat16)


def forward_table():
    return wave_table(np.arange(F), np.arange(S), S)


def lag_table():
    return wave_table(np.arange(F), (np.arange(LAGS) - LAGS // 2) % S, F)


def dot(a, b, dims=(((1,), (0,)), ((), ()))):
    return lax.dot_general(a, b, dims, preferred_element_type=jnp.float32)


def one_hot(rows, cols, hit):
    row = lax.broadcasted_iota(jnp.int32, (rows, cols), 0)
    col = lax.broadcasted_iota(jnp.int32, (rows, cols), 1)
    return jnp.where(hit(row, col), 1.0, 0.0).astype(jnp.bfloat16)


def channel_of(row, fibre, blocks, own):
    to = row // (blocks * own) ^ fibre
    return row % (blocks * own) // own * BLOCK + to * own + row % own


def channel_order(fibre, blocks, own):
    count = blocks * BLOCK
    return one_hot(count, count, lambda r, c: c == channel_of(r, fibre, blocks, own))


def pack_kernel(blocks, own, records_hbm, observed_hbm, mask_hbm, *refs):
    out_refs, (records, observed, mask, sems) = refs[:SPANS], refs[SPANS:]
    fibre = lax.axis_index("fibre")
    span, count = records.shape
    rows = blocks * own
    tiles = span // LANES
    share = observed.shape[0]
    start = lax.axis_index("rec") * share
    records_copy = pltpu.make_async_copy(records_hbm, records, sems.at[0])
    seen_copy = pltpu.make_async_copy(observed_hbm.at[pl.ds(start, share)], observed, sems.at[1])
    mask_copy = pltpu.make_async_copy(mask_hbm, mask, sems.at[2])
    for copy in (records_copy, seen_copy, mask_copy):
        copy.start()
    order = channel_order(fibre, blocks, own)
    lines = share * BLOCK
    halves = LAGS // LANES
    extra = halves * share * own
    place = one_hot(
        SPANS * extra,
        halves * lines,
        lambda r, c: (c % BLOCK // own == r // extra ^ fibre)
        & (c % own == r % own)
        & (c // lines == r % (halves * own) // own)
        & (c % lines // BLOCK == r % extra // (halves * own)),
    )
    seen_copy.wait()
    mask_copy.wait()
    window = jnp.concatenate(
        [mask[pl.ds(start + i, 1), :] + jnp.zeros((BLOCK, 1), jnp.int32) for i in range(share)], axis=0
    )
    seen = jnp.where(window != 0, observed[...].reshape(lines, LAGS), MASKED)
    seen = seen.astype(jnp.bfloat16)
    parts = [seen[:, h * LANES : (h + 1) * LANES] for h in range(halves)]
    packed = dot(place, jnp.concatenate(parts, axis=0)).astype(jnp.bfloat16)
    for k, out_ref in enumerate(out_refs):
        out_ref[tiles * rows :, :] = packed[k * extra : (k + 1) * extra]
    records_copy.wait()
    moved = dot(order, records[...], _NT).astype(jnp.bfloat16)
    for k, out_ref in enumerate(out_refs):
        for q in range(tiles):
            part = moved[k * rows : (k + 1) * rows, q * LANES : (q + 1) * LANES]
            out_ref[q * rows : (q + 1) * rows, :] = part


def prepare_kernel(segs, blocks, own, pairs_dev, share, pairs_hbm, *refs):
    constants = (len(refs) - 6) // 2
    take_ref, give_ref, find_ref, order_ref, pairs_ref, sems = refs[2 * constants :]
    pairs_copy = pltpu.make_async_copy(pairs_hbm, pairs_ref, sems.at[constants])
    copies = [pltpu.make_async_copy(refs[i], refs[constants + i], sems.at[i]) for i in range(constants)]
    for copy in [pairs_copy] + copies:
        copy.start()
    fibre, seg, rec = (lax.axis_index(axis) for axis in ("fibre", "seg", "rec"))
    pair_total = pairs_ref.shape[1]
    rows = blocks * own
    lines = pair_total * own

    def picks(side, line):
        block = jnp.zeros_like(line)
        for n in range(pair_total):
            block = jnp.where(line // own == n, pairs_ref[side, n], block)
        distance = (seg + segs - block // blocks) % segs
        return distance * rows + block % blocks * own + line % own

    halves = LAGS // LANES
    extra = halves * share * own

    def here(half, line, place):
        part = place % extra
        owner = (place // extra % SPANS ^ fibre) * segs + (seg + segs - place // (extra * SPANS)) % segs
        pair = owner * pairs_dev + rec * share + part // (halves * own)
        return (line // own == pair) & (line % own == part % own) & (part % (halves * own) // own == half)

    for h in range(halves):
        find_ref[h] = one_hot(lines, segs * SPANS * extra, functools.partial(here, h))
    order_ref[...] = channel_order(fibre, blocks, own)
    pairs_copy.wait()
    for side in range(2):
        line = lax.broadcasted_iota(jnp.int32, (lines, segs * rows), 0)
        row = lax.broadcasted_iota(jnp.int32, (lines, segs * rows), 1)
        hit = jnp.where(picks(side, line) == row, 1.0, 0.0).astype(jnp.bfloat16)
        take_ref[side * lines : (side + 1) * lines, :] = hit
        line = lax.broadcasted_iota(jnp.int32, (rows, lines), 1)
        row = lax.broadcasted_iota(jnp.int32, (rows, lines), 0)
        hit = jnp.where(picks(side, line) == row, 1.0, 0.0).astype(jnp.bfloat16)
        give_ref[:, side * lines : (side + 1) * lines] = hit
    for copy in copies:
        copy.wait()


def transform(chunks, rows, table_ref):
    fibre = lax.axis_index("fibre")
    span = S // SPANS
    band = F // SPANS
    folds = []
    for chunk in chunks:
        whole = [chunk[q * rows : (q + 1) * rows, :] for q in range(span // LANES)]
        folds.append(jnp.concatenate(whole, axis=1).astype(jnp.float32))
    flip = fibre % 2 == 1
    turn = jnp.where(flip, -1.0, 1.0)
    late = jnp.where(fibre >= 2, -1.0, 1.0)
    near, far = folds[0] + folds[2], folds[1] + folds[3]
    near_gap, far_gap = folds[0] - folds[2], folds[1] - folds[3]
    e_part = late * jnp.where(flip, far_gap, near_gap)
    d_part = late * jnp.where(flip, near_gap, far_gap)
    both = jnp.concatenate([e_part, d_part], axis=0).astype(jnp.bfloat16)
    reals, imags = [], []
    for j in range(SPANS):
        if j % 2 == 0:
            signal = near + far if j == 0 else turn * (near - far)
            part = dot(signal.astype(jnp.bfloat16), table_ref[j])
            real, imag = part[:, :band], part[:, band:]
        else:
            mixed = dot(both, table_ref[j])
            e_c, e_s = mixed[:rows, :band], mixed[:rows, band:]
            d_c, d_s = mixed[rows:, :band], mixed[rows:, band:]
            real, imag = (e_c + d_s, e_s - d_c) if j == 1 else (e_c - d_s, e_s + d_c)
        reals.append(real.astype(jnp.bfloat16))
        imags.append(imag.astype(jnp.bfloat16))
    return jnp.concatenate(reals + imags, axis=1)


def spectra_kernel(blocks, own, *refs):
    refs[-1][...] = transform(refs[:SPANS], blocks * own, refs[SPANS])


def correlate_kernel(segs, blocks, own, *refs):
    chunks = [refs[i] for i in [7, 2, 6, 5, 3, 4, 1, 0]]
    own_ref, table_ref, lag_ref, take_ref, find_ref, chosen_ref, partial_ref, sent_ref = refs[segs * SPANS :]
    rows = blocks * own
    lines = take_ref.shape[0] // 2
    tiles = S // SPANS // LANES
    spectra = [own_ref[...]] + [
        transform(chunks[u * SPANS : (u + 1) * SPANS], rows, table_ref) for u in range(1, segs)
    ]
    spectra = jnp.concatenate(spectra, axis=0)
    chosen = dot(take_ref[...], spectra)
    chosen_ref[...] = chosen.astype(jnp.bfloat16)
    a0, a1 = chosen[:lines, :F], chosen[:lines, F:]
    b0, b1 = chosen[lines:, :F], chosen[lines:, F:]
    cross_re = (a0 * b0 + a1 * b1).astype(jnp.bfloat16)
    cross_im = (a1 * b0 - a0 * b1).astype(jnp.bfloat16)
    partial = dot(jnp.concatenate([cross_re, cross_im], axis=1), lag_ref[...])
    packed = jnp.concatenate([chunk[tiles * rows :, :] for chunk in chunks], axis=0)
    seen = jnp.concatenate([dot(find_ref[h], packed) for h in range(LAGS // LANES)], axis=1)
    partial_ref[...] = partial - seen
    sent_ref[...] = (partial - seen).astype(jnp.bfloat16)


def adjoint_kernel(blocks, own, chosen_ref, mine_ref, other_ref, back_ref, lag_ref, give_ref, *out_refs):
    fibre = lax.axis_index("fibre")
    band = F // SPANS
    lines = mine_ref.shape[0]
    count = blocks * own
    misfit = mine_ref[...] + other_ref[...].astype(jnp.float32)
    weights = jnp.where(misfit > -0.5 * MASKED, jnp.tanh(misfit), 0.0).astype(jnp.bfloat16)
    adjoint = dot(weights, lag_ref[...], _NT).astype(jnp.bfloat16)
    g0, g1 = adjoint[:, :F], adjoint[:, F:]
    a0 = chosen_ref[:lines, :F]
    a1 = chosen_ref[:lines, F:]
    b0 = chosen_ref[lines:, :F]
    b1 = chosen_ref[lines:, F:]
    low = jnp.bfloat16
    first = jnp.concatenate([(g0 * b0 - g1 * b1).astype(low), (g0 * b1 + g1 * b0).astype(low)], axis=1)
    second = jnp.concatenate([(g0 * a0 + g1 * a1).astype(low), (g0 * a1 - g1 * a0).astype(low)], axis=1)
    grad = dot(give_ref[...], jnp.concatenate([first, second], axis=0)).astype(low)
    even, odd = None, None
    for j in range(SPANS):
        real = grad[:, j * band : (j + 1) * band]
        imag = grad[:, F + j * band : F + (j + 1) * band]
        line = jnp.concatenate([real, imag], axis=1)
        if j % 2 == 0:
            part = dot(line, back_ref[j])
            even = (part, part) if j == 0 else (even[0] + part, even[1] - part)
        else:
            turned = jnp.concatenate([-imag, real], axis=1)
            part = dot(jnp.concatenate([line, turned], axis=0), back_ref[j])
            u, v = part[:count], part[count:]
            odd = (u, v) if j == 1 else (odd[0] + u, odd[1] - v)
    flip = fibre % 2 == 1
    late = jnp.where(fibre >= 2, -1.0, 1.0)
    for k, out_ref in enumerate(out_refs):
        other = flip if k % 2 == 0 else ~flip
        base = jnp.where(other, even[1], even[0])
        side = late * jnp.where(other, odd[1], odd[0])
        out_ref[...] = (base + side if k < 2 else base - side).astype(low)


def unpack_kernel(*refs):
    chunks = [refs[i] for i in [3, 1, 2, 0]]
    order_ref, out_hbm, out, sems = refs[SPANS:]
    span = out.shape[0]
    cuts = [pl.ds(q * LANES, LANES) for q in range(span // LANES)]
    leave = [pltpu.make_async_copy(out.at[cut], out_hbm.at[cut], sems.at[q]) for q, cut in enumerate(cuts)]
    for q, copy in enumerate(leave):
        held = jnp.concatenate([chunk[:, q * LANES : (q + 1) * LANES] for chunk in chunks], axis=0)
        out[q * LANES : (q + 1) * LANES, :] = dot(held, order_ref[...], _TN).astype(jnp.bfloat16)
        copy.start()
    for copy in leave:
        copy.wait()


def by_own_k(records, pairs, observed, lag_mask):
    recs, segs, fibres = (lax.axis_size(axis) for axis in ("rec", "seg", "fibre"))
    own = BLOCK // fibres
    span, count = records.shape[1:]
    blocks = count // BLOCK
    rows = blocks * own
    pair_total, pairs_dev = pairs.shape[0], observed.shape[0]
    share = pairs_dev // recs
    lines = pair_total * own
    extra = LAGS // LANES * share * own
    table = forward_table().reshape(F // SPANS, SPANS, 2, SPANS, span)[:, :, :, 0]
    table = np.ascontiguousarray(table.transpose(1, 3, 2, 0)).reshape(SPANS, span, S // SPANS)
    lags = lag_table().reshape(F // SPANS, SPANS, 2, LAGS)
    lags = np.ascontiguousarray(lags.transpose(2, 1, 0, 3)).reshape(2 * F, LAGS)
    low = jnp.bfloat16
    vmem = pl.BlockSpec(memory_space=pltpu.VMEM)
    hbm = pl.BlockSpec(memory_space=pl.ANY)
    limit = pltpu.CompilerParams(vmem_limit_bytes=16 * 2**20)

    def along(axis, array, target):
        return lax.ppermute(array, axis, [(i, target(i)) for i in range(lax.axis_size(axis))])

    send = pl.pallas_call(
        functools.partial(pack_kernel, blocks, own),
        out_shape=[pltpu.VMEM((span // LANES * rows + extra, LANES), low)] * SPANS,
        in_specs=[hbm] * 3,
        out_specs=[vmem] * SPANS,
        scratch_shapes=[
            pltpu.VMEM((span, count), low),
            pltpu.VMEM((share, BLOCK, LAGS), jnp.float32),
            pltpu.VMEM(lag_mask.shape, jnp.int32),
            pltpu.SemaphoreType.DMA((3,)),
        ],
        compiler_params=limit,
    )(*(pltpu.with_memory_space_constraint(x, pltpu.HBM) for x in (records[0], observed, lag_mask)))
    held = [along("fibre", send[k], lambda i: i ^ k) for k in range(SPANS - 1, 0, -1)]
    held = [send[0]] + held[::-1]
    table_back = jnp.asarray(np.ascontiguousarray(table.transpose(0, 2, 1)))
    constants = [jnp.asarray(c) for c in (table, lags)]
    table, lags, take, give, find, order = pl.pallas_call(
        functools.partial(prepare_kernel, segs, blocks, own, pairs_dev, share),
        out_shape=[pltpu.VMEM(c.shape, low) for c in constants]
        + [
            pltpu.VMEM((2 * lines, segs * rows), low),
            pltpu.VMEM((rows, 2 * lines), low),
            pltpu.VMEM((LAGS // LANES, lines, segs * SPANS * extra), low),
            pltpu.VMEM((count, count), low),
        ],
        in_specs=[hbm] * (1 + len(constants)),
        out_specs=[vmem] * (len(constants) + 4),
        scratch_shapes=[pltpu.SMEM(pairs.shape[::-1], jnp.int32), pltpu.SemaphoreType.DMA((1 + len(constants),))],
        compiler_params=limit,
        cost_estimate=pl.CostEstimate(flops=0, bytes_accessed=4 * 2**20, transcendentals=0),
    )(*(pltpu.with_memory_space_constraint(c, pltpu.HBM) for c in [pairs.T] + constants))
    for u in range(1, segs):
        held += [
            along(("fibre", "seg"), send[k], lambda i: (i // segs ^ k) * segs + (i + u) % segs)
            if k in (1,)
            else along("seg", held[k], lambda i: (i + u) % segs)
            for k in range(SPANS - 1, -1, -1)
        ][::-1]
    spectra = pl.pallas_call(
        functools.partial(spectra_kernel, blocks, own),
        out_shape=pltpu.VMEM((rows, 2 * F), low),
        in_specs=[vmem] * (SPANS + 1),
        out_specs=vmem,
        compiler_params=limit,
    )(*held[:SPANS], table)
    chosen, partial, rounded = pl.pallas_call(
        functools.partial(correlate_kernel, segs, blocks, own),
        out_shape=[pltpu.VMEM((2 * lines, 2 * F), low), pltpu.VMEM((lines, LAGS), jnp.float32), pltpu.VMEM((lines, LAGS), low)],
        in_specs=[vmem] * (segs * SPANS + 5),
        out_specs=[vmem] * 3,
        compiler_params=limit,
    )(*[held[i] for i in (7, 6, 1, 4, 5, 3, 2, 0)], spectra, table, lags, take, find)
    mine, other = partial, along("rec", rounded, lambda i: (i + 1) % recs)
    for _ in range(2, recs):
        mine, other = mine + other, along("rec", other, lambda i: (i + 1) % recs)
    back = pl.pallas_call(
        functools.partial(adjoint_kernel, blocks, own),
        out_shape=[pltpu.VMEM((rows, span), low)] * SPANS,
        in_specs=[vmem] * 6,
        out_specs=[vmem] * SPANS,
        compiler_params=limit,
    )(chosen, mine, other, table_back, lags, give)
    own_part = back[0]
    sent = {k: along("fibre", back[k], lambda i: i ^ k) for k in (3, 1, 2)}
    out = pl.pallas_call(
        unpack_kernel,
        out_shape=jax.ShapeDtypeStruct((span, count), low),
        in_specs=[vmem] * (SPANS + 1),
        out_specs=hbm,
        scratch_shapes=[
            pltpu.VMEM((span, count), low),
            pltpu.SemaphoreType.DMA((span // LANES,)),
        ],
        compiler_params=limit,
    )(*sent.values(), own_part, order)
    return out[None]


def by_band(records, pairs, observed, lag_mask):
    fibres, segs = lax.axis_size("fibre"), lax.axis_size("seg")
    own = BLOCK // fibres
    span, count = records.shape[1:]
    blocks = count // BLOCK
    total_blocks = blocks * segs
    pair_total, pairs_dev = pairs.shape[0], observed.shape[0]
    low = jnp.bfloat16
    band = F // segs
    start = lax.axis_index("seg") * band
    table = lax.dynamic_slice_in_dim(jnp.asarray(forward_table()), start, band, 0)
    lags = lax.dynamic_slice_in_dim(jnp.asarray(lag_table()), start, band, 0)
    f32 = functools.partial(jnp.einsum, preferred_element_type=jnp.float32)
    grid = records.reshape(span, blocks, fibres, own).transpose(2, 0, 1, 3)
    signal = lax.all_to_all(grid, "fibre", 0, 0, tiled=True).reshape(S, blocks, own)
    signal = lax.all_gather(signal, "seg", axis=1, tiled=True)
    spectra = f32("wpt,tbk->wpbk", table, signal).astype(low)
    ids = jnp.arange(total_blocks)
    take = [(pairs[:, side, None] == ids).astype(low) for side in range(2)]
    a0, a1 = (f32("nb,wbk->wnk", take[0], spectra[:, p]) for p in range(2))
    b0, b1 = (f32("nb,wbk->wnk", take[1], spectra[:, p]) for p in range(2))
    cross = jnp.stack([a0 * b0 + a1 * b1, a1 * b0 - a0 * b1], axis=1).astype(low)
    corr = f32("wpnk,wpl->nkl", cross, lags)
    corr = corr.reshape(fibres, segs, pairs_dev, own, LAGS)
    corr = lax.psum_scatter(corr, "seg", scatter_dimension=1)
    synthetic = lax.psum(corr, "rec").reshape(fibres * pairs_dev, own, LAGS)
    seen = observed.reshape(pairs_dev, fibres, own, LAGS).transpose(1, 0, 2, 3)
    seen = lax.all_to_all(seen, "fibre", 0, 0, tiled=True).reshape(fibres * pairs_dev, own, LAGS)
    window = lax.all_gather(lag_mask.astype(jnp.float32), "fibre", axis=0, tiled=True)
    weights = (window[:, None, :] * jnp.tanh(synthetic - seen)).astype(low)
    weights = lax.all_gather(weights.reshape(fibres, pairs_dev, own, LAGS), "seg", axis=1)
    weights = weights.reshape(pair_total, own, LAGS)
    adjoint = f32("nkl,wpl->wpnk", weights, lags).astype(low).astype(jnp.float32)
    g0, g1 = adjoint[:, 0], adjoint[:, 1]

    def added(side, terms):
        high = terms.astype(low)
        rest = (terms - high.astype(jnp.float32)).astype(low)
        return f32("nb,wnk->wbk", take[side], high) + f32("nb,wnk->wbk", take[side], rest)

    grad = jnp.stack(
        [
            added(0, g0 * b0 - g1 * b1) + added(1, g0 * a0 + g1 * a1),
            added(0, g0 * b1 + g1 * b0) + added(1, g0 * a1 - g1 * a0),
        ],
        axis=1,
    ).astype(low)
    sources = f32("wpbk,wpt->tbk", grad, table)
    sources = lax.psum_scatter(sources, "seg", scatter_dimension=1, tiled=True).astype(low)
    sources = sources.reshape(fibres, span, blocks, own)
    sources = lax.all_to_all(sources, "fibre", 0, 0, tiled=True)
    return sources.transpose(1, 2, 0, 3).reshape(1, span, count)


def solution(mesh):
    in_specs = (
        P("rec", "fibre", ("groups", "seg")),
        P(),
        P(("groups", "fibre", "seg"), None, None),
        P(("groups", "fibre", "seg"), None),
    )
    out_specs = P("rec", "fibre", ("groups", "seg"))
    small = mesh.shape["fibre"] == SPANS
    return jax.shard_map(
        by_own_k if small else by_band,
        mesh=mesh,
        in_specs=in_specs,
        out_specs=out_specs,
        check_vma=False,
    )
```

```python
import functools

import jax
import jax.numpy as jnp
import numpy as np
from jax import lax
from jax.experimental import pallas as pl
from jax.experimental.pallas import tpu as pltpu
from jax.sharding import PartitionSpec as P

S = 2048
F = 1024
LAGS = 256
BLOCK = 32
SPANS = 4
MASKED = 16384.0
LANES = 128

_NT = (((1,), (1,)), ((), ()))
_TN = (((0,), (0,)), ((), ()))


def wave_table(freq, shift, scale):
    phase = freq[:, None].astype(np.int64) * shift[None, :] % S
    angles = phase.astype(np.float32) * np.float32(2.0 * np.pi / S)
    factor = np.float32(1.0) / np.sqrt(np.float32(scale))
    parts = [(np.cos(angles) * factor), (-np.sin(angles) * factor)]
    return np.stack(parts, axis=1).astype(jnp.bfloat16)


def forward_table():
    return wave_table(np.arange(F), np.arange(S), S)


def lag_table():
    return wave_table(np.arange(F), (np.arange(LAGS) - LAGS // 2) % S, F)


def dot(a, b, dims=(((1,), (0,)), ((), ()))):
    return lax.dot_general(a, b, dims, preferred_element_type=jnp.float32)


def one_hot(rows, cols, hit):
    row = lax.broadcasted_iota(jnp.int32, (rows, cols), 0)
    col = lax.broadcasted_iota(jnp.int32, (rows, cols), 1)
    return jnp.where(hit(row, col), 1.0, 0.0).astype(jnp.bfloat16)


def channel_of(row, fibre, blocks, own):
    to = row // (blocks * own) ^ fibre
    return row % (blocks * own) // own * BLOCK + to * own + row % own


def channel_order(fibre, blocks, own):
    count = blocks * BLOCK
    return one_hot(count, count, lambda r, c: c == channel_of(r, fibre, blocks, own))


def pack_kernel(blocks, own, records_hbm, observed_hbm, mask_hbm, *refs):
    out_refs, (records, observed, mask, sems) = refs[:SPANS], refs[SPANS:]
    fibre = lax.axis_index("fibre")
    span, count = records.shape
    rows = blocks * own
    tiles = span // LANES
    share = observed.shape[0]
    start = lax.axis_index("rec") * share
    records_copy = pltpu.make_async_copy(records_hbm, records, sems.at[0])
    seen_copy = pltpu.make_async_copy(observed_hbm.at[pl.ds(start, share)], observed, sems.at[1])
    mask_copy = pltpu.make_async_copy(mask_hbm, mask, sems.at[2])
    for copy in (records_copy, seen_copy, mask_copy):
        copy.start()
    order = channel_order(fibre, blocks, own)
    lines = share * BLOCK
    halves = LAGS // LANES
    extra = halves * share * own
    place = one_hot(
        SPANS * extra,
        halves * lines,
        lambda r, c: (c % BLOCK // own == r // extra ^ fibre)
        & (c % own == r % own)
        & (c // lines == r % (halves * own) // own)
        & (c % lines // BLOCK == r % extra // (halves * own)),
    )
    seen_copy.wait()
    mask_copy.wait()
    window = jnp.concatenate(
        [mask[pl.ds(start + i, 1), :] + jnp.zeros((BLOCK, 1), jnp.int32) for i in range(share)], axis=0
    )
    seen = jnp.where(window != 0, observed[...].reshape(lines, LAGS), MASKED)
    seen = seen.astype(jnp.bfloat16)
    parts = [seen[:, h * LANES : (h + 1) * LANES] for h in range(halves)]
    packed = dot(place, jnp.concatenate(parts, axis=0)).astype(jnp.bfloat16)
    for k, out_ref in enumerate(out_refs):
        out_ref[tiles * rows :, :] = packed[k * extra : (k + 1) * extra]
    records_copy.wait()
    moved = dot(order, records[...], _NT).astype(jnp.bfloat16)
    for k, out_ref in enumerate(out_refs):
        for q in range(tiles):
            part = moved[k * rows : (k + 1) * rows, q * LANES : (q + 1) * LANES]
            out_ref[q * rows : (q + 1) * rows, :] = part


def prepare_kernel(segs, blocks, own, pairs_dev, share, pairs_hbm, *refs):
    constants = (len(refs) - 6) // 2
    take_ref, give_ref, find_ref, order_ref, pairs_ref, sems = refs[2 * constants :]
    pairs_copy = pltpu.make_async_copy(pairs_hbm, pairs_ref, sems.at[constants])
    copies = [pltpu.make_async_copy(refs[i], refs[constants + i], sems.at[i]) for i in range(constants)]
    for copy in [pairs_copy] + copies:
        copy.start()
    fibre, seg, rec = (lax.axis_index(axis) for axis in ("fibre", "seg", "rec"))
    pair_total = pairs_ref.shape[1]
    rows = blocks * own
    lines = pair_total * own

    def picks(side, line):
        block = jnp.zeros_like(line)
        for n in range(pair_total):
            block = jnp.where(line // own == n, pairs_ref[side, n], block)
        distance = (seg + segs - block // blocks) % segs
        return distance * rows + block % blocks * own + line % own

    halves = LAGS // LANES
    extra = halves * share * own

    def here(half, line, place):
        part = place % extra
        owner = (place // extra % SPANS ^ fibre) * segs + (seg + segs - place // (extra * SPANS)) % segs
        pair = owner * pairs_dev + rec * share + part // (halves * own)
        return (line // own == pair) & (line % own == part % own) & (part % (halves * own) // own == half)

    for h in range(halves):
        find_ref[h] = one_hot(lines, segs * SPANS * extra, functools.partial(here, h))
    order_ref[...] = channel_order(fibre, blocks, own)
    pairs_copy.wait()
    for side in range(2):
        line = lax.broadcasted_iota(jnp.int32, (lines, segs * rows), 0)
        row = lax.broadcasted_iota(jnp.int32, (lines, segs * rows), 1)
        hit = jnp.where(picks(side, line) == row, 1.0, 0.0).astype(jnp.bfloat16)
        take_ref[side * lines : (side + 1) * lines, :] = hit
        line = lax.broadcasted_iota(jnp.int32, (rows, lines), 1)
        row = lax.broadcasted_iota(jnp.int32, (rows, lines), 0)
        hit = jnp.where(picks(side, line) == row, 1.0, 0.0).astype(jnp.bfloat16)
        give_ref[:, side * lines : (side + 1) * lines] = hit
    for copy in copies:
        copy.wait()


def transform(chunks, rows, table_ref):
    fibre = lax.axis_index("fibre")
    span = S // SPANS
    band = F // SPANS
    folds = []
    for chunk in chunks:
        whole = [chunk[q * rows : (q + 1) * rows, :] for q in range(span // LANES)]
        folds.append(jnp.concatenate(whole, axis=1).astype(jnp.float32))
    flip = fibre % 2 == 1
    turn = jnp.where(flip, -1.0, 1.0)
    late = jnp.where(fibre >= 2, -1.0, 1.0)
    near, far = folds[0] + folds[2], folds[1] + folds[3]
    near_gap, far_gap = folds[0] - folds[2], folds[1] - folds[3]
    e_part = late * jnp.where(flip, far_gap, near_gap)
    d_part = late * jnp.where(flip, near_gap, far_gap)
    both = jnp.concatenate([e_part, d_part], axis=0).astype(jnp.bfloat16)
    reals, imags = [], []
    for j in range(SPANS):
        if j % 2 == 0:
            signal = near + far if j == 0 else turn * (near - far)
            part = dot(signal.astype(jnp.bfloat16), table_ref[j])
            real, imag = part[:, :band], part[:, band:]
        else:
            mixed = dot(both, table_ref[j])
            e_c, e_s = mixed[:rows, :band], mixed[:rows, band:]
            d_c, d_s = mixed[rows:, :band], mixed[rows:, band:]
            real, imag = (e_c + d_s, e_s - d_c) if j == 1 else (e_c - d_s, e_s + d_c)
        reals.append(real.astype(jnp.bfloat16))
        imags.append(imag.astype(jnp.bfloat16))
    return jnp.concatenate(reals + imags, axis=1)


def spectra_kernel(blocks, own, *refs):
    refs[-1][...] = transform(refs[:SPANS], blocks * own, refs[SPANS])


def correlate_kernel(segs, blocks, own, *refs):
    chunks = [refs[i] for i in [7, 2, 6, 5, 3, 4, 1, 0]]
    own_ref, table_ref, lag_ref, take_ref, find_ref, chosen_ref, partial_ref = refs[segs * SPANS :]
    rows = blocks * own
    lines = take_ref.shape[0] // 2
    tiles = S // SPANS // LANES
    spectra = [own_ref[...]] + [
        transform(chunks[u * SPANS : (u + 1) * SPANS], rows, table_ref) for u in range(1, segs)
    ]
    spectra = jnp.concatenate(spectra, axis=0)
    chosen = dot(take_ref[...], spectra)
    chosen_ref[...] = chosen.astype(jnp.bfloat16)
    a0, a1 = chosen[:lines, :F], chosen[:lines, F:]
    b0, b1 = chosen[lines:, :F], chosen[lines:, F:]
    cross_re = (a0 * b0 + a1 * b1).astype(jnp.bfloat16)
    cross_im = (a1 * b0 - a0 * b1).astype(jnp.bfloat16)
    partial = dot(jnp.concatenate([cross_re, cross_im], axis=1), lag_ref[...])
    packed = jnp.concatenate([chunk[tiles * rows :, :] for chunk in chunks], axis=0)
    seen = jnp.concatenate([dot(find_ref[h], packed) for h in range(LAGS // LANES)], axis=1)
    partial_ref[...] = partial - seen


def adjoint_kernel(blocks, own, chosen_ref, mine_ref, other_ref, back_ref, lag_ref, give_ref, *out_refs):
    fibre = lax.axis_index("fibre")
    band = F // SPANS
    lines = mine_ref.shape[0]
    count = blocks * own
    misfit = mine_ref[...] + other_ref[...]
    weights = jnp.where(misfit > -0.5 * MASKED, jnp.tanh(misfit), 0.0).astype(jnp.bfloat16)
    adjoint = dot(weights, lag_ref[...], _NT).astype(jnp.bfloat16).astype(jnp.float32)
    g0, g1 = adjoint[:, :F], adjoint[:, F:]
    a0 = chosen_ref[:lines, :F].astype(jnp.float32)
    a1 = chosen_ref[:lines, F:].astype(jnp.float32)
    b0 = chosen_ref[lines:, :F].astype(jnp.float32)
    b1 = chosen_ref[lines:, F:].astype(jnp.float32)
    low = jnp.bfloat16
    first = jnp.concatenate([(g0 * b0 - g1 * b1).astype(low), (g0 * b1 + g1 * b0).astype(low)], axis=1)
    second = jnp.concatenate([(g0 * a0 + g1 * a1).astype(low), (g0 * a1 - g1 * a0).astype(low)], axis=1)
    grad = dot(give_ref[...], jnp.concatenate([first, second], axis=0)).astype(low)
    even, odd = None, None
    for j in range(SPANS):
        real = grad[:, j * band : (j + 1) * band]
        imag = grad[:, F + j * band : F + (j + 1) * band]
        line = jnp.concatenate([real, imag], axis=1)
        if j % 2 == 0:
            part = dot(line, back_ref[j])
            even = (part, part) if j == 0 else (even[0] + part, even[1] - part)
        else:
            turned = jnp.concatenate([-imag, real], axis=1)
            part = dot(jnp.concatenate([line, turned], axis=0), back_ref[j])
            u, v = part[:count], part[count:]
            odd = (u, v) if j == 1 else (odd[0] + u, odd[1] - v)
    flip = fibre % 2 == 1
    late = jnp.where(fibre >= 2, -1.0, 1.0)
    for k, out_ref in enumerate(out_refs):
        other = flip if k % 2 == 0 else ~flip
        base = jnp.where(other, even[1], even[0])
        side = late * jnp.where(other, odd[1], odd[0])
        out_ref[...] = (base + side if k < 2 else base - side).astype(low)


def unpack_kernel(*refs):
    chunks = [refs[i] for i in [3, 1, 2, 0]]
    order_ref, out_hbm, out, sems = refs[SPANS:]
    span = out.shape[0]
    cuts = [pl.ds(q * LANES, LANES) for q in range(span // LANES)]
    leave = [pltpu.make_async_copy(out.at[cut], out_hbm.at[cut], sems.at[q]) for q, cut in enumerate(cuts)]
    for q, copy in enumerate(leave):
        held = jnp.concatenate([chunk[:, q * LANES : (q + 1) * LANES] for chunk in chunks], axis=0)
        out[q * LANES : (q + 1) * LANES, :] = dot(held, order_ref[...], _TN).astype(jnp.bfloat16)
        copy.start()
    for copy in leave:
        copy.wait()


def by_own_k(records, pairs, observed, lag_mask):
    recs, segs, fibres = (lax.axis_size(axis) for axis in ("rec", "seg", "fibre"))
    own = BLOCK // fibres
    span, count = records.shape[1:]
    blocks = count // BLOCK
    rows = blocks * own
    pair_total, pairs_dev = pairs.shape[0], observed.shape[0]
    share = pairs_dev // recs
    lines = pair_total * own
    extra = LAGS // LANES * share * own
    table = forward_table().reshape(F // SPANS, SPANS, 2, SPANS, span)[:, :, :, 0]
    table = np.ascontiguousarray(table.transpose(1, 3, 2, 0)).reshape(SPANS, span, S // SPANS)
    lags = lag_table().reshape(F // SPANS, SPANS, 2, LAGS)
    lags = np.ascontiguousarray(lags.transpose(2, 1, 0, 3)).reshape(2 * F, LAGS)
    low = jnp.bfloat16
    vmem = pl.BlockSpec(memory_space=pltpu.VMEM)
    hbm = pl.BlockSpec(memory_space=pl.ANY)
    limit = pltpu.CompilerParams(vmem_limit_bytes=16 * 2**20)

    def along(axis, array, target):
        return lax.ppermute(array, axis, [(i, target(i)) for i in range(lax.axis_size(axis))])

    send = pl.pallas_call(
        functools.partial(pack_kernel, blocks, own),
        out_shape=[pltpu.VMEM((span // LANES * rows + extra, LANES), low)] * SPANS,
        in_specs=[hbm] * 3,
        out_specs=[vmem] * SPANS,
        scratch_shapes=[
            pltpu.VMEM((span, count), low),
            pltpu.VMEM((share, BLOCK, LAGS), jnp.float32),
            pltpu.VMEM(lag_mask.shape, jnp.int32),
            pltpu.SemaphoreType.DMA((3,)),
        ],
        compiler_params=limit,
    )(*(pltpu.with_memory_space_constraint(x, pltpu.HBM) for x in (records[0], observed, lag_mask)))
    held = [along("fibre", send[k], lambda i: i ^ k) for k in range(SPANS - 1, 0, -1)]
    held = [send[0]] + held[::-1]
    table_back = jnp.asarray(np.ascontiguousarray(table.transpose(0, 2, 1)))
    lags = jnp.asarray(lags)
    constants = [jnp.asarray(table)]
    table, take, give, find, order = pl.pallas_call(
        functools.partial(prepare_kernel, segs, blocks, own, pairs_dev, share),
        out_shape=[pltpu.VMEM(c.shape, low) for c in constants]
        + [
            pltpu.VMEM((2 * lines, segs * rows), low),
            pltpu.VMEM((rows, 2 * lines), low),
            pltpu.VMEM((LAGS // LANES, lines, segs * SPANS * extra), low),
            pltpu.VMEM((count, count), low),
        ],
        in_specs=[hbm] * (1 + len(constants)),
        out_specs=[vmem] * (len(constants) + 4),
        scratch_shapes=[pltpu.SMEM(pairs.shape[::-1], jnp.int32), pltpu.SemaphoreType.DMA((1 + len(constants),))],
        compiler_params=limit,
        cost_estimate=pl.CostEstimate(flops=0, bytes_accessed=4 * 2**20, transcendentals=0),
    )(*(pltpu.with_memory_space_constraint(c, pltpu.HBM) for c in [pairs.T] + constants))
    for u in range(1, segs):
        held += [
            along(("fibre", "seg"), send[k], lambda i: (i // segs ^ k) * segs + (i + u) % segs)
            if k in (1,)
            else along("seg", held[k], lambda i: (i + u) % segs)
            for k in range(SPANS - 1, -1, -1)
        ][::-1]
    spectra = pl.pallas_call(
        functools.partial(spectra_kernel, blocks, own),
        out_shape=pltpu.VMEM((rows, 2 * F), low),
        in_specs=[vmem] * (SPANS + 1),
        out_specs=vmem,
        compiler_params=limit,
    )(*held[:SPANS], table)
    chosen, partial = pl.pallas_call(
        functools.partial(correlate_kernel, segs, blocks, own),
        out_shape=[pltpu.VMEM((2 * lines, 2 * F), low), pltpu.VMEM((lines, LAGS), jnp.float32)],
        in_specs=[vmem] * (segs * SPANS + 5),
        out_specs=[vmem] * 2,
        compiler_params=limit,
    )(*[held[i] for i in (7, 6, 1, 4, 5, 3, 2, 0)], spectra, table, lags, take, find)
    mine, other = partial, along("rec", partial, lambda i: (i + 1) % recs)
    for _ in range(2, recs):
        mine, other = mine + other, along("rec", other, lambda i: (i + 1) % recs)
    back = pl.pallas_call(
        functools.partial(adjoint_kernel, blocks, own),
        out_shape=[pltpu.VMEM((rows, span), low)] * SPANS,
        in_specs=[vmem] * 6,
        out_specs=[vmem] * SPANS,
        compiler_params=limit,
    )(chosen, mine, other, table_back, lags, give)
    own_part = back[0]
    sent = {k: along("fibre", back[k], lambda i: i ^ k) for k in (3, 1, 2)}
    out = pl.pallas_call(
        unpack_kernel,
        out_shape=jax.ShapeDtypeStruct((span, count), low),
        in_specs=[vmem] * (SPANS + 1),
        out_specs=hbm,
        scratch_shapes=[
            pltpu.VMEM((span, count), low),
            pltpu.SemaphoreType.DMA((span // LANES,)),
        ],
        compiler_params=limit,
    )(*sent.values(), own_part, order)
    return out[None]


def by_band(records, pairs, observed, lag_mask):
    fibres, segs = lax.axis_size("fibre"), lax.axis_size("seg")
    own = BLOCK // fibres
    span, count = records.shape[1:]
    blocks = count // BLOCK
    total_blocks = blocks * segs
    pair_total, pairs_dev = pairs.shape[0], observed.shape[0]
    low = jnp.bfloat16
    band = F // segs
    start = lax.axis_index("seg") * band
    table = lax.dynamic_slice_in_dim(jnp.asarray(forward_table()), start, band, 0)
    lags = lax.dynamic_slice_in_dim(jnp.asarray(lag_table()), start, band, 0)
    f32 = functools.partial(jnp.einsum, preferred_element_type=jnp.float32)
    grid = records.reshape(span, blocks, fibres, own).transpose(2, 0, 1, 3)
    signal = lax.all_to_all(grid, "fibre", 0, 0, tiled=True).reshape(S, blocks, own)
    signal = lax.all_gather(signal, "seg", axis=1, tiled=True)
    spectra = f32("wpt,tbk->wpbk", table, signal).astype(low)
    ids = jnp.arange(total_blocks)
    take = [(pairs[:, side, None] == ids).astype(low) for side in range(2)]
    a0, a1 = (f32("nb,wbk->wnk", take[0], spectra[:, p]) for p in range(2))
    b0, b1 = (f32("nb,wbk->wnk", take[1], spectra[:, p]) for p in range(2))
    cross = jnp.stack([a0 * b0 + a1 * b1, a1 * b0 - a0 * b1], axis=1).astype(low)
    corr = f32("wpnk,wpl->nkl", cross, lags)
    corr = corr.reshape(fibres, segs, pairs_dev, own, LAGS)
    corr = lax.psum_scatter(corr, "seg", scatter_dimension=1)
    synthetic = lax.psum(corr, "rec").reshape(fibres * pairs_dev, own, LAGS)
    seen = observed.reshape(pairs_dev, fibres, own, LAGS).transpose(1, 0, 2, 3)
    seen = lax.all_to_all(seen, "fibre", 0, 0, tiled=True).reshape(fibres * pairs_dev, own, LAGS)
    window = lax.all_gather(lag_mask.astype(jnp.float32), "fibre", axis=0, tiled=True)
    weights = (window[:, None, :] * jnp.tanh(synthetic - seen)).astype(low)
    weights = lax.all_gather(weights.reshape(fibres, pairs_dev, own, LAGS), "seg", axis=1)
    weights = weights.reshape(pair_total, own, LAGS)
    adjoint = f32("nkl,wpl->wpnk", weights, lags).astype(low).astype(jnp.float32)
    g0, g1 = adjoint[:, 0], adjoint[:, 1]

    def added(side, terms):
        high = terms.astype(low)
        rest = (terms - high.astype(jnp.float32)).astype(low)
        return f32("nb,wnk->wbk", take[side], high) + f32("nb,wnk->wbk", take[side], rest)

    grad = jnp.stack(
        [
            added(0, g0 * b0 - g1 * b1) + added(1, g0 * a0 + g1 * a1),
            added(0, g0 * b1 + g1 * b0) + added(1, g0 * a1 - g1 * a0),
        ],
        axis=1,
    ).astype(low)
    sources = f32("wpbk,wpt->tbk", grad, table)
    sources = lax.psum_scatter(sources, "seg", scatter_dimension=1, tiled=True).astype(low)
    sources = sources.reshape(fibres, span, blocks, own)
    sources = lax.all_to_all(sources, "fibre", 0, 0, tiled=True)
    return sources.transpose(1, 2, 0, 3).reshape(1, span, count)


def solution(mesh):
    in_specs = (
        P("rec", "fibre", ("groups", "seg")),
        P(),
        P(("groups", "fibre", "seg"), None, None),
        P(("groups", "fibre", "seg"), None),
    )
    out_specs = P("rec", "fibre", ("groups", "seg"))
    small = mesh.shape["fibre"] == SPANS
    return jax.shard_map(
        by_own_k if small else by_band,
        mesh=mesh,
        in_specs=in_specs,
        out_specs=out_specs,
        check_vma=False,
    )
```
